32 devices in a mesh: region: 2 (over y), gx: 16 (over z, x, core).
Axes of the slice: x: 2, y: 2, z: 4, core: 2. Of those that a mesh axis runs over, the one named last changes fastest.
Arguments:
- latent: float32 [16, 512, 2048], P(None, 'gx', 'region'), parts along dimension 2, may hold values from -6 to 6
- counts: int32 [16, 512, 2048], P(None, 'gx', 'region'), parts along dimension 2, may hold values from 0 to 4
- land_mask: int32 [512, 2048], P('gx', 'region'), parts along dimension 1, may hold values 0 or 1
- region_ids: int32 [512, 2048], P('gx', 'region'), parts along dimension 1, may hold values from 0 to 7
- kappa_sq: float32 [512, 2048], P('gx', 'region'), parts along dimension 1, may hold values from 0.05 to 2
- covariates: bfloat16 [32, 512, 2048], P(None, 'gx', 'region'), parts along dimension 2, may hold values from -6 to 6
- effects: bfloat16 [64], P('region'), parts along dimension 0, may hold values from -4 to 4
- intercepts: float32 [16], P('region'), parts along dimension 0, may hold values from -2 to 0.5
Outputs:
- newton_step: float32 [16, 512, 2048], P(None, 'gx', 'region'), parts along dimension 2
- residual: float32 [16, 512, 2048], P(None, 'gx', 'region'), parts along dimension 2
The draws below stay inside these ranges and needn't reach their ends.
There are 2 independent parts, one for each index of `region`. The reference program is written for one: setup_inputs(seed, part) draws one part's arguments, and reference() takes and returns one part's arrays. A program takes and returns all parts, laid end to end along the dimension named above; each array names one. Nothing has to cross between parts.
All inputs are finite; a program needn't handle non-finite values. No bound on the sum of `land_mask` on one device may be relied on, other than what follows from the above.
Results may differ from the reference program's by a relative error of at most 0.0003.
Values sent between devices are 32-bit elements; how exact they have to be, the bound alone decides.
No kernel may reach another device: no remote copies, remote signals or barrier semaphores. Data moves between devices by JAX's collectives and lax.ppermute only.
A program may use at most 64 MiB of HBM per device.

```python
import math
import jax
import jax.numpy as jnp

NY = 1024
WEEKS = 16
COVS = 32
ZONES = 8
TRIALS = 4
ITERS = 2
NX = 512


def with_ends(drawn, rng, least, high):
    extent = drawn.shape
    spot = [jax.random.randint(jax.random.fold_in(rng, axis), (), 0, extent[axis]) for axis in range(len(extent))]
    drawn = drawn.at[tuple(spot)].set(least)
    longest = extent.index(max(extent))
    spot[longest] = (spot[longest] + 1) % extent[longest]
    return drawn.at[tuple(spot)].set(high)


def shard_levels(stream_key, dims, pieces, smallest, largest):
    def one(position, shards_of):
        steps = jax.random.uniform(jax.random.fold_in(jax.random.fold_in(stream_key, 6), position), (shards_of,), jnp.float32, smallest / len(pieces), largest / len(pieces))
        return jnp.repeat(jnp.exp(steps), dims[position] // shards_of).reshape((-1,) + (1,) * (len(dims) - position - 1))

    factor_of = one(*pieces[0])
    for cut in pieces[1:]:
        factor_of = factor_of * one(*cut)
    return factor_of


def scatter_about(key, dims, width, bound, pieces=(), held_as=jnp.bfloat16):
    entries = jax.random.normal(key, dims, jnp.float32) * width
    if len(pieces) > 0:
        entries = shard_levels(key, dims, pieces, -0.22, 0.18) * entries
    return jnp.clip(entries, min=-bound, max=bound).astype(held_as)


def setup_inputs(seed: int = 0, part: int = 0) -> dict:
    arg_keys = jax.random.split(jax.random.key(seed), 9)
    own_keys = jax.random.split(jax.random.fold_in(arg_keys[8], part), 9)
    return {
        "latent": scatter_about(own_keys[0], (WEEKS, NX, NY), 1.0, 6.0, ((1, 16),), jnp.float32),
        "counts": with_ends(jax.random.randint(own_keys[1], (WEEKS, NX, NY), 0, TRIALS + 1), jax.random.fold_in(own_keys[1], 1), 0, TRIALS).astype(jnp.int32),
        "land_mask": with_ends((jax.random.randint(own_keys[2], (NX, NY), 0, 4) < 3).astype(jnp.int32), jax.random.fold_in(own_keys[2], 1), 0, 1),
        "region_ids": with_ends(jax.random.randint(own_keys[3], (NX, NY), 0, ZONES), jax.random.fold_in(own_keys[3], 1), 0, ZONES - 1).astype(jnp.int32),
        "kappa_sq": jnp.clip(jnp.exp(math.log(2.0) - 3.6888794 * jax.random.uniform(own_keys[4], (NX, NY), jnp.float32) ** shard_levels(own_keys[4], (NX, NY), ((0, 16),), -0.2, 0.2)), 0.05, 2.0),
        "covariates": scatter_about(own_keys[5], (COVS, NX, NY), 1.0, 6.0, ((1, 16),)),
        "effects": scatter_about(own_keys[6], (COVS,), 0.3, 4.0),
        "intercepts": jnp.clip(jax.random.uniform(own_keys[7], (ZONES,), jnp.float32, -2.0, 0.5), -2.0, 0.5),
    }


prior_scale = 0.04
time_coupling = 0.5


def stencil(extended, kappa_rows):
    center = extended[:, 1:-1, :]
    side = jnp.pad(center, ((0, 0), (0, 0), (1, 1)))
    beside_all = extended[:, 2:, :] + extended[:, :-2, :] + side[:, :, 2:] + side[:, :, :-2]
    return (kappa_rows + 4.0) * center - beside_all


def temporal(field):
    before = jnp.concatenate([field[:1], field[:-1]], axis=0)
    after = jnp.concatenate([field[1:], field[-1:]], axis=0)
    return 2.0 * field - before - after


def prior(field, kappa_sq):
    inner_image = stencil(jnp.pad(field, ((0, 0), (1, 1), (0, 0))), kappa_sq)
    outer_image = stencil(jnp.pad(inner_image, ((0, 0), (1, 1), (0, 0))), kappa_sq)
    return prior_scale * outer_image + time_coupling * temporal(field)


def reference(latent, counts, land_mask, region_ids, kappa_sq, covariates, effects, intercepts):
    cov_term = jnp.einsum("k,kxy->xy", effects.astype(jnp.float32), covariates.astype(jnp.float32))
    predictor = latent + (cov_term + intercepts[region_ids])[None]
    probability = jax.nn.sigmoid(predictor)
    land = land_mask.astype(jnp.float32)[None]
    weight = land * float(TRIALS) * probability * (1.0 - probability)
    gradient = land * (counts.astype(jnp.float32) - float(TRIALS) * probability) - prior(latent, kappa_sq)
    inverse_diag = 1.0 / (prior_scale * ((kappa_sq + 4.0) ** 2 + 4.0) + 2.0 * time_coupling + weight)
    newton_step = jnp.zeros_like(latent)
    residual = gradient
    scaled = inverse_diag * residual
    search = scaled
    product_now = jnp.sum(residual * scaled)
    for iteration in range(ITERS):
        image = prior(search, kappa_sq) + weight * search
        step_size = product_now / jnp.sum(search * image)
        newton_step = newton_step + step_size * search
        residual = residual - step_size * image
        scaled = inverse_diag * residual
        product_next = jnp.sum(residual * scaled)
        search = scaled + (product_next / product_now) * search
        product_now = product_next
    return newton_step, residual
```

```python
import jax
import jax.numpy as jnp
from jax import lax
from jax.sharding import PartitionSpec as P

AX = "gx"
prior_scale = 0.04
time_coupling = 0.5


def swap_halos(head, tail):
    count = lax.axis_size(AX)
    odd = lax.axis_index(AX) % 2 == 1
    first = [(i, i ^ 1) for i in range(count) if (i ^ 1) < count]
    second = [(i, ((i + 1) ^ 1) - 1) for i in range(count) if 0 <= ((i + 1) ^ 1) - 1 < count]
    got_first = lax.ppermute(jnp.where(odd, head, tail), AX, first)
    got_second = lax.ppermute(jnp.where(odd, tail, head), AX, second)
    return jnp.where(odd, got_first, got_second), jnp.where(odd, got_second, got_first)


def all_sum(values):
    count = lax.axis_size(AX)
    if count & (count - 1):
        return lax.psum(values, AX)
    step = 1
    while step < count:
        values = values + lax.ppermute(values, AX, [(i, i ^ step) for i in range(count)])
        step *= 2
    return values


def laplace(field, kappa_rows):
    center = field[1:-1]
    side = jnp.pad(center, ((0, 0), (0, 0), (1, 1)))
    beside = field[2:] + field[:-2] + side[:, :, 2:] + side[:, :, :-2]
    return (kappa_rows + 4.0)[:, None] * center - beside


def temporal(field):
    before = jnp.concatenate([field[:, :1], field[:, :-1]], axis=1)
    after = jnp.concatenate([field[:, 1:], field[:, -1:]], axis=1)
    return 2.0 * field - before - after


def shards(latent, counts, land_mask, region_ids, kappa_sq, covariates, effects, intercepts):
    weeks, rows, cols = latent.shape
    me = lax.axis_index(AX)
    field = jnp.transpose(latent, (1, 0, 2))

    def inside(depth):
        place = lax.broadcasted_iota(jnp.int32, (rows + 2 * depth, 1, 1), 0) - depth + me * rows
        return ((place >= 0) & (place < rows * lax.axis_size(AX))).astype(jnp.float32)

    def pack(wide, flat):
        return jnp.concatenate([wide.reshape(-1, cols)] + flat, axis=0)

    land_own = land_mask.astype(jnp.float32)
    above, below = swap_halos(
        pack(field[:2], [kappa_sq[:3], land_own[:2]]), pack(field[-2:], [kappa_sq[-3:], land_own[-2:]])
    )
    cut = 2 * weeks

    cov_term = jnp.einsum("k,kxy->xy", effects, covariates, preferred_element_type=jnp.float32)
    offset = jnp.zeros(kappa_sq.shape, jnp.float32)
    for zone in range(intercepts.shape[0]):
        offset = offset + jnp.where(region_ids == zone, intercepts[zone], 0.0)
    eta = cov_term + offset

    field = jnp.concatenate([above[:cut].reshape(2, weeks, cols), field, below[:cut].reshape(2, weeks, cols)])
    kappa = jnp.concatenate([above[cut : cut + 3], kappa_sq, below[cut : cut + 3]])
    land = jnp.concatenate([above[cut + 3 :], land_own, below[cut + 3 :]])[:, None]
    image = laplace(laplace(field, kappa[2:-2]) * inside(1), kappa_sq)
    own = field[2:-2]
    curve = jnp.tanh(0.5 * (own + eta[:, None]))
    tally = jnp.transpose(counts, (1, 0, 2)).astype(jnp.float32)
    gradient = land[2:-2] * (tally - 2.0 - 2.0 * curve) - prior_scale * image - time_coupling * temporal(own)
    diag_base = prior_scale * ((kappa + 4.0) ** 2 + 4.0) + 2.0 * time_coupling
    weight = land[2:-2] * (1.0 - curve * curve)
    search = gradient / (diag_base[3:-3, None] + weight)

    above, below = swap_halos(pack(search[:4], [eta[:2]]), pack(search[-4:], [eta[-2:]]))
    cut = 4 * weeks
    search_all = jnp.concatenate([above[:cut].reshape(4, weeks, cols), search, below[:cut].reshape(4, weeks, cols)])
    eta_all = jnp.concatenate([above[cut:], eta, below[cut:]])
    curve = jnp.tanh(0.5 * (field + eta_all[:, None]))
    weight = land * (1.0 - curve * curve)
    image = laplace(laplace(search_all, kappa) * inside(3), kappa[1:-1])
    image = prior_scale * image + time_coupling * temporal(search_all[2:-2]) + weight * search_all[2:-2]
    other = inside(2) * (image / (diag_base[1:-1, None] + weight))
    own_image = image[2:-2]
    own_other = other[2:-2]
    other_image = laplace(laplace(other, kappa[2:-2]) * inside(1), kappa_sq)
    other_image = prior_scale * other_image + time_coupling * temporal(own_other) + weight[2:-2] * own_other

    sums = jnp.stack(
        [
            jnp.sum(gradient * search),
            jnp.sum(search * own_image),
            jnp.sum(own_image * own_other),
            jnp.sum(own_other * other_image),
        ]
    )
    rz, pq, cross, last = all_sum(sums)
    first_step = rz / pq
    rz_next = first_step * first_step * cross - rz
    turn = 1.0 + rz_next / rz
    second_step = rz_next / (turn * (turn * pq - 2.0 * first_step * cross) + first_step * first_step * last)
    along = first_step + second_step * turn
    across = second_step * first_step
    newton = along * search - across * own_other
    residual = gradient - along * own_image + across * other_image
    return jnp.transpose(newton, (1, 0, 2)), jnp.transpose(residual, (1, 0, 2))


def solution(mesh):
    placed = (
        P(None, "gx", "region"),
        P(None, "gx", "region"),
        P("gx", "region"),
        P("gx", "region"),
        P("gx", "region"),
        P(None, "gx", "region"),
        P("region"),
        P("region"),
    )
    return jax.shard_map(
        shards,
        mesh=mesh,
        in_specs=placed,
        out_specs=(P(None, "gx", "region"), P(None, "gx", "region")),
        check_vma=False,
    )
```

```python
import functools

import jax
import jax.numpy as jnp
from jax import lax
from jax.experimental import pallas as pl
from jax.experimental.pallas import tpu as pltpu
from jax.sharding import PartitionSpec as P

AX = "gx"
LANES = 128
prior_scale = 0.04
time_coupling = 0.5
F32 = jnp.float32
VMEM = pltpu.VMEM
MIB = 1 << 20


def swap_halos(head, tail):
    count = lax.axis_size(AX)
    odd = lax.axis_index(AX) % 2 == 1
    first = [(i, i ^ 1) for i in range(count) if (i ^ 1) < count]
    second = [(i, ((i + 1) ^ 1) - 1) for i in range(count) if 0 <= ((i + 1) ^ 1) - 1 < count]
    got_first = lax.ppermute(jnp.where(odd, head, tail), AX, first)
    got_second = lax.ppermute(jnp.where(odd, tail, head), AX, second)
    return jnp.where(odd, got_first, got_second), jnp.where(odd, got_second, got_first)


def all_sum(values):
    count = lax.axis_size(AX)
    if count & (count - 1):
        return lax.psum(values, AX)
    step = 1
    while step < count:
        values = values + lax.ppermute(values, AX, [(i, i ^ step) for i in range(count)])
        step *= 2
    return values


def row_of(ref, row):
    return [ref[row, :, c : c + LANES] for c in range(0, ref.shape[2], LANES)]


def put_row(ref, row, tiles):
    for j, tile in enumerate(tiles):
        ref[row, :, j * LANES : (j + 1) * LANES] = tile


def map_row(ref, row):
    return [ref[row, :, c : c + LANES] for c in range(0, ref.shape[2], LANES)]


def masks(weeks):
    lane = lax.broadcasted_iota(jnp.int32, (weeks, LANES), 1)
    week = lax.broadcasted_iota(jnp.int32, (weeks, LANES), 0)
    return lane == 0, lane == LANES - 1, week == 0, week == weeks - 1


def laplace_row(up, mid, down, kappa, mask):
    first, last = mask[0], mask[1]
    count = len(mid)
    to_right = [pltpu.roll(t, 1, 1) for t in mid]
    to_left = [pltpu.roll(t, LANES - 1, 1) for t in mid]
    out = []
    for j in range(count):
        west = jnp.where(first, to_right[j - 1] if j > 0 else 0.0, to_right[j])
        east = jnp.where(last, to_left[j + 1] if j + 1 < count else 0.0, to_left[j])
        out.append((kappa[j] + 4.0) * mid[j] - ((up[j] + down[j]) + (west + east)))
    return out


def temporal_tile(tile, mask):
    weeks = tile.shape[0]
    before = jnp.where(mask[2], tile, pltpu.roll(tile, 1, 0))
    after = jnp.where(mask[3], tile, pltpu.roll(tile, weeks - 1, 0))
    return (2.0 * tile - before) - after


def fold(tiles):
    parts = [t[h : h + 8] for t in tiles for h in range(0, t.shape[0], 8)]
    while len(parts) > 1:
        parts = [a + b for a, b in zip(parts[::2], parts[1::2])] + ([parts[-1]] if len(parts) % 2 else [])
    return parts[0]


def diag_base(kappa):
    return prior_scale * ((kappa + 4.0) * (kappa + 4.0) + 4.0) + 2.0 * time_coupling


def start_kernel(effects, intercepts, latent, counts, covariates, land, zones, kappa,
                 field, grad, weight, inv, search, image, eta,
                 tally, covs, field_sem, tally_sem, cov_sem):
    weeks, rows, cols = latent.shape
    num_covs = covariates.shape[0]
    mask = masks(weeks)

    def field_copy(r):
        return pltpu.make_async_copy(latent.at[:, r, :], field.at[r + 2], field_sem.at[r])

    def tally_copy(r):
        return pltpu.make_async_copy(counts.at[:, r, :], tally.at[r], tally_sem.at[r])

    cov_copy = pltpu.make_async_copy(covariates, covs, cov_sem)
    for r in range(rows):
        field_copy(r).start()
    cov_copy.start()
    for r in range(rows):
        tally_copy(r).start()
    field_copy(0).wait()
    field_copy(1).wait()

    @pl.loop(1, rows - 1)
    def _(r):
        field_copy(r + 1).wait()
        put_row(image, r + 1, laplace_row(
            row_of(field, r + 1), row_of(field, r + 2), row_of(field, r + 3), map_row(kappa, r), mask))

    cov_copy.wait()
    width = 2 * LANES
    for c in range(0, cols, width):
        total = jnp.zeros((rows, width), F32)
        ids = zones[:, c : c + width]
        for z in range(intercepts.shape[0]):
            total = jnp.where(ids == z, intercepts[z], total)
        for k in range(num_covs):
            total = total + effects[k] * covs[k, :, c : c + width].astype(F32)
        for r in range(rows):
            eta[r, :, c : c + width] = total[r : r + 1]

    def pointwise(r):
        tally_copy(r).wait()
        lat, eta_row, land_row, kap, count_row = (
            row_of(field, r + 2), map_row(eta, r), map_row(land, r), map_row(kappa, r), row_of(tally, r))
        out, heavy, inverse = [], [], []
        for j, tile in enumerate(lat):
            on = land_row[j]
            curve = jnp.tanh(0.5 * (tile + eta_row[j]))
            heavy.append(on * (1.0 - curve * curve))
            inverse.append(1.0 / (diag_base(kap[j]) + heavy[j]))
            out.append(on * (count_row[j].astype(F32) - 2.0 - 2.0 * curve) - time_coupling * temporal_tile(tile, mask))
        put_row(weight, r + 2, heavy)
        put_row(inv, r + 2, inverse)
        return out, inverse, kap

    @pl.loop(0, 4)
    def _(i):
        r = jnp.where(i < 2, i, rows - 4 + i)
        put_row(grad, r, pointwise(r)[0])

    @pl.loop(2, rows - 2)
    def _(r):
        out, inverse, kap = pointwise(r)
        outer = laplace_row(row_of(image, r), row_of(image, r + 1), row_of(image, r + 2), kap, mask)
        out = [a - prior_scale * b for a, b in zip(out, outer)]
        put_row(grad, r, out)
        put_row(search, r + 4, [a * b for a, b in zip(out, inverse)])


def scale_of(r, rows, inside):
    return jnp.where(r < 0, inside[0], jnp.where(r >= rows, inside[1], 1.0))


def put_halo(ref, row, packed, at, weeks):
    for c in range(0, packed.shape[1], LANES):
        ref[row, :, c : c + LANES] = packed[at : at + weeks, c : c + LANES]


def edge_kernel(inside, above, below, kappa, eta, inv, field_in, grad_in, search_in, image_in,
                field, grad, search, image, head, tail):
    weeks = field.shape[1]
    rows, _, cols = eta.shape
    mask = masks(weeks)
    for d in range(2):
        put_halo(field, d, above, d * weeks, weeks)
        put_halo(field, rows + 2 + d, below, d * weeks, weeks)

    @pl.loop(0, 4)
    def _(i):
        r = jnp.where(i < 2, i - 1, rows - 3 + i)
        keep = scale_of(r, rows, inside)
        out = laplace_row(row_of(field, r + 1), row_of(field, r + 2), row_of(field, r + 3), map_row(kappa, r + 3), mask)
        put_row(image, r + 1, [keep * t for t in out])

    @pl.loop(0, 4)
    def _(i):
        r = jnp.where(i < 2, i, rows - 4 + i)
        outer = laplace_row(row_of(image, r), row_of(image, r + 1), row_of(image, r + 2), map_row(kappa, r + 3), mask)
        out = [a - prior_scale * b for a, b in zip(row_of(grad, r), outer)]
        put_row(grad, r, out)
        put_row(search, r + 4, [a * b for a, b in zip(out, row_of(inv, r + 2))])

    for d in range(4):
        for c in range(0, cols, LANES):
            head[d * weeks : (d + 1) * weeks, c : c + LANES] = search[4 + d, :, c : c + LANES]
            tail[d * weeks : (d + 1) * weeks, c : c + LANES] = search[rows + d, :, c : c + LANES]
    for d in range(2):
        head[4 * weeks + d : 4 * weeks + d + 1, :] = eta[d]
        tail[4 * weeks + d : 4 * weeks + d + 1, :] = eta[rows - 2 + d]


def hessian_row(r, source, at, image, kappa, weight, mask):
    outer = laplace_row(image(r - 1), image(r), image(r + 1), map_row(kappa, r + 3), mask)
    mid = row_of(source, at)
    heavy = row_of(weight, r + 2)
    return mid, [
        prior_scale * o + (time_coupling * temporal_tile(m, mask) + h * m) for o, m, h in zip(outer, mid, heavy)
    ]


def inner_kernel(kappa, grad, weight, inv, search, first, image, second, second_image, last, sums):
    weeks = grad.shape[1]
    rows = grad.shape[0]
    mask = masks(weeks)

    @pl.loop(1, rows - 1)
    def _(r):
        put_row(first, r + 3, laplace_row(
            row_of(search, r + 3), row_of(search, r + 4), row_of(search, r + 5), map_row(kappa, r + 3), mask))

    zero = jnp.zeros((8, LANES), F32)

    def apply(r, carry):
        rz, pq, cross = carry
        mid, out = hessian_row(r, search, r + 4, lambda q: row_of(first, q + 3), kappa, weight, mask)
        other = [a * b for a, b in zip(out, row_of(inv, r + 2))]
        put_row(image, r, out)
        put_row(second, r + 2, other)
        return (
            rz + fold([a * b for a, b in zip(mid, row_of(grad, r))]),
            pq + fold([a * b for a, b in zip(mid, out)]),
            cross + fold([a * b for a, b in zip(other, out)]),
        )

    rz, pq, cross = lax.fori_loop(2, rows - 2, apply, (zero, zero, zero))

    @pl.loop(3, rows - 3)
    def _(r):
        put_row(second_image, r + 1, laplace_row(
            row_of(second, r + 1), row_of(second, r + 2), row_of(second, r + 3), map_row(kappa, r + 3), mask))

    def apply_second(r, total):
        mid, out = hessian_row(r, second, r + 2, lambda q: row_of(second_image, q + 1), kappa, weight, mask)
        put_row(last, r, out)
        return total + fold([a * b for a, b in zip(mid, out)])

    total = lax.fori_loop(4, rows - 4, apply_second, zero)
    for k, value in enumerate((rz, pq, cross, total)):
        sums[8 * k : 8 * k + 8, :] = value


def outer_kernel(inside, above, below, kappa, eta, land, field, grad, partial,
                 weight_in, inv_in, search_in, first_in, image_in, second_in, second_image_in, last_in,
                 weight, inv, search, first, image, second, second_image, last, sums):
    weeks = grad.shape[1]
    rows = grad.shape[0]
    mask = masks(weeks)
    for d in range(4):
        put_halo(search, d, above, d * weeks, weeks)
        put_halo(search, rows + 4 + d, below, d * weeks, weeks)

    @pl.loop(0, 4)
    def _(i):
        r = jnp.where(i < 2, i - 2, rows - 2 + i)
        eta_row, land_row, kap = map_row(eta, r + 2), map_row(land, r + 2), map_row(kappa, r + 3)
        heavy = []
        for j, tile in enumerate(row_of(field, r + 2)):
            curve = jnp.tanh(0.5 * (tile + eta_row[j]))
            heavy.append(land_row[j] * (1.0 - curve * curve))
        put_row(weight, r + 2, heavy)
        put_row(inv, r + 2, [1.0 / (diag_base(k) + h) for k, h in zip(kap, heavy)])

    @pl.loop(0, 8)
    def _(i):
        r = jnp.where(i < 4, i - 3, rows - 5 + i)
        keep = scale_of(r, rows, inside)
        out = laplace_row(
            row_of(search, r + 3), row_of(search, r + 4), row_of(search, r + 5), map_row(kappa, r + 3), mask)
        put_row(first, r + 3, [keep * t for t in out])

    def apply(i, carry):
        rz, pq, cross = carry
        r = jnp.where(i < 4, i - 2, rows - 6 + i)
        keep = scale_of(r, rows, inside)
        mine = jnp.where((r >= 0) & (r < rows), 1.0, 0.0)
        own = jnp.clip(r, 0, rows - 1)
        mid, out = hessian_row(r, search, r + 4, lambda q: row_of(first, q + 3), kappa, weight, mask)
        other = [keep * (a * b) for a, b in zip(out, row_of(inv, r + 2))]
        put_row(second, r + 2, other)

        @pl.when((r >= 0) & (r < rows))
        def _():
            put_row(image, own, out)

        return (
            rz + mine * fold([a * b for a, b in zip(mid, row_of(grad, own))]),
            pq + mine * fold([a * b for a, b in zip(mid, out)]),
            cross + mine * fold([a * b for a, b in zip(other, out)]),
        )

    rz, pq, cross = lax.fori_loop(0, 8, apply, tuple(partial[8 * k : 8 * k + 8, :] for k in range(3)))

    @pl.loop(0, 8)
    def _(i):
        r = jnp.where(i < 4, i - 1, rows - 7 + i)
        keep = scale_of(r, rows, inside)
        out = laplace_row(
            row_of(second, r + 1), row_of(second, r + 2), row_of(second, r + 3), map_row(kappa, r + 3), mask)
        put_row(second_image, r + 1, [keep * t for t in out])

    def apply_second(i, total):
        r = jnp.where(i < 4, i, rows - 8 + i)
        mid, out = hessian_row(r, second, r + 2, lambda q: row_of(second_image, q + 1), kappa, weight, mask)
        put_row(last, r, out)
        return total + fold([a * b for a, b in zip(mid, out)])

    total = lax.fori_loop(0, 8, apply_second, partial[24:32, :])
    sums[...] = jnp.zeros_like(sums)
    for k, value in enumerate((rz, pq, cross, total)):
        sums[k : k + 1, :] = jnp.sum(value, axis=0, keepdims=True)


def final_kernel(sums, grad, search, image, second, last, newton_out, residual_out, newton, residual, newton_sem, residual_sem):
    rows, weeks, cols = grad.shape
    rz, pq, cross, total = (jnp.sum(sums[k : k + 1, :], axis=1, keepdims=True) for k in range(4))
    first_step = rz / pq
    rz_next = first_step * first_step * cross - rz
    turn = 1.0 + rz_next / rz
    second_step = rz_next / (turn * (turn * pq - 2.0 * first_step * cross) + first_step * first_step * total)
    along = jnp.broadcast_to(first_step + second_step * turn, (weeks, LANES))
    across = jnp.broadcast_to(second_step * first_step, (weeks, LANES))

    def copies(r):
        return (
            pltpu.make_async_copy(newton.at[r], newton_out.at[:, r, :], newton_sem.at[r]),
            pltpu.make_async_copy(residual.at[r], residual_out.at[:, r, :], residual_sem.at[r]),
        )

    @pl.loop(0, rows)
    def _(r):
        put_row(newton, r, [along * p - across * y for p, y in zip(row_of(search, r + 4), row_of(second, r + 2))])
        put_row(residual, r, [
            g - along * w + across * h for g, w, h in zip(row_of(grad, r), row_of(image, r), row_of(last, r))])
        for copy in copies(r):
            copy.start()

    @pl.loop(0, rows)
    def _(r):
        for copy in copies(r):
            copy.wait()


def call(kernel, outs, ins, scratch=(), aliases=None, limit=2, flops=0, moved=0):
    shapes = tuple(VMEM(shape, F32) if space is VMEM else jax.ShapeDtypeStruct(shape, F32) for shape, space in outs)
    return pl.pallas_call(
        kernel,
        out_shape=shapes,
        in_specs=[pl.BlockSpec(memory_space=space) for _, space in ins],
        out_specs=tuple(pl.BlockSpec(memory_space=space) for _, space in outs),
        scratch_shapes=list(scratch),
        input_output_aliases=aliases or {},
        compiler_params=pltpu.CompilerParams(vmem_limit_bytes=limit * MIB),
        cost_estimate=pl.CostEstimate(flops=flops, bytes_accessed=moved, transcendentals=0),
    )(*[array for array, _ in ins])


def shards(latent, counts, land_mask, region_ids, kappa_sq, covariates, effects, intercepts):
    weeks, rows, cols = latent.shape
    me = lax.axis_index(AX)
    land_own = land_mask.astype(F32)
    inside = jnp.stack([me > 0, me < lax.axis_size(AX) - 1]).astype(F32)

    def pack(wide, flat):
        return jnp.concatenate([jnp.transpose(wide, (1, 0, 2)).reshape(-1, cols)] + flat, axis=0)

    head = pack(latent[:, :2], [kappa_sq[:3], land_own[:2]])
    tail = pack(latent[:, -2:], [kappa_sq[-3:], land_own[-2:]])
    above, below = swap_halos(head, tail)
    cut = 2 * weeks

    def ext(depth):
        return ((rows + 2 * depth, weeks, cols), VMEM)

    def as_map(flat):
        return flat.reshape(-1, 1, cols)

    cells = weeks * rows * cols
    SMEM, ANY = pltpu.SMEM, pl.ANY
    field, grad, weight, inv, search, image, eta = call(
        start_kernel,
        [ext(2), ext(0), ext(2), ext(2), ext(4), ext(1), ((rows, 1, cols), VMEM)],
        [(effects.astype(F32), SMEM), (intercepts, SMEM), (latent, ANY), (counts, ANY), (covariates, ANY),
         (as_map(land_own), VMEM), (region_ids, VMEM), (as_map(kappa_sq), VMEM)],
        scratch=[pltpu.VMEM((rows, weeks, cols), jnp.int32), pltpu.VMEM(covariates.shape, covariates.dtype),
                 pltpu.SemaphoreType.DMA((rows,)), pltpu.SemaphoreType.DMA((rows,)), pltpu.SemaphoreType.DMA],
        flops=80 * cells, moved=12 * cells, limit=8,
    )
    kappa = as_map(jnp.concatenate([above[cut : cut + 3], kappa_sq, below[cut : cut + 3]]))
    land = as_map(jnp.concatenate([above[cut + 3 :], land_own, below[cut + 3 :]]))
    packed = ((4 * weeks + 8, cols), VMEM)
    field, grad, search, image, head, tail = call(
        edge_kernel,
        [ext(2), ext(0), ext(4), ext(1), packed, packed],
        [(inside, SMEM), (above, VMEM), (below, VMEM), (kappa, VMEM), (eta, VMEM), (inv, VMEM),
         (field, VMEM), (grad, VMEM), (search, VMEM), (image, VMEM)],
        aliases={6: 0, 7: 1, 8: 2, 9: 3},
        flops=10 * cells, moved=cells,
    )
    above, below = swap_halos(head, tail)
    first, image, second, second_image, last, partial = call(
        inner_kernel,
        [ext(3), ext(0), ext(2), ext(1), ext(0), ((32, LANES), VMEM)],
        [(kappa, VMEM), (grad, VMEM), (weight, VMEM), (inv, VMEM), (search, VMEM)],
        flops=80 * cells, moved=12 * cells,
    )
    cut = 4 * weeks
    eta = jnp.concatenate([as_map(above[cut : cut + 2]), eta, as_map(below[cut : cut + 2])])
    weight, inv, search, first, image, second, second_image, last, sums = call(
        outer_kernel,
        [ext(2), ext(2), ext(4), ext(3), ext(0), ext(2), ext(1), ext(0), ((8, LANES), VMEM)],
        [(inside, SMEM), (above, VMEM), (below, VMEM), (kappa, VMEM), (eta, VMEM), (land, VMEM), (field, VMEM),
         (grad, VMEM), (partial, VMEM), (weight, VMEM), (inv, VMEM), (search, VMEM), (first, VMEM), (image, VMEM),
         (second, VMEM), (second_image, VMEM), (last, VMEM)],
        aliases={9 + k: k for k in range(8)},
        flops=20 * cells, moved=cells,
    )
    return call(
        final_kernel,
        [(latent.shape, ANY), (latent.shape, ANY)],
        [(all_sum(sums), VMEM), (grad, VMEM), (search, VMEM), (image, VMEM), (second, VMEM), (last, VMEM)],
        scratch=[pltpu.VMEM((rows, weeks, cols), F32), pltpu.VMEM((rows, weeks, cols), F32),
                 pltpu.SemaphoreType.DMA((rows,)), pltpu.SemaphoreType.DMA((rows,))],
        flops=8 * cells, moved=8 * cells, limit=6,
    )


def solution(mesh):
    placed = (
        P(None, "gx", "region"),
        P(None, "gx", "region"),
        P("gx", "region"),
        P("gx", "region"),
        P("gx", "region"),
        P(None, "gx", "region"),
        P("region"),
        P("region"),
    )
    return jax.shard_map(
        shards,
        mesh=mesh,
        in_specs=placed,
        out_specs=(P(None, "gx", "region"), P(None, "gx", "region")),
        check_vma=False,
    )
```

```python
import functools

import jax
import jax.numpy as jnp
from jax import lax
from jax.experimental import pallas as pl
from jax.experimental.pallas import tpu as pltpu
from jax.sharding import PartitionSpec as P

AX = "gx"
LANES = 128
prior_scale = 0.04
time_coupling = 0.5
F32 = jnp.float32
VMEM = pltpu.VMEM
MIB = 1 << 20


def pair_maps(count):
    first = [(i, i ^ 1) for i in range(count) if (i ^ 1) < count]
    second = [(i, ((i + 1) ^ 1) - 1) for i in range(count) if 0 <= ((i + 1) ^ 1) - 1 < count]
    return first, second


def all_sum(values):
    count = lax.axis_size(AX)
    if count & (count - 1):
        return lax.psum(values, AX)
    step = 1
    while step < count:
        values = values + lax.ppermute(values, AX, [(i, i ^ step) for i in range(count)])
        step *= 2
    return values


def row_of(ref, row):
    return [ref[row, :, c : c + LANES] for c in range(0, ref.shape[2], LANES)]


def put_row(ref, row, tiles):
    for j, tile in enumerate(tiles):
        ref[row, :, j * LANES : (j + 1) * LANES] = tile


def map_row(ref, row):
    return [ref[row, :, c : c + LANES] for c in range(0, ref.shape[2], LANES)]


def masks(weeks):
    lane = lax.broadcasted_iota(jnp.int32, (weeks, LANES), 1)
    week = lax.broadcasted_iota(jnp.int32, (weeks, LANES), 0)
    return lane == 0, lane == LANES - 1, week == 0, week == weeks - 1


def laplace_row(up, mid, down, kappa, mask):
    first, last = mask[0], mask[1]
    count = len(mid)
    to_right = [pltpu.roll(t, 1, 1) for t in mid]
    to_left = [pltpu.roll(t, LANES - 1, 1) for t in mid]
    out = []
    for j in range(count):
        west = jnp.where(first, to_right[j - 1] if j > 0 else 0.0, to_right[j])
        east = jnp.where(last, to_left[j + 1] if j + 1 < count else 0.0, to_left[j])
        out.append((kappa[j] + 4.0) * mid[j] - ((up[j] + down[j]) + (west + east)))
    return out


def temporal_tile(tile, mask):
    weeks = tile.shape[0]
    before = jnp.where(mask[2], tile, pltpu.roll(tile, 1, 0))
    after = jnp.where(mask[3], tile, pltpu.roll(tile, weeks - 1, 0))
    return (2.0 * tile - before) - after


def fold(tiles):
    parts = [t[h : h + 8] for t in tiles for h in range(0, t.shape[0], 8)]
    while len(parts) > 1:
        parts = [a + b for a, b in zip(parts[::2], parts[1::2])] + ([parts[-1]] if len(parts) % 2 else [])
    return parts[0]


def diag_base(kappa):
    return prior_scale * ((kappa + 4.0) * (kappa + 4.0) + 4.0) + 2.0 * time_coupling


def is_odd():
    return lax.axis_index(AX) % 2 == 1


def row_loop(low, high, body, carry=None, most=14):
    count = high - low
    step = max(k for k in range(1, most + 1) if count % k == 0)

    def chunk(i, value):
        for k in range(step):
            value = body(low + i * step + k, value)
        return value

    if step == count:
        return chunk(0, carry)
    if carry is None:
        lax.fori_loop(0, count // step, lambda i, z: (chunk(i, None), z)[1], 0)
        return None
    return lax.fori_loop(0, count // step, chunk, carry)


def pack_kernel(latent, kappa, land, first, second, kappa_out, land_out, sems):
    weeks, rows, cols = latent.shape
    odd = is_odd()
    copies = []
    for k, (out, base) in enumerate(((first, jnp.where(odd, 0, rows - 2)), (second, jnp.where(odd, rows - 2, 0)))):
        for d in range(2):
            copies.append(pltpu.make_async_copy(
                latent.at[:, base + d, :], out.at[d * weeks : (d + 1) * weeks, :], sems.at[2 * k + d]))
    for copy in copies:
        copy.start()
    for r in range(rows):
        kappa_out[r + 3] = kappa[r : r + 1, :]
        land_out[r] = land[r : r + 1, :].astype(F32)
    at = 2 * weeks
    for d in range(3):
        top, bottom = kappa[d : d + 1, :], kappa[rows - 3 + d : rows - 2 + d, :]
        first[at + d : at + d + 1, :] = jnp.where(odd, top, bottom)
        second[at + d : at + d + 1, :] = jnp.where(odd, bottom, top)
    for d in range(2):
        top, bottom = (land[q : q + 1, :].astype(F32) for q in (d, rows - 2 + d))
        first[at + 3 + d : at + 4 + d, :] = jnp.where(odd, top, bottom)
        second[at + 3 + d : at + 4 + d, :] = jnp.where(odd, bottom, top)
    first[at + 5 :, :] = jnp.zeros((3, cols), F32)
    second[at + 5 :, :] = jnp.zeros((3, cols), F32)
    for copy in copies:
        copy.wait()


def start_kernel(effects, intercepts, latent, counts, covariates, land, zones, kappa,
                 field, grad, weight, inv, search, image, eta,
                 tally, covs, field_sem, tally_sem, cov_sem):
    weeks, rows, cols = latent.shape
    num_covs = covariates.shape[0]
    mask = masks(weeks)

    def field_copy(r):
        return pltpu.make_async_copy(latent.at[:, r, :], field.at[r + 2], field_sem.at[r])

    def tally_copy(r):
        return pltpu.make_async_copy(counts.at[:, r, :], tally.at[r], tally_sem.at[r])

    cov_copy = pltpu.make_async_copy(covariates, covs, cov_sem)
    for r in range(rows):
        field_copy(r).start()
    cov_copy.start()
    for r in range(rows):
        tally_copy(r).start()
    field_copy(0).wait()
    field_copy(1).wait()

    def inner_image(r, _):
        field_copy(r + 1).wait()
        put_row(image, r + 1, laplace_row(
            row_of(field, r + 1), row_of(field, r + 2), row_of(field, r + 3), map_row(kappa, r + 3), mask))

    row_loop(1, rows - 1, inner_image)
    cov_copy.wait()
    width = 2 * LANES
    for c in range(0, cols, width):
        total = jnp.zeros((rows, width), F32)
        ids = zones[:, c : c + width]
        for z in range(intercepts.shape[0]):
            total = jnp.where(ids == z, intercepts[z], total)
        for k in range(num_covs):
            total = total + effects[k] * covs[k, :, c : c + width].astype(F32)
        for r in range(rows):
            eta[r, :, c : c + width] = total[r : r + 1]

    def pointwise(r):
        tally_copy(r).wait()
        lat, eta_row, land_row, kap, count_row = (
            row_of(field, r + 2), map_row(eta, r), map_row(land, r), map_row(kappa, r + 3), row_of(tally, r))
        out, heavy, inverse = [], [], []
        for j, tile in enumerate(lat):
            on = land_row[j]
            curve = jnp.tanh(0.5 * (tile + eta_row[j]))
            heavy.append(on * (1.0 - curve * curve))
            inverse.append(1.0 / (diag_base(kap[j]) + heavy[j]))
            out.append(on * (count_row[j].astype(F32) - 2.0 - 2.0 * curve) - time_coupling * temporal_tile(tile, mask))
        put_row(weight, r + 2, heavy)
        put_row(inv, r + 2, inverse)
        return out, inverse, kap

    for r in (0, 1, rows - 2, rows - 1):
        put_row(grad, r, pointwise(r)[0])

    def gradient(r, _):
        out, inverse, kap = pointwise(r)
        outer = laplace_row(row_of(image, r), row_of(image, r + 1), row_of(image, r + 2), kap, mask)
        out = [a - prior_scale * b for a, b in zip(out, outer)]
        put_row(grad, r, out)
        put_row(search, r + 4, [a * b for a, b in zip(out, inverse)])

    row_loop(2, rows - 2, gradient, most=7)


def keep_inside(r, rows, tiles):
    if 0 <= r < rows:
        return tiles
    place, count = lax.axis_index(AX), lax.axis_size(AX)
    keep = jnp.where(place > 0 if r < 0 else place < count - 1, 1.0, 0.0)
    return [keep * t for t in tiles]


def halo_row(r, rows, depth, height, first, second):
    odd = is_odd()
    at = (r + depth if r < 0 else r - rows) * height
    a, b = (first, second) if r < 0 else (second, first)
    return [jnp.where(odd, a[at : at + height, c : c + LANES], b[at : at + height, c : c + LANES])
            for c in range(0, first.shape[1], LANES)]


def halo_line(above, line, first, second):
    odd = is_odd()
    a, b = (first, second) if above else (second, first)
    return [jnp.where(odd, a[line : line + 1, c : c + LANES], b[line : line + 1, c : c + LANES])
            for c in range(0, first.shape[1], LANES)]


def edge_kernel(got_first, got_second, eta, inv, kappa_in, field_in, grad_in, search_in, image_in,
                kappa, field, grad, search, image, first, second):
    weeks = field.shape[1]
    rows, _, cols = eta.shape
    mask = masks(weeks)
    odd = is_odd()
    for d in range(2):
        put_row(field, d, halo_row(d - 2, rows, 2, weeks, got_first, got_second))
        put_row(field, rows + 2 + d, halo_row(rows + d, rows, 2, weeks, got_first, got_second))
    for d in range(3):
        put_row(kappa, d, halo_line(True, 2 * weeks + d, got_first, got_second))
        put_row(kappa, rows + 3 + d, halo_line(False, 2 * weeks + d, got_first, got_second))
    for r in (-1, 0, rows - 1, rows):
        put_row(image, r + 1, keep_inside(r, rows, laplace_row(
            row_of(field, r + 1), row_of(field, r + 2), row_of(field, r + 3), map_row(kappa, r + 3), mask)))
    for r in (0, 1, rows - 2, rows - 1):
        outer = laplace_row(row_of(image, r), row_of(image, r + 1), row_of(image, r + 2), map_row(kappa, r + 3), mask)
        out = [a - prior_scale * b for a, b in zip(row_of(grad, r), outer)]
        put_row(grad, r, out)
        put_row(search, r + 4, [a * b for a, b in zip(out, row_of(inv, r + 2))])
    at = 4 * weeks
    for c in range(0, cols, LANES):
        part = slice(c, c + LANES)
        for d in range(4):
            top, bottom = search[4 + d, :, part], search[rows + d, :, part]
            first[d * weeks : (d + 1) * weeks, part] = jnp.where(odd, top, bottom)
            second[d * weeks : (d + 1) * weeks, part] = jnp.where(odd, bottom, top)
        for d in range(2):
            top, bottom = eta[d, :, part], eta[rows - 2 + d, :, part]
            first[at + d : at + d + 1, part] = jnp.where(odd, top, bottom)
            second[at + d : at + d + 1, part] = jnp.where(odd, bottom, top)
        first[at + 2 :, part] = jnp.zeros((6, LANES), F32)
        second[at + 2 :, part] = jnp.zeros((6, LANES), F32)


def hessian_row(r, source, at, image, offset, kappa, weight, mask):
    outer = laplace_row(row_of(image, r + offset - 1), row_of(image, r + offset), row_of(image, r + offset + 1),
                        map_row(kappa, r + 3), mask)
    mid = row_of(source, at)
    heavy = row_of(weight, r + 2)
    return mid, [
        prior_scale * o + (time_coupling * temporal_tile(m, mask) + h * m) for o, m, h in zip(outer, mid, heavy)
    ]


def dot_rows(a, b):
    return fold([x * y for x, y in zip(a, b)])


def inner_kernel(kappa, grad, weight, inv, search, first, image, second, second_image, last, sums):
    weeks = grad.shape[1]
    rows = grad.shape[0]
    mask = masks(weeks)

    def inner_image(r, _):
        put_row(first, r + 3, laplace_row(
            row_of(search, r + 3), row_of(search, r + 4), row_of(search, r + 5), map_row(kappa, r + 3), mask))

    row_loop(1, rows - 1, inner_image)
    zero = jnp.zeros((8, LANES), F32)

    def apply(r, carry):
        rz, pq, cross = carry
        mid, out = hessian_row(r, search, r + 4, first, 3, kappa, weight, mask)
        other = [a * b for a, b in zip(out, row_of(inv, r + 2))]
        put_row(image, r, out)
        put_row(second, r + 2, other)
        return rz + dot_rows(mid, row_of(grad, r)), pq + dot_rows(mid, out), cross + dot_rows(other, out)

    rz, pq, cross = row_loop(2, rows - 2, apply, (zero, zero, zero), most=7)

    def second_inner(r, _):
        put_row(second_image, r + 1, laplace_row(
            row_of(second, r + 1), row_of(second, r + 2), row_of(second, r + 3), map_row(kappa, r + 3), mask))

    row_loop(3, rows - 3, second_inner)

    def apply_second(r, total):
        mid, out = hessian_row(r, second, r + 2, second_image, 1, kappa, weight, mask)
        put_row(last, r, out)
        return total + dot_rows(mid, out)

    total = row_loop(4, rows - 4, apply_second, zero, most=8)
    for k, value in enumerate((rz, pq, cross, total)):
        sums[8 * k : 8 * k + 8, :] = value


def outer_kernel(old_first, old_second, got_first, got_second, kappa, field, grad, partial,
                 weight_in, inv_in, search_in, first_in, image_in, second_in, second_image_in, last_in,
                 weight, inv, search, first, image, second, second_image, last, sums):
    weeks = grad.shape[1]
    rows = grad.shape[0]
    mask = masks(weeks)
    for d in range(4):
        put_row(search, d, halo_row(d - 4, rows, 4, weeks, got_first, got_second))
        put_row(search, rows + 4 + d, halo_row(rows + d, rows, 4, weeks, got_first, got_second))
    for above in (True, False):
        for d in range(2):
            r = d - 2 if above else rows + d
            eta_row = halo_line(above, 4 * weeks + d, got_first, got_second)
            land_row = halo_line(above, 2 * weeks + 3 + d, old_first, old_second)
            heavy = []
            for j, tile in enumerate(row_of(field, r + 2)):
                curve = jnp.tanh(0.5 * (tile + eta_row[j]))
                heavy.append(land_row[j] * (1.0 - curve * curve))
            put_row(weight, r + 2, heavy)
            put_row(inv, r + 2, [1.0 / (diag_base(k) + h) for k, h in zip(map_row(kappa, r + 3), heavy)])

    for r in (-3, -2, -1, 0, rows - 1, rows, rows + 1, rows + 2):
        put_row(first, r + 3, keep_inside(r, rows, laplace_row(
            row_of(search, r + 3), row_of(search, r + 4), row_of(search, r + 5), map_row(kappa, r + 3), mask)))
    rz, pq, cross, total = (partial[8 * k : 8 * k + 8, :] for k in range(4))
    for r in (-2, -1, 0, 1, rows - 2, rows - 1, rows, rows + 1):
        mid, out = hessian_row(r, search, r + 4, first, 3, kappa, weight, mask)
        other = keep_inside(r, rows, [a * b for a, b in zip(out, row_of(inv, r + 2))])
        put_row(second, r + 2, other)
        if 0 <= r < rows:
            put_row(image, r, out)
            rz, pq, cross = rz + dot_rows(mid, row_of(grad, r)), pq + dot_rows(mid, out), cross + dot_rows(other, out)
    for r in (-1, 0, 1, 2, rows - 3, rows - 2, rows - 1, rows):
        put_row(second_image, r + 1, keep_inside(r, rows, laplace_row(
            row_of(second, r + 1), row_of(second, r + 2), row_of(second, r + 3), map_row(kappa, r + 3), mask)))
    for r in (0, 1, 2, 3, rows - 4, rows - 3, rows - 2, rows - 1):
        mid, out = hessian_row(r, second, r + 2, second_image, 1, kappa, weight, mask)
        put_row(last, r, out)
        total = total + dot_rows(mid, out)
    sums[...] = jnp.zeros_like(sums)
    for k, value in enumerate((rz, pq, cross, total)):
        sums[k : k + 1, :] = jnp.sum(value, axis=0, keepdims=True)


def final_kernel(sums, grad, search, image, second, last, newton_out, residual_out, newton, residual, newton_sem, residual_sem):
    rows, weeks, cols = grad.shape
    rz, pq, cross, total = (jnp.sum(sums[k : k + 1, :], axis=1, keepdims=True) for k in range(4))
    first_step = rz / pq
    rz_next = first_step * first_step * cross - rz
    turn = 1.0 + rz_next / rz
    second_step = rz_next / (turn * (turn * pq - 2.0 * first_step * cross) + first_step * first_step * total)
    along = jnp.broadcast_to(first_step + second_step * turn, (weeks, LANES))
    across = jnp.broadcast_to(second_step * first_step, (weeks, LANES))

    def copies(r):
        return (
            pltpu.make_async_copy(newton.at[r], newton_out.at[:, r, :], newton_sem.at[r]),
            pltpu.make_async_copy(residual.at[r], residual_out.at[:, r, :], residual_sem.at[r]),
        )

    def combine(r, _):
        put_row(newton, r, [along * p - across * y for p, y in zip(row_of(search, r + 4), row_of(second, r + 2))])
        put_row(residual, r, [
            g - along * w + across * h for g, w, h in zip(row_of(grad, r), row_of(image, r), row_of(last, r))])
        for copy in copies(r):
            copy.start()

    row_loop(0, rows, combine, most=8)
    for r in range(rows):
        for copy in copies(r):
            copy.wait()


def call(kernel, outs, ins, scratch=(), aliases=None, limit=2, flops=0, moved=0):
    shapes = tuple(VMEM(shape, F32) if space is VMEM else jax.ShapeDtypeStruct(shape, F32) for shape, space in outs)
    return pl.pallas_call(
        kernel,
        out_shape=shapes,
        in_specs=[pl.BlockSpec(memory_space=space) for _, space in ins],
        out_specs=tuple(pl.BlockSpec(memory_space=space) for _, space in outs),
        scratch_shapes=list(scratch),
        input_output_aliases=aliases or {},
        compiler_params=pltpu.CompilerParams(vmem_limit_bytes=limit * MIB),
        cost_estimate=pl.CostEstimate(flops=flops, bytes_accessed=moved, transcendentals=0),
    )(*[pltpu.with_memory_space_constraint(array, space) if space is pltpu.HBM else array for array, space in ins])


def shards(latent, counts, land_mask, region_ids, kappa_sq, covariates, effects, intercepts):
    weeks, rows, cols = latent.shape
    swap, cross = pair_maps(lax.axis_size(AX))

    def ext(depth):
        return ((rows + 2 * depth, weeks, cols), VMEM)

    def maps(depth):
        return ((rows + 2 * depth, 1, cols), VMEM)

    cells = weeks * rows * cols
    SMEM, ANY, HBM, DMA = pltpu.SMEM, pl.ANY, pltpu.HBM, pltpu.SemaphoreType.DMA
    packed = ((2 * weeks + 8, cols), VMEM)
    near, far, kappa, land = call(
        pack_kernel,
        [packed, packed, maps(3), maps(0)],
        [(latent, HBM), (kappa_sq, VMEM), (land_mask, VMEM)],
        scratch=[DMA((4,))],
        flops=cells // 16, moved=cells,
    )
    old_near, old_far = lax.ppermute(near, AX, swap), lax.ppermute(far, AX, cross)
    field, grad, weight, inv, search, image, eta = call(
        start_kernel,
        [ext(2), ext(0), ext(2), ext(2), ext(4), ext(1), maps(0)],
        [(effects.astype(F32), SMEM), (intercepts, SMEM), (latent, ANY), (counts, HBM), (covariates, HBM),
         (land, VMEM), (region_ids, VMEM), (kappa, VMEM)],
        scratch=[pltpu.VMEM((rows, weeks, cols), jnp.int32), pltpu.VMEM(covariates.shape, covariates.dtype),
                 DMA((rows,)), DMA((rows,)), DMA],
        flops=80 * cells, moved=12 * cells, limit=8,
    )
    packed = ((4 * weeks + 8, cols), VMEM)
    kappa, field, grad, search, image, near, far = call(
        edge_kernel,
        [maps(3), ext(2), ext(0), ext(4), ext(1), packed, packed],
        [(old_near, VMEM), (old_far, VMEM), (eta, VMEM), (inv, VMEM),
         (kappa, VMEM), (field, VMEM), (grad, VMEM), (search, VMEM), (image, VMEM)],
        aliases={4 + k: k for k in range(5)},
        flops=10 * cells, moved=cells,
    )
    near, far = lax.ppermute(near, AX, swap), lax.ppermute(far, AX, cross)
    first, image, second, second_image, last, partial = call(
        inner_kernel,
        [ext(3), ext(0), ext(2), ext(1), ext(0), ((32, LANES), VMEM)],
        [(kappa, VMEM), (grad, VMEM), (weight, VMEM), (inv, VMEM), (search, VMEM)],
        flops=80 * cells, moved=12 * cells,
    )
    weight, inv, search, first, image, second, second_image, last, sums = call(
        outer_kernel,
        [ext(2), ext(2), ext(4), ext(3), ext(0), ext(2), ext(1), ext(0), ((8, LANES), VMEM)],
        [(old_near, VMEM), (old_far, VMEM), (near, VMEM), (far, VMEM), (kappa, VMEM), (field, VMEM),
         (grad, VMEM), (partial, VMEM), (weight, VMEM), (inv, VMEM), (search, VMEM), (first, VMEM), (image, VMEM),
         (second, VMEM), (second_image, VMEM), (last, VMEM)],
        aliases={8 + k: k for k in range(8)},
        flops=20 * cells, moved=cells,
    )
    return call(
        final_kernel,
        [(latent.shape, ANY), (latent.shape, ANY)],
        [(all_sum(sums), VMEM), (grad, VMEM), (search, VMEM), (image, VMEM), (second, VMEM), (last, VMEM)],
        scratch=[pltpu.VMEM((rows, weeks, cols), F32), pltpu.VMEM((rows, weeks, cols), F32), DMA((rows,)), DMA((rows,))],
        flops=8 * cells, moved=8 * cells, limit=6,
    )


def solution(mesh):
    placed = (
        P(None, "gx", "region"),
        P(None, "gx", "region"),
        P("gx", "region"),
        P("gx", "region"),
        P("gx", "region"),
        P(None, "gx", "region"),
        P("region"),
        P("region"),
    )
    return jax.shard_map(
        shards,
        mesh=mesh,
        in_specs=placed,
        out_specs=(P(None, "gx", "region"), P(None, "gx", "region")),
        check_vma=False,
    )
```

```python
import functools

import jax
import jax.numpy as jnp
from jax import lax
from jax.experimental import pallas as pl
from jax.experimental.pallas import tpu as pltpu
from jax.sharding import PartitionSpec as P

AX = "gx"
LANES = 128
prior_scale = 0.04
time_coupling = 0.5
F32 = jnp.float32
VMEM = pltpu.VMEM
MIB = 1 << 20


def pair_maps(count):
    first = [(i, i ^ 1) for i in range(count) if (i ^ 1) < count]
    second = [(i, ((i + 1) ^ 1) - 1) for i in range(count) if 0 <= ((i + 1) ^ 1) - 1 < count]
    return first, second


def all_sum(values):
    count = lax.axis_size(AX)
    if count & (count - 1):
        return lax.psum(values, AX)
    step = 1
    while step < count:
        values = values + lax.ppermute(values, AX, [(i, i ^ step) for i in range(count)])
        step *= 2
    return values


def row_of(ref, row):
    return [ref[row, :, c : c + LANES] for c in range(0, ref.shape[2], LANES)]


def put_row(ref, row, tiles):
    for j, tile in enumerate(tiles):
        ref[row, :, j * LANES : (j + 1) * LANES] = tile


def map_row(ref, row):
    return [ref[row, :, c : c + LANES] for c in range(0, ref.shape[2], LANES)]


def masks(weeks):
    lane = lax.broadcasted_iota(jnp.int32, (weeks, LANES), 1)
    week = lax.broadcasted_iota(jnp.int32, (weeks, LANES), 0)
    return lane == 0, lane == LANES - 1, week == 0, week == weeks - 1


def laplace_row(up, mid, down, kappa, mask):
    first, last = mask[0], mask[1]
    count = len(mid)
    to_right = [pltpu.roll(t, 1, 1) for t in mid]
    to_left = [pltpu.roll(t, LANES - 1, 1) for t in mid]
    out = []
    for j in range(count):
        west = jnp.where(first, to_right[j - 1] if j > 0 else 0.0, to_right[j])
        east = jnp.where(last, to_left[j + 1] if j + 1 < count else 0.0, to_left[j])
        out.append((kappa[j] + 4.0) * mid[j] - ((up[j] + down[j]) + (west + east)))
    return out


def temporal_tile(tile, mask):
    weeks = tile.shape[0]
    before = jnp.where(mask[2], tile, pltpu.roll(tile, 1, 0))
    after = jnp.where(mask[3], tile, pltpu.roll(tile, weeks - 1, 0))
    return (2.0 * tile - before) - after


def fold(tiles):
    parts = [t[h : h + 8] for t in tiles for h in range(0, t.shape[0], 8)]
    while len(parts) > 1:
        parts = [a + b for a, b in zip(parts[::2], parts[1::2])] + ([parts[-1]] if len(parts) % 2 else [])
    return parts[0]


def diag_base(kappa):
    return prior_scale * ((kappa + 4.0) * (kappa + 4.0) + 4.0) + 2.0 * time_coupling


def is_odd():
    return lax.axis_index(AX) % 2 == 1


def row_loop(low, high, body, carry=None, most=14):
    count = high - low
    step = max(k for k in range(1, most + 1) if count % k == 0)

    def chunk(i, value):
        for k in range(step):
            value = body(low + i * step + k, value)
        return value

    if step == count:
        return chunk(0, carry)
    if carry is None:
        lax.fori_loop(0, count // step, lambda i, z: (chunk(i, None), z)[1], 0)
        return None
    return lax.fori_loop(0, count // step, chunk, carry)


def pack_kernel(latent, kappa_hbm, land_hbm, first, second, kappa_out, land_out, kappa, land, sems):
    weeks, rows, cols = latent.shape
    odd = is_odd()
    map_copies = [pltpu.make_async_copy(kappa_hbm, kappa, sems.at[4]), pltpu.make_async_copy(land_hbm, land, sems.at[5])]
    copies = []
    for k, (out, base) in enumerate(((first, jnp.where(odd, 0, rows - 2)), (second, jnp.where(odd, rows - 2, 0)))):
        for d in range(2):
            copies.append(pltpu.make_async_copy(
                latent.at[:, base + d, :], out.at[d * weeks : (d + 1) * weeks, :], sems.at[2 * k + d]))
    for copy in map_copies + copies:
        copy.start()
    for copy in map_copies:
        copy.wait()
    for r in range(rows):
        kappa_out[r + 3] = kappa[r : r + 1, :]
        land_out[r] = land[r : r + 1, :].astype(F32)
    at = 2 * weeks
    for d in range(3):
        top, bottom = kappa[d : d + 1, :], kappa[rows - 3 + d : rows - 2 + d, :]
        first[at + d : at + d + 1, :] = jnp.where(odd, top, bottom)
        second[at + d : at + d + 1, :] = jnp.where(odd, bottom, top)
    for d in range(2):
        top, bottom = (land[q : q + 1, :].astype(F32) for q in (d, rows - 2 + d))
        first[at + 3 + d : at + 4 + d, :] = jnp.where(odd, top, bottom)
        second[at + 3 + d : at + 4 + d, :] = jnp.where(odd, bottom, top)
    first[at + 5 :, :] = jnp.zeros((3, cols), F32)
    second[at + 5 :, :] = jnp.zeros((3, cols), F32)
    for copy in copies:
        copy.wait()


def rows_first(source, target, shift):
    weeks, rows, cols = source.shape
    for r in range(0, rows, 8):
        for c in range(0, cols, LANES):
            block = source[:, r : r + 8, c : c + LANES].astype(F32)
            target[r + shift : r + shift + 8, :, c : c + LANES] = jnp.swapaxes(block, 0, 1)


def front_kernel(effects, intercepts, latent, covariates, zones, kappa, counts,
                 field, image, eta, tally, covs, raw, cov_sem, sem):
    weeks, rows, cols = latent.shape
    mask = masks(weeks)
    copy = pltpu.make_async_copy(counts, raw, sem)
    cov_copy = pltpu.make_async_copy(covariates, covs, cov_sem)
    cov_copy.start()
    copy.start()
    rows_first(latent, field, 2)

    def inner_image(r, _):
        put_row(image, r + 1, laplace_row(
            row_of(field, r + 1), row_of(field, r + 2), row_of(field, r + 3), map_row(kappa, r + 3), mask))

    row_loop(1, rows - 1, inner_image)
    cov_copy.wait()
    width = 2 * LANES
    for c in range(0, cols, width):
        total = jnp.zeros((rows, width), F32)
        ids = zones[:, c : c + width]
        for z in range(intercepts.shape[0]):
            total = jnp.where(ids == z, intercepts[z], total)
        for k in range(covs.shape[0]):
            total = total + effects[k] * covs[k, :, c : c + width].astype(F32)
        for r in range(rows):
            eta[r, :, c : c + width] = total[r : r + 1]
    copy.wait()
    rows_first(raw, tally, 0)


def gradient_row(r, field, tally, eta, land, kappa, image, grad, weight, inv, search, mask):
    outer = laplace_row(row_of(image, r), row_of(image, r + 1), row_of(image, r + 2), map_row(kappa, r + 3), mask)
    eta_row, land_row, kap, count_row = map_row(eta, r), map_row(land, r), map_row(kappa, r + 3), row_of(tally, r)
    for j, tile in enumerate(row_of(field, r + 2)):
        on = land_row[j]
        curve = jnp.tanh(0.5 * (tile + eta_row[j]))
        heavy = on * (1.0 - curve * curve)
        inverse = 1.0 / (diag_base(kap[j]) + heavy)
        out = on * (count_row[j] - 2.0 - 2.0 * curve) - time_coupling * temporal_tile(tile, mask)
        out = out - prior_scale * outer[j]
        part = slice(j * LANES, (j + 1) * LANES)
        weight[r + 2, :, part] = heavy
        inv[r + 2, :, part] = inverse
        grad[r, :, part] = out
        search[r + 4, :, part] = out * inverse


def keep_inside(r, rows, tiles):
    if 0 <= r < rows:
        return tiles
    place, count = lax.axis_index(AX), lax.axis_size(AX)
    keep = jnp.where(place > 0 if r < 0 else place < count - 1, 1.0, 0.0)
    return [keep * t for t in tiles]


def halo_row(r, rows, depth, height, first, second):
    odd = is_odd()
    at = (r + depth if r < 0 else r - rows) * height
    a, b = (first, second) if r < 0 else (second, first)
    return [jnp.where(odd, a[at : at + height, c : c + LANES], b[at : at + height, c : c + LANES])
            for c in range(0, first.shape[1], LANES)]


def halo_line(above, line, first, second):
    odd = is_odd()
    a, b = (first, second) if above else (second, first)
    return [jnp.where(odd, a[line : line + 1, c : c + LANES], b[line : line + 1, c : c + LANES])
            for c in range(0, first.shape[1], LANES)]


def edge_kernel(got_first, got_second, eta, land, tally, kappa_in, field_in, image_in,
                kappa, field, image, grad, weight, inv, search, first, second):
    weeks = field.shape[1]
    rows, _, cols = eta.shape
    mask = masks(weeks)
    odd = is_odd()
    for d in range(2):
        put_row(field, d, halo_row(d - 2, rows, 2, weeks, got_first, got_second))
        put_row(field, rows + 2 + d, halo_row(rows + d, rows, 2, weeks, got_first, got_second))
    for d in range(3):
        put_row(kappa, d, halo_line(True, 2 * weeks + d, got_first, got_second))
        put_row(kappa, rows + 3 + d, halo_line(False, 2 * weeks + d, got_first, got_second))
    for r in (-1, 0, rows - 1, rows):
        put_row(image, r + 1, keep_inside(r, rows, laplace_row(
            row_of(field, r + 1), row_of(field, r + 2), row_of(field, r + 3), map_row(kappa, r + 3), mask)))
    for r in (0, 1, 2, 3, rows - 4, rows - 3, rows - 2, rows - 1):
        gradient_row(r, field, tally, eta, land, kappa, image, grad, weight, inv, search, mask)
    at = 4 * weeks
    for c in range(0, cols, LANES):
        part = slice(c, c + LANES)
        for d in range(4):
            top, bottom = search[4 + d, :, part], search[rows + d, :, part]
            first[d * weeks : (d + 1) * weeks, part] = jnp.where(odd, top, bottom)
            second[d * weeks : (d + 1) * weeks, part] = jnp.where(odd, bottom, top)
        for d in range(2):
            top, bottom = eta[d, :, part], eta[rows - 2 + d, :, part]
            first[at + d : at + d + 1, part] = jnp.where(odd, top, bottom)
            second[at + d : at + d + 1, part] = jnp.where(odd, bottom, top)
        first[at + 2 :, part] = jnp.zeros((6, LANES), F32)
        second[at + 2 :, part] = jnp.zeros((6, LANES), F32)


def hessian_row(r, source, at, image, offset, kappa, weight, mask):
    outer = laplace_row(row_of(image, r + offset - 1), row_of(image, r + offset), row_of(image, r + offset + 1),
                        map_row(kappa, r + 3), mask)
    mid = row_of(source, at)
    heavy = row_of(weight, r + 2)
    return mid, [
        prior_scale * o + (time_coupling * temporal_tile(m, mask) + h * m) for o, m, h in zip(outer, mid, heavy)
    ]


def dot_rows(a, b):
    return fold([x * y for x, y in zip(a, b)])


def inner_kernel(kappa, eta, land, tally, field, start_image, grad_in, weight_in, inv_in, search_in,
                 grad, weight, inv, search, first, image, second, second_image, last, sums):
    weeks = grad.shape[1]
    rows = grad.shape[0]
    mask = masks(weeks)

    def gradient(r, _):
        gradient_row(r, field, tally, eta, land, kappa, start_image, grad, weight, inv, search, mask)

    row_loop(4, rows - 4, gradient, most=8)

    def inner_image(r, _):
        put_row(first, r + 3, laplace_row(
            row_of(search, r + 3), row_of(search, r + 4), row_of(search, r + 5), map_row(kappa, r + 3), mask))

    row_loop(1, rows - 1, inner_image)
    zero = jnp.zeros((8, LANES), F32)

    def apply(r, carry):
        rz, pq, cross = carry
        mid, out = hessian_row(r, search, r + 4, first, 3, kappa, weight, mask)
        other = [a * b for a, b in zip(out, row_of(inv, r + 2))]
        put_row(image, r, out)
        put_row(second, r + 2, other)
        return rz + dot_rows(mid, row_of(grad, r)), pq + dot_rows(mid, out), cross + dot_rows(other, out)

    rz, pq, cross = row_loop(2, rows - 2, apply, (zero, zero, zero), most=7)

    def second_inner(r, _):
        put_row(second_image, r + 1, laplace_row(
            row_of(second, r + 1), row_of(second, r + 2), row_of(second, r + 3), map_row(kappa, r + 3), mask))

    row_loop(3, rows - 3, second_inner)

    def apply_second(r, total):
        mid, out = hessian_row(r, second, r + 2, second_image, 1, kappa, weight, mask)
        put_row(last, r, out)
        return total + dot_rows(mid, out)

    total = row_loop(4, rows - 4, apply_second, zero, most=8)
    for k, value in enumerate((rz, pq, cross, total)):
        sums[8 * k : 8 * k + 8, :] = value


def outer_kernel(old_first, old_second, got_first, got_second, kappa, field, grad, partial,
                 weight_in, inv_in, search_in, first_in, image_in, second_in, second_image_in, last_in,
                 weight, inv, search, first, image, second, second_image, last, sums):
    weeks = grad.shape[1]
    rows = grad.shape[0]
    mask = masks(weeks)
    for d in range(4):
        put_row(search, d, halo_row(d - 4, rows, 4, weeks, got_first, got_second))
        put_row(search, rows + 4 + d, halo_row(rows + d, rows, 4, weeks, got_first, got_second))
    for above in (True, False):
        for d in range(2):
            r = d - 2 if above else rows + d
            eta_row = halo_line(above, 4 * weeks + d, got_first, got_second)
            land_row = halo_line(above, 2 * weeks + 3 + d, old_first, old_second)
            heavy = []
            for j, tile in enumerate(row_of(field, r + 2)):
                curve = jnp.tanh(0.5 * (tile + eta_row[j]))
                heavy.append(land_row[j] * (1.0 - curve * curve))
            put_row(weight, r + 2, heavy)
            put_row(inv, r + 2, [1.0 / (diag_base(k) + h) for k, h in zip(map_row(kappa, r + 3), heavy)])

    for r in (-3, -2, -1, 0, rows - 1, rows, rows + 1, rows + 2):
        put_row(first, r + 3, keep_inside(r, rows, laplace_row(
            row_of(search, r + 3), row_of(search, r + 4), row_of(search, r + 5), map_row(kappa, r + 3), mask)))
    rz, pq, cross, total = (partial[8 * k : 8 * k + 8, :] for k in range(4))
    for r in (-2, -1, 0, 1, rows - 2, rows - 1, rows, rows + 1):
        mid, out = hessian_row(r, search, r + 4, first, 3, kappa, weight, mask)
        other = keep_inside(r, rows, [a * b for a, b in zip(out, row_of(inv, r + 2))])
        put_row(second, r + 2, other)
        if 0 <= r < rows:
            put_row(image, r, out)
            rz, pq, cross = rz + dot_rows(mid, row_of(grad, r)), pq + dot_rows(mid, out), cross + dot_rows(other, out)
    for r in (-1, 0, 1, 2, rows - 3, rows - 2, rows - 1, rows):
        put_row(second_image, r + 1, keep_inside(r, rows, laplace_row(
            row_of(second, r + 1), row_of(second, r + 2), row_of(second, r + 3), map_row(kappa, r + 3), mask)))
    for r in (0, 1, 2, 3, rows - 4, rows - 3, rows - 2, rows - 1):
        mid, out = hessian_row(r, second, r + 2, second_image, 1, kappa, weight, mask)
        put_row(last, r, out)
        total = total + dot_rows(mid, out)
    sums[...] = jnp.zeros_like(sums)
    for k, value in enumerate((rz, pq, cross, total)):
        sums[k : k + 1, :] = jnp.sum(value, axis=0, keepdims=True)


def final_kernel(sums, grad, search, image, second, last, newton_out, residual_out, newton, residual, newton_sem, residual_sem):
    rows, weeks, cols = grad.shape
    rz, pq, cross, total = (jnp.sum(sums[k : k + 1, :], axis=1, keepdims=True) for k in range(4))
    first_step = rz / pq
    rz_next = first_step * first_step * cross - rz
    turn = 1.0 + rz_next / rz
    second_step = rz_next / (turn * (turn * pq - 2.0 * first_step * cross) + first_step * first_step * total)
    along = jnp.broadcast_to(first_step + second_step * turn, (weeks, LANES))
    across = jnp.broadcast_to(second_step * first_step, (weeks, LANES))

    def copies(r):
        return (
            pltpu.make_async_copy(newton.at[r], newton_out.at[:, r, :], newton_sem.at[r]),
            pltpu.make_async_copy(residual.at[r], residual_out.at[:, r, :], residual_sem.at[r]),
        )

    def combine(r, _):
        put_row(newton, r, [along * p - across * y for p, y in zip(row_of(search, r + 4), row_of(second, r + 2))])
        put_row(residual, r, [
            g - along * w + across * h for g, w, h in zip(row_of(grad, r), row_of(image, r), row_of(last, r))])
        for copy in copies(r):
            copy.start()

    row_loop(0, rows, combine, most=8)
    for r in range(rows):
        for copy in copies(r):
            copy.wait()


def call(kernel, outs, ins, scratch=(), aliases=None, limit=2, flops=0, moved=0):
    shapes = tuple(VMEM(shape, F32) if space is VMEM else jax.ShapeDtypeStruct(shape, F32) for shape, space in outs)
    return pl.pallas_call(
        kernel,
        out_shape=shapes,
        in_specs=[pl.BlockSpec(memory_space=space) for _, space in ins],
        out_specs=tuple(pl.BlockSpec(memory_space=space) for _, space in outs),
        scratch_shapes=list(scratch),
        input_output_aliases=aliases or {},
        compiler_params=pltpu.CompilerParams(vmem_limit_bytes=limit * MIB),
        cost_estimate=pl.CostEstimate(flops=flops, bytes_accessed=moved, transcendentals=0),
    )(*[pltpu.with_memory_space_constraint(array, space) if space is pltpu.HBM else array for array, space in ins])


def shards(latent, counts, land_mask, region_ids, kappa_sq, covariates, effects, intercepts):
    weeks, rows, cols = latent.shape
    swap, cross = pair_maps(lax.axis_size(AX))

    def ext(depth):
        return ((rows + 2 * depth, weeks, cols), VMEM)

    def maps(depth):
        return ((rows + 2 * depth, 1, cols), VMEM)

    cells = weeks * rows * cols
    SMEM, ANY, HBM, DMA = pltpu.SMEM, pl.ANY, pltpu.HBM, pltpu.SemaphoreType.DMA
    packed = ((2 * weeks + 8, cols), VMEM)
    near, far, kappa, land = call(
        pack_kernel,
        [packed, packed, maps(3), maps(0)],
        [(latent, HBM), (kappa_sq, HBM), (land_mask, HBM)],
        scratch=[pltpu.VMEM((rows, cols), F32), pltpu.VMEM((rows, cols), jnp.int32), DMA((6,))],
        flops=cells // 16, moved=cells,
    )
    old_near, old_far = lax.ppermute(near, AX, swap), lax.ppermute(far, AX, cross)
    field, image, eta, tally = call(
        front_kernel,
        [ext(2), ext(1), maps(0), ext(0)],
        [(effects.astype(F32), SMEM), (intercepts, SMEM), (latent, VMEM), (covariates, HBM),
         (region_ids, VMEM), (kappa, VMEM), (counts, HBM)],
        scratch=[pltpu.VMEM(covariates.shape, covariates.dtype), pltpu.VMEM(counts.shape, jnp.int32), DMA, DMA],
        flops=40 * cells, moved=12 * cells, limit=8,
    )
    packed = ((4 * weeks + 8, cols), VMEM)
    kappa, field, image, grad, weight, inv, search, near, far = call(
        edge_kernel,
        [maps(3), ext(2), ext(1), ext(0), ext(2), ext(2), ext(4), packed, packed],
        [(old_near, VMEM), (old_far, VMEM), (eta, VMEM), (land, VMEM), (tally, VMEM),
         (kappa, VMEM), (field, VMEM), (image, VMEM)],
        aliases={5 + k: k for k in range(3)},
        flops=10 * cells, moved=cells,
    )
    near, far = lax.ppermute(near, AX, swap), lax.ppermute(far, AX, cross)
    grad, weight, inv, search, first, image, second, second_image, last, partial = call(
        inner_kernel,
        [ext(0), ext(2), ext(2), ext(4), ext(3), ext(0), ext(2), ext(1), ext(0), ((32, LANES), VMEM)],
        [(kappa, VMEM), (eta, VMEM), (land, VMEM), (tally, VMEM), (field, VMEM), (image, VMEM),
         (grad, VMEM), (weight, VMEM), (inv, VMEM), (search, VMEM)],
        aliases={6 + k: k for k in range(4)},
        flops=120 * cells, moved=12 * cells,
    )
    weight, inv, search, first, image, second, second_image, last, sums = call(
        outer_kernel,
        [ext(2), ext(2), ext(4), ext(3), ext(0), ext(2), ext(1), ext(0), ((8, LANES), VMEM)],
        [(old_near, VMEM), (old_far, VMEM), (near, VMEM), (far, VMEM), (kappa, VMEM), (field, VMEM),
         (grad, VMEM), (partial, VMEM), (weight, VMEM), (inv, VMEM), (search, VMEM), (first, VMEM), (image, VMEM),
         (second, VMEM), (second_image, VMEM), (last, VMEM)],
        aliases={8 + k: k for k in range(8)},
        flops=20 * cells, moved=cells,
    )
    return call(
        final_kernel,
        [(latent.shape, ANY), (latent.shape, ANY)],
        [(all_sum(sums), VMEM), (grad, VMEM), (search, VMEM), (image, VMEM), (second, VMEM), (last, VMEM)],
        scratch=[pltpu.VMEM((rows, weeks, cols), F32), pltpu.VMEM((rows, weeks, cols), F32), DMA((rows,)), DMA((rows,))],
        flops=8 * cells, moved=8 * cells, limit=6,
    )


def solution(mesh):
    placed = (
        P(None, "gx", "region"),
        P(None, "gx", "region"),
        P("gx", "region"),
        P("gx", "region"),
        P("gx", "region"),
        P(None, "gx", "region"),
        P("region"),
        P("region"),
    )
    return jax.shard_map(
        shards,
        mesh=mesh,
        in_specs=placed,
        out_specs=(P(None, "gx", "region"), P(None, "gx", "region")),
        check_vma=False,
    )
```

```python
import functools

import jax
import jax.numpy as jnp
from jax import lax
from jax.experimental import pallas as pl
from jax.experimental.pallas import tpu as pltpu
from jax.sharding import PartitionSpec as P

AX = "gx"
LANES = 128
prior_scale = 0.04
time_coupling = 0.5
F32 = jnp.float32
VMEM = pltpu.VMEM
MIB = 1 << 20


def pair_maps(count):
    first = [(i, i ^ 1) for i in range(count) if (i ^ 1) < count]
    second = [(i, ((i + 1) ^ 1) - 1) for i in range(count) if 0 <= ((i + 1) ^ 1) - 1 < count]
    return first, second


def swap_rows(near, far):
    swap, cross = pair_maps(lax.axis_size(AX))
    far = lax.ppermute(far, AX, cross)
    return lax.ppermute(near, AX, swap), far


def all_sum(values, works):
    count = lax.axis_size(AX)
    results = []
    if count & (count - 1):
        return lax.psum(values, AX), [work(values) for work in works]
    step = 1
    while step < count:
        got = lax.ppermute(values, AX, [(i, i ^ step) for i in range(count)])
        if step > 1 and len(results) < len(works):
            piece = works[len(results)](values)
            got, piece = lax.optimization_barrier((got, piece))
            results.append(piece)
        values = values + got
        step *= 2
    while len(results) < len(works):
        results.append(works[len(results)](values))
    return values, results


def row_of(ref, row):
    return [ref[row, :, c : c + LANES] for c in range(0, ref.shape[2], LANES)]


def put_row(ref, row, tiles):
    for j, tile in enumerate(tiles):
        ref[row, :, j * LANES : (j + 1) * LANES] = tile


def map_row(ref, row):
    return [ref[row, :, c : c + LANES] for c in range(0, ref.shape[2], LANES)]


def masks(weeks):
    lane = lax.broadcasted_iota(jnp.int32, (weeks, LANES), 1)
    week = lax.broadcasted_iota(jnp.int32, (weeks, LANES), 0)
    return lane == 0, lane == LANES - 1, week == 0, week == weeks - 1


def laplace_row(up, mid, down, kappa, mask):
    first, last = mask[0], mask[1]
    count = len(mid)
    to_right = [pltpu.roll(t, 1, 1) for t in mid]
    to_left = [pltpu.roll(t, LANES - 1, 1) for t in mid]
    out = []
    for j in range(count):
        west = jnp.where(first, to_right[j - 1] if j > 0 else 0.0, to_right[j])
        east = jnp.where(last, to_left[j + 1] if j + 1 < count else 0.0, to_left[j])
        out.append((kappa[j] + 4.0) * mid[j] - ((up[j] + down[j]) + (west + east)))
    return out


def temporal_tile(tile, mask):
    weeks = tile.shape[0]
    before = jnp.where(mask[2], tile, pltpu.roll(tile, 1, 0))
    after = jnp.where(mask[3], tile, pltpu.roll(tile, weeks - 1, 0))
    return (2.0 * tile - before) - after


def fold(tiles):
    parts = [t[h : h + 8] for t in tiles for h in range(0, t.shape[0], 8)]
    while len(parts) > 1:
        parts = [a + b for a, b in zip(parts[::2], parts[1::2])] + ([parts[-1]] if len(parts) % 2 else [])
    return parts[0]


def diag_base(kappa):
    return prior_scale * ((kappa + 4.0) * (kappa + 4.0) + 4.0) + 2.0 * time_coupling


def is_odd():
    return lax.axis_index(AX) % 2 == 1


def row_loop(low, high, body, carry=None, most=14):
    count = high - low
    step = max(k for k in range(1, most + 1) if count % k == 0)

    def chunk(i, value):
        for k in range(step):
            value = body(low + i * step + k, value)
        return value

    if step == count:
        return chunk(0, carry)
    if carry is None:
        lax.fori_loop(0, count // step, lambda i, z: (chunk(i, None), z)[1], 0)
        return None
    return lax.fori_loop(0, count // step, chunk, carry)


def pack_kernel(latent, kappa_hbm, land_hbm, first, second, kappa_out, land_out, kappa, land, sems):
    weeks, rows, cols = latent.shape
    odd = is_odd()
    map_copies = [pltpu.make_async_copy(kappa_hbm, kappa, sems.at[4]), pltpu.make_async_copy(land_hbm, land, sems.at[5])]
    copies = []
    for k, (out, base) in enumerate(((first, jnp.where(odd, 0, rows - 2)), (second, jnp.where(odd, rows - 2, 0)))):
        for d in range(2):
            copies.append(pltpu.make_async_copy(
                latent.at[:, base + d, :], out.at[d * weeks : (d + 1) * weeks, :], sems.at[2 * k + d]))
    for copy in map_copies + copies:
        copy.start()
    for copy in map_copies:
        copy.wait()
    for r in range(rows):
        kappa_out[r + 3] = kappa[r : r + 1, :]
        land_out[r] = land[r : r + 1, :].astype(F32)
    at = 2 * weeks
    for d in range(3):
        top, bottom = kappa[d : d + 1, :], kappa[rows - 3 + d : rows - 2 + d, :]
        first[at + d : at + d + 1, :] = jnp.where(odd, top, bottom)
        second[at + d : at + d + 1, :] = jnp.where(odd, bottom, top)
    for d in range(2):
        top, bottom = (land[q : q + 1, :].astype(F32) for q in (d, rows - 2 + d))
        first[at + 3 + d : at + 4 + d, :] = jnp.where(odd, top, bottom)
        second[at + 3 + d : at + 4 + d, :] = jnp.where(odd, bottom, top)
    for copy in copies:
        copy.wait()


def rows_first(source, target, shift):
    weeks, rows, cols = source.shape
    for r in range(0, rows, 8):
        for c in range(0, cols, LANES):
            block = source[:, r : r + 8, c : c + LANES].astype(F32)
            target[r + shift : r + shift + 8, :, c : c + LANES] = jnp.swapaxes(block, 0, 1)


def front_kernel(effects, intercepts, latent, covariates, zones, kappa, counts,
                 field, image, eta, tally, covs, raw, cov_sem, sem):
    weeks, rows, cols = latent.shape
    mask = masks(weeks)
    copy = pltpu.make_async_copy(counts, raw, sem)
    cov_copy = pltpu.make_async_copy(covariates, covs, cov_sem)
    cov_copy.start()
    copy.start()
    rows_first(latent, field, 2)

    def inner_image(r, _):
        put_row(image, r + 1, laplace_row(
            row_of(field, r + 1), row_of(field, r + 2), row_of(field, r + 3), map_row(kappa, r + 3), mask))

    row_loop(1, rows - 1, inner_image)
    cov_copy.wait()
    width = 2 * LANES
    for c in range(0, cols, width):
        total = jnp.zeros((rows, width), F32)
        ids = zones[:, c : c + width]
        for z in range(intercepts.shape[0]):
            total = jnp.where(ids == z, intercepts[z], total)
        for k in range(covs.shape[0]):
            total = total + effects[k] * covs[k, :, c : c + width].astype(F32)
        for r in range(rows):
            eta[r, :, c : c + width] = total[r : r + 1]
    copy.wait()
    rows_first(raw, tally, 0)


def gradient_row(r, field, tally, eta, land, kappa, image, grad, weight, inv, search, mask):
    outer = laplace_row(row_of(image, r), row_of(image, r + 1), row_of(image, r + 2), map_row(kappa, r + 3), mask)
    eta_row, land_row, kap, count_row = map_row(eta, r), map_row(land, r), map_row(kappa, r + 3), row_of(tally, r)
    for j, tile in enumerate(row_of(field, r + 2)):
        on = land_row[j]
        curve = jnp.tanh(0.5 * (tile + eta_row[j]))
        heavy = on * (1.0 - curve * curve)
        inverse = 1.0 / (diag_base(kap[j]) + heavy)
        out = on * (count_row[j] - 2.0 - 2.0 * curve) - time_coupling * temporal_tile(tile, mask)
        out = out - prior_scale * outer[j]
        part = slice(j * LANES, (j + 1) * LANES)
        weight[r + 2, :, part] = heavy
        inv[r + 2, :, part] = inverse
        grad[r, :, part] = out
        search[r + 4, :, part] = out * inverse


def keep_inside(r, rows, tiles):
    if 0 <= r < rows:
        return tiles
    place, count = lax.axis_index(AX), lax.axis_size(AX)
    keep = jnp.where(place > 0 if r < 0 else place < count - 1, 1.0, 0.0)
    return [keep * t for t in tiles]


def halo_row(r, rows, depth, height, first, second):
    odd = is_odd()
    at = (r + depth if r < 0 else r - rows) * height
    a, b = (first, second) if r < 0 else (second, first)
    return [jnp.where(odd, a[at : at + height, c : c + LANES], b[at : at + height, c : c + LANES])
            for c in range(0, first.shape[1], LANES)]


def halo_line(above, line, first, second):
    odd = is_odd()
    a, b = (first, second) if above else (second, first)
    return [jnp.where(odd, a[line : line + 1, c : c + LANES], b[line : line + 1, c : c + LANES])
            for c in range(0, first.shape[1], LANES)]


def edge_kernel(got_first, got_second, eta, land, tally, kappa_in, field_in, image_in,
                kappa, field, image, grad, weight, inv, search, first, second):
    weeks = field.shape[1]
    rows, _, cols = eta.shape
    mask = masks(weeks)
    odd = is_odd()
    for d in range(2):
        put_row(field, d, halo_row(d - 2, rows, 2, weeks, got_first, got_second))
        put_row(field, rows + 2 + d, halo_row(rows + d, rows, 2, weeks, got_first, got_second))
    for d in range(3):
        put_row(kappa, d, halo_line(True, 2 * weeks + d, got_first, got_second))
        put_row(kappa, rows + 3 + d, halo_line(False, 2 * weeks + d, got_first, got_second))
    for r in (-1, 0, rows - 1, rows):
        put_row(image, r + 1, keep_inside(r, rows, laplace_row(
            row_of(field, r + 1), row_of(field, r + 2), row_of(field, r + 3), map_row(kappa, r + 3), mask)))
    for r in (0, 1, 2, 3, rows - 4, rows - 3, rows - 2, rows - 1):
        gradient_row(r, field, tally, eta, land, kappa, image, grad, weight, inv, search, mask)
    at = 4 * weeks
    for c in range(0, cols, LANES):
        part = slice(c, c + LANES)
        for d in range(4):
            top, bottom = search[4 + d, :, part], search[rows + d, :, part]
            first[d * weeks : (d + 1) * weeks, part] = jnp.where(odd, top, bottom)
            second[d * weeks : (d + 1) * weeks, part] = jnp.where(odd, bottom, top)
        for d in range(2):
            top, bottom = eta[d, :, part], eta[rows - 2 + d, :, part]
            first[at + d : at + d + 1, part] = jnp.where(odd, top, bottom)
            second[at + d : at + d + 1, part] = jnp.where(odd, bottom, top)


def mass_row(r, source, at, weight, mask):
    mid = row_of(source, at)
    return mid, [time_coupling * temporal_tile(m, mask) + h * m for m, h in zip(mid, row_of(weight, r + 2))]


def hessian_row(r, source, at, image, offset, kappa, weight, mask):
    outer = laplace_row(row_of(image, r + offset - 1), row_of(image, r + offset), row_of(image, r + offset + 1),
                        map_row(kappa, r + 3), mask)
    mid, mass = mass_row(r, source, at, weight, mask)
    return mid, [prior_scale * o + m for o, m in zip(outer, mass)]


def dot_rows(a, b):
    return fold([x * y for x, y in zip(a, b)])


def inner_kernel(kappa, eta, land, tally, field, start_image, grad_in, weight_in, inv_in, search_in,
                 grad, weight, inv, search, first, image, second, second_image, sums):
    weeks = grad.shape[1]
    rows = grad.shape[0]
    mask = masks(weeks)

    def gradient(r, _):
        gradient_row(r, field, tally, eta, land, kappa, start_image, grad, weight, inv, search, mask)

    row_loop(4, rows - 4, gradient, most=8)

    def inner_image(r, _):
        put_row(first, r + 3, laplace_row(
            row_of(search, r + 3), row_of(search, r + 4), row_of(search, r + 5), map_row(kappa, r + 3), mask))

    row_loop(1, rows - 1, inner_image)
    zero = jnp.zeros((8, LANES), F32)

    def apply(r, carry):
        rz, pq, cross, total = carry
        mid, out = hessian_row(r, search, r + 4, first, 3, kappa, weight, mask)
        other = [a * b for a, b in zip(out, row_of(inv, r + 2))]
        mass = [time_coupling * temporal_tile(y, mask) + h * y for y, h in zip(other, row_of(weight, r + 2))]
        put_row(image, r, out)
        put_row(second, r + 2, other)
        return (rz + dot_rows(mid, row_of(grad, r)), pq + dot_rows(mid, out), cross + dot_rows(other, out),
                total + dot_rows(other, mass))

    rz, pq, cross, total = row_loop(2, rows - 2, apply, (zero, zero, zero, zero), most=7)

    def second_inner(r, square):
        out = laplace_row(
            row_of(second, r + 1), row_of(second, r + 2), row_of(second, r + 3), map_row(kappa, r + 3), mask)
        put_row(second_image, r + 1, out)
        return square + dot_rows(out, out)

    square = row_loop(3, rows - 3, second_inner, zero)
    for k, value in enumerate((rz, pq, cross, total + prior_scale * square)):
        sums[8 * k : 8 * k + 8, :] = value


def outer_kernel(old_first, old_second, got_first, got_second, kappa, field, grad, partial,
                 weight_in, inv_in, search_in, first_in, image_in, second_in, second_image_in,
                 weight, inv, search, first, image, second, second_image, sums):
    weeks = grad.shape[1]
    rows = grad.shape[0]
    mask = masks(weeks)
    for d in range(4):
        put_row(search, d, halo_row(d - 4, rows, 4, weeks, got_first, got_second))
        put_row(search, rows + 4 + d, halo_row(rows + d, rows, 4, weeks, got_first, got_second))
    for above in (True, False):
        for d in range(2):
            r = d - 2 if above else rows + d
            eta_row = halo_line(above, 4 * weeks + d, got_first, got_second)
            land_row = halo_line(above, 2 * weeks + 3 + d, old_first, old_second)
            heavy = []
            for j, tile in enumerate(row_of(field, r + 2)):
                curve = jnp.tanh(0.5 * (tile + eta_row[j]))
                heavy.append(land_row[j] * (1.0 - curve * curve))
            put_row(weight, r + 2, heavy)
            put_row(inv, r + 2, [1.0 / (diag_base(k) + h) for k, h in zip(map_row(kappa, r + 3), heavy)])

    for r in (-3, -2, -1, 0, rows - 1, rows, rows + 1, rows + 2):
        put_row(first, r + 3, keep_inside(r, rows, laplace_row(
            row_of(search, r + 3), row_of(search, r + 4), row_of(search, r + 5), map_row(kappa, r + 3), mask)))
    rz, pq, cross, total = (partial[8 * k : 8 * k + 8, :] for k in range(4))
    for r in (-2, -1, 0, 1, rows - 2, rows - 1, rows, rows + 1):
        mid, out = hessian_row(r, search, r + 4, first, 3, kappa, weight, mask)
        other = keep_inside(r, rows, [a * b for a, b in zip(out, row_of(inv, r + 2))])
        put_row(second, r + 2, other)
        if 0 <= r < rows:
            put_row(image, r, out)
            mass = [time_coupling * temporal_tile(y, mask) + h * y for y, h in zip(other, row_of(weight, r + 2))]
            rz, pq, cross = rz + dot_rows(mid, row_of(grad, r)), pq + dot_rows(mid, out), cross + dot_rows(other, out)
            total = total + dot_rows(other, mass)
    for r in (-1, 0, 1, 2, rows - 3, rows - 2, rows - 1, rows):
        out = keep_inside(r, rows, laplace_row(
            row_of(second, r + 1), row_of(second, r + 2), row_of(second, r + 3), map_row(kappa, r + 3), mask))
        put_row(second_image, r + 1, out)
        if 0 <= r < rows:
            total = total + prior_scale * dot_rows(out, out)
    sums[...] = jnp.zeros_like(sums)
    for k, value in enumerate((rz, pq, cross, total)):
        sums[k : k + 1, :] = jnp.sum(value, axis=0, keepdims=True)


def last_kernel(low, gate, kappa, weight, second, second_image, last):
    mask = masks(last.shape[1])

    def apply(r, _):
        put_row(last, r, hessian_row(r + low, second, r + low + 2, second_image, 1, kappa, weight, mask)[1])

    row_loop(0, last.shape[0], apply, most=8)


def final_kernel(sums, grad, search, image, second, upper, lower, newton_out, residual_out, newton, residual, newton_sem, residual_sem):
    rows, weeks, cols = grad.shape
    rz, pq, cross, total = (jnp.sum(sums[k : k + 1, :], axis=1, keepdims=True) for k in range(4))
    first_step = rz / pq
    rz_next = first_step * first_step * cross - rz
    turn = 1.0 + rz_next / rz
    second_step = rz_next / (turn * (turn * pq - 2.0 * first_step * cross) + first_step * first_step * total)
    along = jnp.broadcast_to(first_step + second_step * turn, (weeks, LANES))
    across = jnp.broadcast_to(second_step * first_step, (weeks, LANES))

    def copies(r):
        return (
            pltpu.make_async_copy(newton.at[r], newton_out.at[:, r, :], newton_sem.at[r]),
            pltpu.make_async_copy(residual.at[r], residual_out.at[:, r, :], residual_sem.at[r]),
        )

    half = upper.shape[0]

    def combine(r, last, at):
        put_row(newton, r, [along * p - across * y for p, y in zip(row_of(search, r + 4), row_of(second, r + 2))])
        put_row(residual, r, [
            g - along * w + across * h for g, w, h in zip(row_of(grad, r), row_of(image, r), row_of(last, r - at))])
        for copy in copies(r):
            copy.start()

    row_loop(0, half, lambda r, _: combine(r, upper, 0), most=8)
    row_loop(half, rows, lambda r, _: combine(r, lower, half), most=8)
    for r in range(rows):
        for copy in copies(r):
            copy.wait()


def call(kernel, outs, ins, scratch=(), aliases=None, limit=2, flops=0, moved=0):
    shapes = tuple(VMEM(shape, F32) if space is VMEM else jax.ShapeDtypeStruct(shape, F32) for shape, space in outs)
    return pl.pallas_call(
        kernel,
        out_shape=shapes,
        in_specs=[pl.BlockSpec(memory_space=space) for _, space in ins],
        out_specs=tuple(pl.BlockSpec(memory_space=space) for _, space in outs),
        scratch_shapes=list(scratch),
        input_output_aliases=aliases or {},
        compiler_params=pltpu.CompilerParams(vmem_limit_bytes=limit * MIB),
        cost_estimate=pl.CostEstimate(flops=flops, bytes_accessed=moved, transcendentals=0),
    )(*[pltpu.with_memory_space_constraint(array, space) if space is pltpu.HBM else array for array, space in ins])


def shards(latent, counts, land_mask, region_ids, kappa_sq, covariates, effects, intercepts):
    weeks, rows, cols = latent.shape

    def ext(depth):
        return ((rows + 2 * depth, weeks, cols), VMEM)

    def maps(depth):
        return ((rows + 2 * depth, 1, cols), VMEM)

    cells = weeks * rows * cols
    SMEM, ANY, HBM, DMA = pltpu.SMEM, pl.ANY, pltpu.HBM, pltpu.SemaphoreType.DMA
    packed = ((2 * weeks + 5, cols), VMEM)
    near, far, kappa, land = call(
        pack_kernel,
        [packed, packed, maps(3), maps(0)],
        [(latent, HBM), (kappa_sq, HBM), (land_mask, HBM)],
        scratch=[pltpu.VMEM((rows, cols), F32), pltpu.VMEM((rows, cols), jnp.int32), DMA((6,))],
        flops=cells // 16, moved=cells,
    )
    old_near, old_far = swap_rows(near, far)
    field, image, eta, tally = call(
        front_kernel,
        [ext(2), ext(1), maps(0), ext(0)],
        [(effects.astype(F32), SMEM), (intercepts, SMEM), (latent, VMEM), (covariates, HBM),
         (region_ids, VMEM), (kappa, VMEM), (counts, HBM)],
        scratch=[pltpu.VMEM(covariates.shape, covariates.dtype), pltpu.VMEM(counts.shape, jnp.int32), DMA, DMA],
        flops=40 * cells, moved=12 * cells, limit=8,
    )
    packed = ((4 * weeks + 2, cols), VMEM)
    kappa, field, image, grad, weight, inv, search, near, far = call(
        edge_kernel,
        [maps(3), ext(2), ext(1), ext(0), ext(2), ext(2), ext(4), packed, packed],
        [(old_near, VMEM), (old_far, VMEM), (eta, VMEM), (land, VMEM), (tally, VMEM),
         (kappa, VMEM), (field, VMEM), (image, VMEM)],
        aliases={5 + k: k for k in range(3)},
        flops=10 * cells, moved=cells,
    )
    near, far = swap_rows(near, far)
    grad, weight, inv, search, first, image, second, second_image, partial = call(
        inner_kernel,
        [ext(0), ext(2), ext(2), ext(4), ext(3), ext(0), ext(2), ext(1), ((32, LANES), VMEM)],
        [(kappa, VMEM), (eta, VMEM), (land, VMEM), (tally, VMEM), (field, VMEM), (image, VMEM),
         (grad, VMEM), (weight, VMEM), (inv, VMEM), (search, VMEM)],
        aliases={6 + k: k for k in range(4)},
        flops=120 * cells, moved=12 * cells,
    )
    weight, inv, search, first, image, second, second_image, sums = call(
        outer_kernel,
        [ext(2), ext(2), ext(4), ext(3), ext(0), ext(2), ext(1), ((8, LANES), VMEM)],
        [(old_near, VMEM), (old_far, VMEM), (near, VMEM), (far, VMEM), (kappa, VMEM), (field, VMEM),
         (grad, VMEM), (partial, VMEM), (weight, VMEM), (inv, VMEM), (search, VMEM), (first, VMEM), (image, VMEM),
         (second, VMEM), (second_image, VMEM)],
        aliases={8 + k: k for k in range(7)},
        flops=20 * cells, moved=cells,
    )
    half = rows // 2

    def last_rows(low, count):
        return lambda gate: call(
            functools.partial(last_kernel, low),
            [((count, weeks, cols), VMEM)],
            [(gate, VMEM), (kappa, VMEM), (weight, VMEM), (second, VMEM), (second_image, VMEM)],
            flops=4 * cells, moved=cells,
        )[0]

    sums, (upper, lower) = all_sum(sums, [last_rows(0, half), last_rows(half, rows - half)])
    return call(
        final_kernel,
        [(latent.shape, ANY), (latent.shape, ANY)],
        [(sums, VMEM), (grad, VMEM), (search, VMEM), (image, VMEM), (second, VMEM), (upper, VMEM), (lower, VMEM)],
        scratch=[pltpu.VMEM((rows, weeks, cols), F32), pltpu.VMEM((rows, weeks, cols), F32), DMA((rows,)), DMA((rows,))],
        flops=8 * cells, moved=8 * cells, limit=6,
    )


def solution(mesh):
    placed = (
        P(None, "gx", "region"),
        P(None, "gx", "region"),
        P("gx", "region"),
        P("gx", "region"),
        P("gx", "region"),
        P(None, "gx", "region"),
        P("region"),
        P("region"),
    )
    return jax.shard_map(
        shards,
        mesh=mesh,
        in_specs=placed,
        out_specs=(P(None, "gx", "region"), P(None, "gx", "region")),
        check_vma=False,
    )
```

```python
import functools

import jax
import jax.numpy as jnp
from jax import lax
from jax.experimental import pallas as pl
from jax.experimental.pallas import tpu as pltpu
from jax.sharding import PartitionSpec as P

AX = "gx"
LANES = 128
prior_scale = 0.04
time_coupling = 0.5
F32 = jnp.float32
VMEM = pltpu.VMEM
MIB = 1 << 20


def pair_maps(count):
    first = [(i, i ^ 1) for i in range(count) if (i ^ 1) < count]
    second = [(i, ((i + 1) ^ 1) - 1) for i in range(count) if 0 <= ((i + 1) ^ 1) - 1 < count]
    return first, second


def swap_rows(near, far):
    swap, cross = pair_maps(lax.axis_size(AX))
    far = lax.ppermute(far, AX, cross)
    return lax.ppermute(near, AX, swap), far


def all_sum(values, works):
    count = lax.axis_size(AX)
    results = []
    if count & (count - 1):
        return lax.psum(values, AX), [work(values) for work in works]
    step = 1
    while step < count:
        got = lax.ppermute(values, AX, [(i, i ^ step) for i in range(count)])
        if step > 1 and len(results) < len(works):
            piece = works[len(results)](values)
            got, piece = lax.optimization_barrier((got, piece))
            results.append(piece)
        values = values + got
        step *= 2
    while len(results) < len(works):
        results.append(works[len(results)](values))
    return values, results


def row_of(ref, row):
    return [ref[row, :, c : c + LANES] for c in range(0, ref.shape[2], LANES)]


def put_row(ref, row, tiles):
    for j, tile in enumerate(tiles):
        ref[row, :, j * LANES : (j + 1) * LANES] = tile


def map_row(ref, row):
    return [ref[row, :, c : c + LANES] for c in range(0, ref.shape[2], LANES)]


def masks(weeks):
    lane = lax.broadcasted_iota(jnp.int32, (weeks, LANES), 1)
    week = lax.broadcasted_iota(jnp.int32, (weeks, LANES), 0)
    return lane == 0, lane == LANES - 1, week == 0, week == weeks - 1


def laplace_row(up, mid, down, kappa, mask):
    first, last = mask[0], mask[1]
    count = len(mid)
    to_right = [pltpu.roll(t, 1, 1) for t in mid]
    to_left = [pltpu.roll(t, LANES - 1, 1) for t in mid]
    out = []
    for j in range(count):
        west = jnp.where(first, to_right[j - 1] if j > 0 else 0.0, to_right[j])
        east = jnp.where(last, to_left[j + 1] if j + 1 < count else 0.0, to_left[j])
        out.append((kappa[j] + 4.0) * mid[j] - ((up[j] + down[j]) + (west + east)))
    return out


def temporal_tile(tile, mask):
    weeks = tile.shape[0]
    before = jnp.where(mask[2], tile, pltpu.roll(tile, 1, 0))
    after = jnp.where(mask[3], tile, pltpu.roll(tile, weeks - 1, 0))
    return (2.0 * tile - before) - after


def fold(tiles):
    parts = [t[h : h + 8] for t in tiles for h in range(0, t.shape[0], 8)]
    while len(parts) > 1:
        parts = [a + b for a, b in zip(parts[::2], parts[1::2])] + ([parts[-1]] if len(parts) % 2 else [])
    return parts[0]


def diag_base(kappa):
    return prior_scale * ((kappa + 4.0) * (kappa + 4.0) + 4.0) + 2.0 * time_coupling


def is_odd():
    return lax.axis_index(AX) % 2 == 1


def row_loop(low, high, body, carry=None, most=14):
    count = high - low
    step = max(k for k in range(1, most + 1) if count % k == 0)

    def chunk(i, value):
        for k in range(step):
            value = body(low + i * step + k, value)
        return value

    if step == count:
        return chunk(0, carry)
    if carry is None:
        lax.fori_loop(0, count // step, lambda i, z: (chunk(i, None), z)[1], 0)
        return None
    return lax.fori_loop(0, count // step, chunk, carry)


def pack_kernel(latent, kappa_hbm, land_hbm, first, second, kappa, land, sems):
    weeks, rows, cols = latent.shape
    odd = is_odd()
    copies = []
    for k, (out, base) in enumerate(((first, jnp.where(odd, 0, rows - 2)), (second, jnp.where(odd, rows - 2, 0)))):
        for d in range(2):
            copies.append(pltpu.make_async_copy(
                latent.at[:, base + d, :], out.at[d * weeks : (d + 1) * weeks, :], sems.at[2 * k + d]))
    map_copies = []
    for k, (source, target) in enumerate(((kappa_hbm, kappa), (land_hbm, land))):
        for d, at in enumerate((0, rows - 8)):
            map_copies.append(pltpu.make_async_copy(
                source.at[at : at + 8, :], target.at[8 * d : 8 * d + 8, :], sems.at[4 + 2 * k + d]))
    for copy in copies + map_copies:
        copy.start()
    for copy in map_copies:
        copy.wait()
    at = 2 * weeks
    for d in range(3):
        top, bottom = kappa[d : d + 1, :], kappa[13 + d : 14 + d, :]
        first[at + d : at + d + 1, :] = jnp.where(odd, top, bottom)
        second[at + d : at + d + 1, :] = jnp.where(odd, bottom, top)
    for d in range(2):
        top, bottom = (land[q : q + 1, :].astype(F32) for q in (d, 14 + d))
        first[at + 3 + d : at + 4 + d, :] = jnp.where(odd, top, bottom)
        second[at + 3 + d : at + 4 + d, :] = jnp.where(odd, bottom, top)
    for copy in copies:
        copy.wait()


def rows_first(source, target, shift):
    weeks, rows, cols = source.shape
    for r in range(0, rows, 8):
        for c in range(0, cols, LANES):
            block = source[:, r : r + 8, c : c + LANES].astype(F32)
            target[r + shift : r + shift + 8, :, c : c + LANES] = jnp.swapaxes(block, 0, 1)


def front_kernel(effects, intercepts, latent, covariates, zones, kappa_flat, land_flat, counts,
                 field, image, eta, tally, kappa, land, grad, weight, inv, search, covs, raw, cov_sem, sem):
    weeks, rows, cols = latent.shape
    mask = masks(weeks)
    copy = pltpu.make_async_copy(counts, raw, sem)
    cov_copy = pltpu.make_async_copy(covariates, covs, cov_sem)
    cov_copy.start()
    copy.start()
    rows_first(latent, field, 2)
    for r in range(rows):
        kappa[r + 3] = kappa_flat[r : r + 1, :]
        land[r] = land_flat[r : r + 1, :].astype(F32)

    def inner_image(r, _):
        put_row(image, r + 1, laplace_row(
            row_of(field, r + 1), row_of(field, r + 2), row_of(field, r + 3), map_row(kappa, r + 3), mask))

    row_loop(1, rows - 1, inner_image)
    cov_copy.wait()
    width = 2 * LANES
    for c in range(0, cols, width):
        total = jnp.zeros((rows, width), F32)
        ids = zones[:, c : c + width]
        for z in range(intercepts.shape[0]):
            total = jnp.where(ids == z, intercepts[z], total)
        for k in range(covs.shape[0]):
            total = total + effects[k] * covs[k, :, c : c + width].astype(F32)
        for r in range(rows):
            eta[r, :, c : c + width] = total[r : r + 1]
    copy.wait()
    rows_first(raw, tally, 0)
    for r in (0, 1, rows - 2, rows - 1):
        gradient_row(r, field, tally, eta, land, kappa, None, grad, weight, inv, search, mask)
    for r in (2, 3, rows - 4, rows - 3):
        gradient_row(r, field, tally, eta, land, kappa, image, grad, weight, inv, search, mask)


def gradient_row(r, field, tally, eta, land, kappa, image, grad, weight, inv, search, mask):
    eta_row, land_row, kap, count_row = map_row(eta, r), map_row(land, r), map_row(kappa, r + 3), row_of(tally, r)
    if image is not None:
        outer = laplace_row(row_of(image, r), row_of(image, r + 1), row_of(image, r + 2), kap, mask)
    for j, tile in enumerate(row_of(field, r + 2)):
        on = land_row[j]
        curve = jnp.tanh(0.5 * (tile + eta_row[j]))
        heavy = on * (1.0 - curve * curve)
        inverse = 1.0 / (diag_base(kap[j]) + heavy)
        out = on * (count_row[j] - 2.0 - 2.0 * curve) - time_coupling * temporal_tile(tile, mask)
        part = slice(j * LANES, (j + 1) * LANES)
        weight[r + 2, :, part] = heavy
        inv[r + 2, :, part] = inverse
        if image is not None:
            out = out - prior_scale * outer[j]
            search[r + 4, :, part] = out * inverse
        grad[r, :, part] = out


def keep_inside(r, rows, tiles):
    if 0 <= r < rows:
        return tiles
    place, count = lax.axis_index(AX), lax.axis_size(AX)
    keep = jnp.where(place > 0 if r < 0 else place < count - 1, 1.0, 0.0)
    return [keep * t for t in tiles]


def halo_row(r, rows, depth, height, first, second):
    odd = is_odd()
    at = (r + depth if r < 0 else r - rows) * height
    a, b = (first, second) if r < 0 else (second, first)
    return [jnp.where(odd, a[at : at + height, c : c + LANES], b[at : at + height, c : c + LANES])
            for c in range(0, first.shape[1], LANES)]


def halo_line(above, line, first, second):
    odd = is_odd()
    a, b = (first, second) if above else (second, first)
    return [jnp.where(odd, a[line : line + 1, c : c + LANES], b[line : line + 1, c : c + LANES])
            for c in range(0, first.shape[1], LANES)]


def edge_kernel(got_second, got_first, eta, inv, kappa_in, field_in, image_in, grad_in, search_in,
                kappa, field, image, grad, search, first, second):
    weeks = field.shape[1]
    rows, _, cols = eta.shape
    mask = masks(weeks)
    odd = is_odd()
    for d in range(2):
        put_row(field, d, halo_row(d - 2, rows, 2, weeks, got_first, got_second))
        put_row(field, rows + 2 + d, halo_row(rows + d, rows, 2, weeks, got_first, got_second))
    for d in range(3):
        put_row(kappa, d, halo_line(True, 2 * weeks + d, got_first, got_second))
        put_row(kappa, rows + 3 + d, halo_line(False, 2 * weeks + d, got_first, got_second))
    for r in (-1, 0, rows - 1, rows):
        put_row(image, r + 1, keep_inside(r, rows, laplace_row(
            row_of(field, r + 1), row_of(field, r + 2), row_of(field, r + 3), map_row(kappa, r + 3), mask)))
    for r in (0, 1, rows - 2, rows - 1):
        outer = laplace_row(row_of(image, r), row_of(image, r + 1), row_of(image, r + 2), map_row(kappa, r + 3), mask)
        out = [a - prior_scale * b for a, b in zip(row_of(grad, r), outer)]
        put_row(grad, r, out)
        put_row(search, r + 4, [a * b for a, b in zip(out, row_of(inv, r + 2))])
    at = 4 * weeks
    for c in range(0, cols, LANES):
        part = slice(c, c + LANES)
        for d in range(4):
            top, bottom = search[4 + d, :, part], search[rows + d, :, part]
            first[d * weeks : (d + 1) * weeks, part] = jnp.where(odd, top, bottom)
            second[d * weeks : (d + 1) * weeks, part] = jnp.where(odd, bottom, top)
        for d in range(2):
            top, bottom = eta[d, :, part], eta[rows - 2 + d, :, part]
            first[at + d : at + d + 1, part] = jnp.where(odd, top, bottom)
            second[at + d : at + d + 1, part] = jnp.where(odd, bottom, top)


def mass_row(r, source, at, weight, mask):
    mid = row_of(source, at)
    return mid, [time_coupling * temporal_tile(m, mask) + h * m for m, h in zip(mid, row_of(weight, r + 2))]


def hessian_row(r, source, at, image, offset, kappa, weight, mask):
    outer = laplace_row(row_of(image, r + offset - 1), row_of(image, r + offset), row_of(image, r + offset + 1),
                        map_row(kappa, r + 3), mask)
    mid, mass = mass_row(r, source, at, weight, mask)
    return mid, [prior_scale * o + m for o, m in zip(outer, mass)]


def dot_rows(a, b):
    return fold([x * y for x, y in zip(a, b)])


def inner_kernel(kappa, eta, land, tally, field, start_image, grad_in, weight_in, inv_in, search_in,
                 grad, weight, inv, search, first, image, second, second_image, sums):
    weeks = grad.shape[1]
    rows = grad.shape[0]
    mask = masks(weeks)

    def gradient(r, _):
        gradient_row(r, field, tally, eta, land, kappa, start_image, grad, weight, inv, search, mask)

    row_loop(4, rows - 4, gradient, most=8)

    def inner_image(r, _):
        put_row(first, r + 3, laplace_row(
            row_of(search, r + 3), row_of(search, r + 4), row_of(search, r + 5), map_row(kappa, r + 3), mask))

    row_loop(1, rows - 1, inner_image)
    zero = jnp.zeros((8, LANES), F32)

    def apply(r, carry):
        rz, pq, cross, total = carry
        mid, out = hessian_row(r, search, r + 4, first, 3, kappa, weight, mask)
        other = [a * b for a, b in zip(out, row_of(inv, r + 2))]
        mass = [time_coupling * temporal_tile(y, mask) + h * y for y, h in zip(other, row_of(weight, r + 2))]
        put_row(image, r, out)
        put_row(second, r + 2, other)
        return (rz + dot_rows(mid, row_of(grad, r)), pq + dot_rows(mid, out), cross + dot_rows(other, out),
                total + dot_rows(other, mass))

    rz, pq, cross, total = row_loop(2, rows - 2, apply, (zero, zero, zero, zero), most=7)

    def second_inner(r, square):
        out = laplace_row(
            row_of(second, r + 1), row_of(second, r + 2), row_of(second, r + 3), map_row(kappa, r + 3), mask)
        put_row(second_image, r + 1, out)
        return square + dot_rows(out, out)

    square = row_loop(3, rows - 3, second_inner, zero)
    for k, value in enumerate((rz, pq, cross, total + prior_scale * square)):
        sums[8 * k : 8 * k + 8, :] = value


def outer_kernel(old_second, old_first, got_second, got_first, kappa, field, grad, partial,
                 weight_in, inv_in, search_in, first_in, image_in, second_in, second_image_in,
                 weight, inv, search, first, image, second, second_image, sums):
    weeks = grad.shape[1]
    rows = grad.shape[0]
    mask = masks(weeks)
    for d in range(4):
        put_row(search, d, halo_row(d - 4, rows, 4, weeks, got_first, got_second))
        put_row(search, rows + 4 + d, halo_row(rows + d, rows, 4, weeks, got_first, got_second))
    for above in (True, False):
        for d in range(2):
            r = d - 2 if above else rows + d
            eta_row = halo_line(above, 4 * weeks + d, got_first, got_second)
            land_row = halo_line(above, 2 * weeks + 3 + d, old_first, old_second)
            heavy = []
            for j, tile in enumerate(row_of(field, r + 2)):
                curve = jnp.tanh(0.5 * (tile + eta_row[j]))
                heavy.append(land_row[j] * (1.0 - curve * curve))
            put_row(weight, r + 2, heavy)
            put_row(inv, r + 2, [1.0 / (diag_base(k) + h) for k, h in zip(map_row(kappa, r + 3), heavy)])

    for r in (-3, -2, -1, 0, rows - 1, rows, rows + 1, rows + 2):
        put_row(first, r + 3, keep_inside(r, rows, laplace_row(
            row_of(search, r + 3), row_of(search, r + 4), row_of(search, r + 5), map_row(kappa, r + 3), mask)))
    rz, pq, cross, total = (partial[8 * k : 8 * k + 8, :] for k in range(4))
    for r in (-2, -1, 0, 1, rows - 2, rows - 1, rows, rows + 1):
        mid, out = hessian_row(r, search, r + 4, first, 3, kappa, weight, mask)
        other = keep_inside(r, rows, [a * b for a, b in zip(out, row_of(inv, r + 2))])
        put_row(second, r + 2, other)
        if 0 <= r < rows:
            put_row(image, r, out)
            mass = [time_coupling * temporal_tile(y, mask) + h * y for y, h in zip(other, row_of(weight, r + 2))]
            rz, pq, cross = rz + dot_rows(mid, row_of(grad, r)), pq + dot_rows(mid, out), cross + dot_rows(other, out)
            total = total + dot_rows(other, mass)
    for r in (-1, 0, 1, 2, rows - 3, rows - 2, rows - 1, rows):
        out = keep_inside(r, rows, laplace_row(
            row_of(second, r + 1), row_of(second, r + 2), row_of(second, r + 3), map_row(kappa, r + 3), mask))
        put_row(second_image, r + 1, out)
        if 0 <= r < rows:
            total = total + prior_scale * dot_rows(out, out)
    sums[...] = jnp.zeros_like(sums)
    for k, value in enumerate((rz, pq, cross, total)):
        sums[k : k + 1, :] = jnp.sum(value, axis=0, keepdims=True)


def last_kernel(low, gate, kappa, weight, second, second_image, last):
    mask = masks(last.shape[1])

    def apply(r, _):
        put_row(last, r, hessian_row(r + low, second, r + low + 2, second_image, 1, kappa, weight, mask)[1])

    row_loop(0, last.shape[0], apply, most=8)


def final_kernel(sums, grad, search, image, second, upper, lower, newton_out, residual_out, newton, residual, newton_sem, residual_sem):
    rows, weeks, cols = grad.shape
    rz, pq, cross, total = (jnp.sum(sums[k : k + 1, :], axis=1, keepdims=True) for k in range(4))
    first_step = rz / pq
    rz_next = first_step * first_step * cross - rz
    turn = 1.0 + rz_next / rz
    second_step = rz_next / (turn * (turn * pq - 2.0 * first_step * cross) + first_step * first_step * total)
    along = jnp.broadcast_to(first_step + second_step * turn, (weeks, LANES))
    across = jnp.broadcast_to(second_step * first_step, (weeks, LANES))

    def copies(r):
        return (
            pltpu.make_async_copy(newton.at[r], newton_out.at[:, r, :], newton_sem.at[r]),
            pltpu.make_async_copy(residual.at[r], residual_out.at[:, r, :], residual_sem.at[r]),
        )

    half = upper.shape[0]

    def combine(r, last, at):
        put_row(newton, r, [along * p - across * y for p, y in zip(row_of(search, r + 4), row_of(second, r + 2))])
        put_row(residual, r, [
            g - along * w + across * h for g, w, h in zip(row_of(grad, r), row_of(image, r), row_of(last, r - at))])
        for copy in copies(r):
            copy.start()

    row_loop(0, half, lambda r, _: combine(r, upper, 0), most=8)
    row_loop(half, rows, lambda r, _: combine(r, lower, half), most=8)
    for r in range(rows):
        for copy in copies(r):
            copy.wait()


def call(kernel, outs, ins, scratch=(), aliases=None, limit=2, flops=0, moved=0):
    shapes = tuple(VMEM(shape, F32) if space is VMEM else jax.ShapeDtypeStruct(shape, F32) for shape, space in outs)
    return pl.pallas_call(
        kernel,
        out_shape=shapes,
        in_specs=[pl.BlockSpec(memory_space=space) for _, space in ins],
        out_specs=tuple(pl.BlockSpec(memory_space=space) for _, space in outs),
        scratch_shapes=list(scratch),
        input_output_aliases=aliases or {},
        compiler_params=pltpu.CompilerParams(vmem_limit_bytes=limit * MIB),
        cost_estimate=pl.CostEstimate(flops=flops, bytes_accessed=moved, transcendentals=0),
    )(*[pltpu.with_memory_space_constraint(array, space) if space is pltpu.HBM else array for array, space in ins])


def shards(latent, counts, land_mask, region_ids, kappa_sq, covariates, effects, intercepts):
    weeks, rows, cols = latent.shape

    def ext(depth):
        return ((rows + 2 * depth, weeks, cols), VMEM)

    def maps(depth):
        return ((rows + 2 * depth, 1, cols), VMEM)

    cells = weeks * rows * cols
    SMEM, ANY, HBM, DMA = pltpu.SMEM, pl.ANY, pltpu.HBM, pltpu.SemaphoreType.DMA
    packed = ((2 * weeks + 5, cols), VMEM)
    near, far = call(
        pack_kernel,
        [packed, packed],
        [(latent, HBM), (kappa_sq, HBM), (land_mask, HBM)],
        scratch=[pltpu.VMEM((16, cols), F32), pltpu.VMEM((16, cols), jnp.int32), DMA((8,))],
        flops=cells // 16, moved=cells,
    )
    old_near, old_far = swap_rows(near, far)
    field, image, eta, tally, kappa, land, grad, weight, inv, search = call(
        front_kernel,
        [ext(2), ext(1), maps(0), ext(0), maps(3), maps(0), ext(0), ext(2), ext(2), ext(4)],
        [(effects.astype(F32), SMEM), (intercepts, SMEM), (latent, VMEM), (covariates, HBM),
         (region_ids, VMEM), (kappa_sq, VMEM), (land_mask, VMEM), (counts, HBM)],
        scratch=[pltpu.VMEM(covariates.shape, covariates.dtype), pltpu.VMEM(counts.shape, jnp.int32), DMA, DMA],
        flops=40 * cells, moved=12 * cells, limit=8,
    )
    packed = ((4 * weeks + 2, cols), VMEM)
    kappa, field, image, grad, search, near, far = call(
        edge_kernel,
        [maps(3), ext(2), ext(1), ext(0), ext(4), packed, packed],
        [(old_far, VMEM), (old_near, VMEM), (eta, VMEM), (inv, VMEM),
         (kappa, VMEM), (field, VMEM), (image, VMEM), (grad, VMEM), (search, VMEM)],
        aliases={4 + k: k for k in range(5)},
        flops=10 * cells, moved=cells,
    )
    near, far = swap_rows(near, far)
    grad, weight, inv, search, first, image, second, second_image, partial = call(
        inner_kernel,
        [ext(0), ext(2), ext(2), ext(4), ext(3), ext(0), ext(2), ext(1), ((32, LANES), VMEM)],
        [(kappa, VMEM), (eta, VMEM), (land, VMEM), (tally, VMEM), (field, VMEM), (image, VMEM),
         (grad, VMEM), (weight, VMEM), (inv, VMEM), (search, VMEM)],
        aliases={6 + k: k for k in range(4)},
        flops=120 * cells, moved=12 * cells,
    )
    weight, inv, search, first, image, second, second_image, sums = call(
        outer_kernel,
        [ext(2), ext(2), ext(4), ext(3), ext(0), ext(2), ext(1), ((8, LANES), VMEM)],
        [(old_far, VMEM), (old_near, VMEM), (far, VMEM), (near, VMEM), (kappa, VMEM), (field, VMEM),
         (grad, VMEM), (partial, VMEM), (weight, VMEM), (inv, VMEM), (search, VMEM), (first, VMEM), (image, VMEM),
         (second, VMEM), (second_image, VMEM)],
        aliases={8 + k: k for k in range(7)},
        flops=20 * cells, moved=cells,
    )
    half = rows // 2

    def last_rows(low, count):
        return lambda gate: call(
            functools.partial(last_kernel, low),
            [((count, weeks, cols), VMEM)],
            [(gate, VMEM), (kappa, VMEM), (weight, VMEM), (second, VMEM), (second_image, VMEM)],
            flops=4 * cells, moved=cells,
        )[0]

    sums, (upper, lower) = all_sum(sums, [last_rows(0, half), last_rows(half, rows - half)])
    return call(
        final_kernel,
        [(latent.shape, ANY), (latent.shape, ANY)],
        [(sums, VMEM), (grad, VMEM), (search, VMEM), (image, VMEM), (second, VMEM), (upper, VMEM), (lower, VMEM)],
        scratch=[pltpu.VMEM((rows, weeks, cols), F32), pltpu.VMEM((rows, weeks, cols), F32), DMA((rows,)), DMA((rows,))],
        flops=8 * cells, moved=8 * cells, limit=6,
    )


def solution(mesh):
    placed = (
        P(None, "gx", "region"),
        P(None, "gx", "region"),
        P("gx", "region"),
        P("gx", "region"),
        P("gx", "region"),
        P(None, "gx", "region"),
        P("region"),
        P("region"),
    )
    return jax.shard_map(
        shards,
        mesh=mesh,
        in_specs=placed,
        out_specs=(P(None, "gx", "region"), P(None, "gx", "region")),
        check_vma=False,
    )
```

```python
import functools

import jax
import jax.numpy as jnp
from jax import lax
from jax.experimental import pallas as pl
from jax.experimental.pallas import tpu as pltpu
from jax.sharding import PartitionSpec as P

AX = "gx"
LANES = 128
prior_scale = 0.04
time_coupling = 0.5
F32 = jnp.float32
VMEM = pltpu.VMEM
MIB = 1 << 20


def pair_maps(count):
    first = [(i, i ^ 1) for i in range(count) if (i ^ 1) < count]
    second = [(i, ((i + 1) ^ 1) - 1) for i in range(count) if 0 <= ((i + 1) ^ 1) - 1 < count]
    return first, second


def swap_rows(near, far):
    swap, cross = pair_maps(lax.axis_size(AX))
    far = lax.ppermute(far, AX, cross)
    return lax.ppermute(near, AX, swap), far


def all_sum(values, works):
    count = lax.axis_size(AX)
    results = []
    if count & (count - 1):
        return lax.psum(values, AX), [work(values) for work in works]
    step = 1
    while step < count:
        got = lax.ppermute(values, AX, [(i, i ^ step) for i in range(count)])
        if step > 1 and len(results) < len(works):
            piece = works[len(results)](values)
            got, piece = lax.optimization_barrier((got, piece))
            results.append(piece)
        values = values + got
        step *= 2
    while len(results) < len(works):
        results.append(works[len(results)](values))
    return values, results


def row_of(ref, row):
    return [ref[row, :, c : c + LANES] for c in range(0, ref.shape[2], LANES)]


def put_row(ref, row, tiles):
    for j, tile in enumerate(tiles):
        ref[row, :, j * LANES : (j + 1) * LANES] = tile


def map_row(ref, row):
    return [ref[row, :, c : c + LANES] for c in range(0, ref.shape[2], LANES)]


def masks(weeks):
    lane = lax.broadcasted_iota(jnp.int32, (weeks, LANES), 1)
    week = lax.broadcasted_iota(jnp.int32, (weeks, LANES), 0)
    return lane == 0, lane == LANES - 1, week == 0, week == weeks - 1


def laplace_row(up, mid, down, kappa, mask):
    first, last = mask[0], mask[1]
    count = len(mid)
    to_right = [pltpu.roll(t, 1, 1) for t in mid]
    to_left = [pltpu.roll(t, LANES - 1, 1) for t in mid]
    out = []
    for j in range(count):
        west = jnp.where(first, to_right[j - 1] if j > 0 else 0.0, to_right[j])
        east = jnp.where(last, to_left[j + 1] if j + 1 < count else 0.0, to_left[j])
        out.append((kappa[j] + 4.0) * mid[j] - ((up[j] + down[j]) + (west + east)))
    return out


def temporal_tile(tile, mask):
    weeks = tile.shape[0]
    before = jnp.where(mask[2], tile, pltpu.roll(tile, 1, 0))
    after = jnp.where(mask[3], tile, pltpu.roll(tile, weeks - 1, 0))
    return (2.0 * tile - before) - after


def fold(tiles):
    parts = [t[h : h + 8] for t in tiles for h in range(0, t.shape[0], 8)]
    while len(parts) > 1:
        parts = [a + b for a, b in zip(parts[::2], parts[1::2])] + ([parts[-1]] if len(parts) % 2 else [])
    return parts[0]


def diag_base(kappa):
    return prior_scale * ((kappa + 4.0) * (kappa + 4.0) + 4.0) + 2.0 * time_coupling


def is_odd():
    return lax.axis_index(AX) % 2 == 1


def row_loop(low, high, body, carry=None, most=14):
    count = high - low
    step = max(k for k in range(1, most + 1) if count % k == 0)

    def chunk(i, value):
        for k in range(step):
            value = body(low + i * step + k, value)
        return value

    if step == count:
        return chunk(0, carry)
    if carry is None:
        lax.fori_loop(0, count // step, lambda i, z: (chunk(i, None), z)[1], 0)
        return None
    return lax.fori_loop(0, count // step, chunk, carry)


def pack_kernel(latent, kappa_hbm, land_hbm, first, second, kappa, land, sems):
    weeks, rows, cols = latent.shape
    odd = is_odd()
    copies = []
    for k, (out, base) in enumerate(((first, jnp.where(odd, 0, rows - 2)), (second, jnp.where(odd, rows - 2, 0)))):
        for d in range(2):
            copies.append(pltpu.make_async_copy(
                latent.at[:, base + d, :], out.at[d * weeks : (d + 1) * weeks, :], sems.at[2 * k + d]))
    map_copies = []
    for k, (source, target) in enumerate(((kappa_hbm, kappa), (land_hbm, land))):
        for d, at in enumerate((0, rows - 8)):
            map_copies.append(pltpu.make_async_copy(
                source.at[at : at + 8, :], target.at[8 * d : 8 * d + 8, :], sems.at[4 + 2 * k + d]))
    for copy in copies + map_copies:
        copy.start()
    for copy in map_copies:
        copy.wait()
    at = 2 * weeks
    for d in range(3):
        top, bottom = kappa[d : d + 1, :], kappa[13 + d : 14 + d, :]
        first[at + d : at + d + 1, :] = jnp.where(odd, top, bottom)
        second[at + d : at + d + 1, :] = jnp.where(odd, bottom, top)
    for d in range(2):
        top, bottom = (land[q : q + 1, :].astype(F32) for q in (d, 14 + d))
        first[at + 3 + d : at + 4 + d, :] = jnp.where(odd, top, bottom)
        second[at + 3 + d : at + 4 + d, :] = jnp.where(odd, bottom, top)
    for copy in copies:
        copy.wait()


def rows_first(source, target, shift):
    weeks, rows, cols = source.shape
    for r in range(0, rows, 8):
        for c in range(0, cols, LANES):
            block = source[:, r : r + 8, c : c + LANES].astype(F32)
            target[r + shift : r + shift + 8, :, c : c + LANES] = jnp.swapaxes(block, 0, 1)


def front_kernel(effects, intercepts, latent, covariates, zones, kappa_flat, land_flat, counts,
                 field, image, eta, tally, kappa, land, grad, weight, inv, search, covs, raw, ids_all, cov_sem, sem, zone_sem):
    weeks, rows, cols = latent.shape
    mask = masks(weeks)
    copy = pltpu.make_async_copy(counts, raw, sem)
    cov_copy = pltpu.make_async_copy(covariates, covs, cov_sem)
    zone_copy = pltpu.make_async_copy(zones, ids_all, zone_sem)
    zone_copy.start()
    cov_copy.start()
    copy.start()
    rows_first(latent, field, 2)
    for r in range(rows):
        kappa[r + 3] = kappa_flat[r : r + 1, :]
        land[r] = land_flat[r : r + 1, :].astype(F32)

    def inner_image(r, _):
        put_row(image, r + 1, laplace_row(
            row_of(field, r + 1), row_of(field, r + 2), row_of(field, r + 3), map_row(kappa, r + 3), mask))

    row_loop(1, rows - 1, inner_image)
    zone_copy.wait()
    cov_copy.wait()
    width = 2 * LANES
    for c in range(0, cols, width):
        total = jnp.zeros((rows, width), F32)
        ids = ids_all[:, c : c + width]
        for z in range(intercepts.shape[0]):
            total = jnp.where(ids == z, intercepts[z], total)
        for k in range(covs.shape[0]):
            total = total + effects[k] * covs[k, :, c : c + width].astype(F32)
        for r in range(rows):
            eta[r, :, c : c + width] = total[r : r + 1]
    copy.wait()
    rows_first(raw, tally, 0)
    for r in (0, 1, rows - 2, rows - 1):
        gradient_row(r, field, tally, eta, land, kappa, None, grad, weight, inv, search, mask)
    for r in (2, 3, rows - 4, rows - 3):
        gradient_row(r, field, tally, eta, land, kappa, image, grad, weight, inv, search, mask)


def gradient_row(r, field, tally, eta, land, kappa, image, grad, weight, inv, search, mask):
    eta_row, land_row, kap, count_row = map_row(eta, r), map_row(land, r), map_row(kappa, r + 3), row_of(tally, r)
    if image is not None:
        outer = laplace_row(row_of(image, r), row_of(image, r + 1), row_of(image, r + 2), kap, mask)
    for j, tile in enumerate(row_of(field, r + 2)):
        on = land_row[j]
        curve = jnp.tanh(0.5 * (tile + eta_row[j]))
        heavy = on * (1.0 - curve * curve)
        inverse = 1.0 / (diag_base(kap[j]) + heavy)
        out = on * (count_row[j] - 2.0 - 2.0 * curve) - time_coupling * temporal_tile(tile, mask)
        part = slice(j * LANES, (j + 1) * LANES)
        weight[r + 2, :, part] = heavy
        inv[r + 2, :, part] = inverse
        if image is not None:
            out = out - prior_scale * outer[j]
            search[r + 4, :, part] = out * inverse
        grad[r, :, part] = out


def keep_inside(r, rows, tiles):
    if 0 <= r < rows:
        return tiles
    place, count = lax.axis_index(AX), lax.axis_size(AX)
    keep = jnp.where(place > 0 if r < 0 else place < count - 1, 1.0, 0.0)
    return [keep * t for t in tiles]


def halo_row(r, rows, depth, height, first, second):
    odd = is_odd()
    at = (r + depth if r < 0 else r - rows) * height
    a, b = (first, second) if r < 0 else (second, first)
    return [jnp.where(odd, a[at : at + height, c : c + LANES], b[at : at + height, c : c + LANES])
            for c in range(0, first.shape[1], LANES)]


def halo_line(above, line, first, second):
    odd = is_odd()
    a, b = (first, second) if above else (second, first)
    return [jnp.where(odd, a[line : line + 1, c : c + LANES], b[line : line + 1, c : c + LANES])
            for c in range(0, first.shape[1], LANES)]


def edge_kernel(got_second, got_first, eta, inv, kappa_in, field_in, image_in, grad_in, search_in,
                kappa, field, image, grad, search, first, second):
    weeks = field.shape[1]
    rows, _, cols = eta.shape
    mask = masks(weeks)
    odd = is_odd()
    for d in range(2):
        put_row(field, d, halo_row(d - 2, rows, 2, weeks, got_first, got_second))
        put_row(field, rows + 2 + d, halo_row(rows + d, rows, 2, weeks, got_first, got_second))
    for d in range(3):
        put_row(kappa, d, halo_line(True, 2 * weeks + d, got_first, got_second))
        put_row(kappa, rows + 3 + d, halo_line(False, 2 * weeks + d, got_first, got_second))
    for r in (-1, 0, rows - 1, rows):
        put_row(image, r + 1, keep_inside(r, rows, laplace_row(
            row_of(field, r + 1), row_of(field, r + 2), row_of(field, r + 3), map_row(kappa, r + 3), mask)))
    for r in (0, 1, rows - 2, rows - 1):
        outer = laplace_row(row_of(image, r), row_of(image, r + 1), row_of(image, r + 2), map_row(kappa, r + 3), mask)
        out = [a - prior_scale * b for a, b in zip(row_of(grad, r), outer)]
        put_row(grad, r, out)
        put_row(search, r + 4, [a * b for a, b in zip(out, row_of(inv, r + 2))])
    at = 4 * weeks
    for c in range(0, cols, LANES):
        part = slice(c, c + LANES)
        for d in range(4):
            top, bottom = search[4 + d, :, part], search[rows + d, :, part]
            first[d * weeks : (d + 1) * weeks, part] = jnp.where(odd, top, bottom)
            second[d * weeks : (d + 1) * weeks, part] = jnp.where(odd, bottom, top)
        for d in range(2):
            top, bottom = eta[d, :, part], eta[rows - 2 + d, :, part]
            first[at + d : at + d + 1, part] = jnp.where(odd, top, bottom)
            second[at + d : at + d + 1, part] = jnp.where(odd, bottom, top)


def mass_row(r, source, at, weight, mask):
    mid = row_of(source, at)
    return mid, [time_coupling * temporal_tile(m, mask) + h * m for m, h in zip(mid, row_of(weight, r + 2))]


def hessian_row(r, source, at, image, offset, kappa, weight, mask):
    outer = laplace_row(row_of(image, r + offset - 1), row_of(image, r + offset), row_of(image, r + offset + 1),
                        map_row(kappa, r + 3), mask)
    mid, mass = mass_row(r, source, at, weight, mask)
    return mid, [prior_scale * o + m for o, m in zip(outer, mass)]


def dot_rows(a, b):
    return fold([x * y for x, y in zip(a, b)])


def inner_kernel(kappa, eta, land, tally, field, start_image, grad_in, weight_in, inv_in, search_in,
                 grad, weight, inv, search, first, image, second, second_image, sums):
    weeks = grad.shape[1]
    rows = grad.shape[0]
    mask = masks(weeks)

    def gradient(r, _):
        gradient_row(r, field, tally, eta, land, kappa, start_image, grad, weight, inv, search, mask)

    row_loop(4, rows - 4, gradient, most=8)

    def inner_image(r, _):
        put_row(first, r + 3, laplace_row(
            row_of(search, r + 3), row_of(search, r + 4), row_of(search, r + 5), map_row(kappa, r + 3), mask))

    row_loop(1, rows - 1, inner_image)
    zero = jnp.zeros((8, LANES), F32)

    def apply(r, carry):
        rz, pq, cross, total = carry
        mid, out = hessian_row(r, search, r + 4, first, 3, kappa, weight, mask)
        other = [a * b for a, b in zip(out, row_of(inv, r + 2))]
        mass = [time_coupling * temporal_tile(y, mask) + h * y for y, h in zip(other, row_of(weight, r + 2))]
        put_row(image, r, out)
        put_row(second, r + 2, other)
        return (rz + dot_rows(mid, row_of(grad, r)), pq + dot_rows(mid, out), cross + dot_rows(other, out),
                total + dot_rows(other, mass))

    rz, pq, cross, total = row_loop(2, rows - 2, apply, (zero, zero, zero, zero), most=7)

    def second_inner(r, square):
        out = laplace_row(
            row_of(second, r + 1), row_of(second, r + 2), row_of(second, r + 3), map_row(kappa, r + 3), mask)
        put_row(second_image, r + 1, out)
        return square + dot_rows(out, out)

    square = row_loop(3, rows - 3, second_inner, zero)
    for k, value in enumerate((rz, pq, cross, total + prior_scale * square)):
        sums[8 * k : 8 * k + 8, :] = value


def outer_kernel(old_second, old_first, got_second, got_first, kappa, field, grad, partial,
                 weight_in, inv_in, search_in, first_in, image_in, second_in, second_image_in,
                 weight, inv, search, first, image, second, second_image, sums):
    weeks = grad.shape[1]
    rows = grad.shape[0]
    mask = masks(weeks)
    for d in range(4):
        put_row(search, d, halo_row(d - 4, rows, 4, weeks, got_first, got_second))
        put_row(search, rows + 4 + d, halo_row(rows + d, rows, 4, weeks, got_first, got_second))
    for above in (True, False):
        for d in range(2):
            r = d - 2 if above else rows + d
            eta_row = halo_line(above, 4 * weeks + d, got_first, got_second)
            land_row = halo_line(above, 2 * weeks + 3 + d, old_first, old_second)
            heavy = []
            for j, tile in enumerate(row_of(field, r + 2)):
                curve = jnp.tanh(0.5 * (tile + eta_row[j]))
                heavy.append(land_row[j] * (1.0 - curve * curve))
            put_row(weight, r + 2, heavy)
            put_row(inv, r + 2, [1.0 / (diag_base(k) + h) for k, h in zip(map_row(kappa, r + 3), heavy)])

    for r in (-2, -1, 0, rows - 1, rows, rows + 1):
        put_row(first, r + 3, keep_inside(r, rows, laplace_row(
            row_of(search, r + 3), row_of(search, r + 4), row_of(search, r + 5), map_row(kappa, r + 3), mask)))
    rz, pq, cross, total = (partial[8 * k : 8 * k + 8, :] for k in range(4))
    for r in (-1, 0, 1, rows - 2, rows - 1, rows):
        mid, out = hessian_row(r, search, r + 4, first, 3, kappa, weight, mask)
        other = keep_inside(r, rows, [a * b for a, b in zip(out, row_of(inv, r + 2))])
        put_row(second, r + 2, other)
        if 0 <= r < rows:
            put_row(image, r, out)
            mass = [time_coupling * temporal_tile(y, mask) + h * y for y, h in zip(other, row_of(weight, r + 2))]
            rz, pq, cross = rz + dot_rows(mid, row_of(grad, r)), pq + dot_rows(mid, out), cross + dot_rows(other, out)
            total = total + dot_rows(other, mass)
    for r in (0, 1, 2, rows - 3, rows - 2, rows - 1):
        out = laplace_row(
            row_of(second, r + 1), row_of(second, r + 2), row_of(second, r + 3), map_row(kappa, r + 3), mask)
        put_row(second_image, r + 1, out)
        total = total + prior_scale * dot_rows(out, out)
    sums[...] = jnp.zeros_like(sums)
    for k, value in enumerate((rz, pq, cross, total)):
        sums[k : k + 1, :] = jnp.sum(value, axis=0, keepdims=True)


def last_kernel(low, gate, kappa, weight, second, second_image, last):
    mask = masks(last.shape[1])

    def apply(r, _):
        put_row(last, r, hessian_row(r + low, second, r + low + 2, second_image, 1, kappa, weight, mask)[1])

    row_loop(0, last.shape[0], apply, most=8)


def rim_kernel(gate, kappa, weight, inv, search, first, second, second_image, last):
    rows = second_image.shape[0] - 2
    count = last.shape[0] - 1
    mask = masks(last.shape[1])
    for r, away in ((0, -1), (rows - 1, 1)):
        rim = [r + away * d for d in range(5)]
        tiles = keep_inside(rim[3], rows, laplace_row(
            row_of(search, rim[4] + 4), row_of(search, rim[3] + 4), row_of(search, rim[2] + 4),
            map_row(kappa, rim[3] + 3), mask))
        outer = laplace_row(tiles, row_of(first, rim[2] + 3), row_of(first, rim[1] + 3), map_row(kappa, rim[2] + 3), mask)
        mass = mass_row(rim[2], search, rim[2] + 4, weight, mask)[1]
        tiles = keep_inside(rim[2], rows, [
            (prior_scale * o + m) * d for o, m, d in zip(outer, mass, row_of(inv, rim[2] + 2))])
        tiles = keep_inside(rim[1], rows, laplace_row(
            tiles, row_of(second, rim[1] + 2), row_of(second, r + 2), map_row(kappa, rim[1] + 3), mask))
        outer = laplace_row(
            tiles, row_of(second_image, r + 1), row_of(second_image, r - away + 1), map_row(kappa, r + 3), mask)
        mass = mass_row(r, second, r + 2, weight, mask)[1]
        put_row(last, 0 if r == 0 else count, [prior_scale * o + m for o, m in zip(outer, mass)])

    def apply(r, _):
        put_row(last, r, hessian_row(r, second, r + 2, second_image, 1, kappa, weight, mask)[1])

    row_loop(1, count, apply, most=8)


def final_kernel(sums, grad, search, image, second, rim, upper, lower, newton_out, residual_out, newton, residual, newton_sem, residual_sem):
    rows, weeks, cols = grad.shape
    rz, pq, cross, total = (jnp.sum(sums[k : k + 1, :], axis=1, keepdims=True) for k in range(4))
    first, cross, total = rz / pq, cross / pq, total / pq
    scale = 1.0 / (total - cross * cross)
    along = jnp.broadcast_to((first * total - cross) * scale, (weeks, LANES))
    across = jnp.broadcast_to((first * cross - 1.0) * scale, (weeks, LANES))

    def copies(r):
        return (
            pltpu.make_async_copy(newton.at[r], newton_out.at[:, r, :], newton_sem.at[r]),
            pltpu.make_async_copy(residual.at[r], residual_out.at[:, r, :], residual_sem.at[r]),
        )

    one = rim.shape[0] - 1
    two = one + upper.shape[0]

    def combine(r, last, at):
        put_row(newton, r, [along * p - across * y for p, y in zip(row_of(search, r + 4), row_of(second, r + 2))])
        put_row(residual, r, [
            g - along * w + across * h for g, w, h in zip(row_of(grad, r), row_of(image, r), row_of(last, r - at))])
        for copy in copies(r):
            copy.start()

    row_loop(0, one, lambda r, _: combine(r, rim, 0), most=7)
    row_loop(one, two, lambda r, _: combine(r, upper, one), most=7)
    row_loop(two, rows - 1, lambda r, _: combine(r, lower, two), most=7)
    combine(rows - 1, rim, rows - 1 - one)
    for r in range(rows):
        for copy in copies(r):
            copy.wait()


def call(kernel, outs, ins, scratch=(), aliases=None, limit=2, flops=0, moved=0):
    shapes = tuple(VMEM(shape, F32) if space is VMEM else jax.ShapeDtypeStruct(shape, F32) for shape, space in outs)
    return pl.pallas_call(
        kernel,
        out_shape=shapes,
        in_specs=[pl.BlockSpec(memory_space=space) for _, space in ins],
        out_specs=tuple(pl.BlockSpec(memory_space=space) for _, space in outs),
        scratch_shapes=list(scratch),
        input_output_aliases=aliases or {},
        compiler_params=pltpu.CompilerParams(vmem_limit_bytes=limit * MIB),
        cost_estimate=pl.CostEstimate(flops=flops, bytes_accessed=moved, transcendentals=0),
    )(*[pltpu.with_memory_space_constraint(array, space) if space is pltpu.HBM else array for array, space in ins])


def shards(latent, counts, land_mask, region_ids, kappa_sq, covariates, effects, intercepts):
    weeks, rows, cols = latent.shape

    def ext(depth):
        return ((rows + 2 * depth, weeks, cols), VMEM)

    def maps(depth):
        return ((rows + 2 * depth, 1, cols), VMEM)

    cells = weeks * rows * cols
    SMEM, ANY, HBM, DMA = pltpu.SMEM, pl.ANY, pltpu.HBM, pltpu.SemaphoreType.DMA
    packed = ((2 * weeks + 5, cols), VMEM)
    near, far = call(
        pack_kernel,
        [packed, packed],
        [(latent, HBM), (kappa_sq, HBM), (land_mask, HBM)],
        scratch=[pltpu.VMEM((16, cols), F32), pltpu.VMEM((16, cols), jnp.int32), DMA((8,))],
        flops=cells // 16, moved=cells,
    )
    old_near, old_far = swap_rows(near, far)
    field, image, eta, tally, kappa, land, grad, weight, inv, search = call(
        front_kernel,
        [ext(2), ext(1), maps(0), ext(0), maps(3), maps(0), ext(0), ext(2), ext(2), ext(4)],
        [(effects.astype(F32), SMEM), (intercepts, SMEM), (latent, VMEM), (covariates, HBM),
         (region_ids, HBM), (kappa_sq, VMEM), (land_mask, VMEM), (counts, HBM)],
        scratch=[pltpu.VMEM(covariates.shape, covariates.dtype), pltpu.VMEM(counts.shape, jnp.int32),
                 pltpu.VMEM((rows, cols), jnp.int32), DMA, DMA, DMA],
        flops=40 * cells, moved=12 * cells, limit=8,
    )
    packed = ((4 * weeks + 2, cols), VMEM)
    kappa, field, image, grad, search, near, far = call(
        edge_kernel,
        [maps(3), ext(2), ext(1), ext(0), ext(4), packed, packed],
        [(old_far, VMEM), (old_near, VMEM), (eta, VMEM), (inv, VMEM),
         (kappa, VMEM), (field, VMEM), (image, VMEM), (grad, VMEM), (search, VMEM)],
        aliases={4 + k: k for k in range(5)},
        flops=10 * cells, moved=cells,
    )
    near, far = swap_rows(near, far)
    grad, weight, inv, search, first, image, second, second_image, partial = call(
        inner_kernel,
        [ext(0), ext(2), ext(2), ext(4), ext(3), ext(0), ext(2), ext(1), ((32, LANES), VMEM)],
        [(kappa, VMEM), (eta, VMEM), (land, VMEM), (tally, VMEM), (field, VMEM), (image, VMEM),
         (grad, VMEM), (weight, VMEM), (inv, VMEM), (search, VMEM)],
        aliases={6 + k: k for k in range(4)},
        flops=120 * cells, moved=12 * cells,
    )
    weight, inv, search, first, image, second, second_image, sums = call(
        outer_kernel,
        [ext(2), ext(2), ext(4), ext(3), ext(0), ext(2), ext(1), ((8, LANES), VMEM)],
        [(old_far, VMEM), (old_near, VMEM), (far, VMEM), (near, VMEM), (kappa, VMEM), (field, VMEM),
         (grad, VMEM), (partial, VMEM), (weight, VMEM), (inv, VMEM), (search, VMEM), (first, VMEM), (image, VMEM),
         (second, VMEM), (second_image, VMEM)],
        aliases={8 + k: k for k in range(7)},
        flops=20 * cells, moved=cells,
    )
    one = 1 + (rows - 2) // 5
    two = one + (rows - 1 - one) // 2

    def rim_rows(gate):
        return call(
            rim_kernel,
            [((one + 1, weeks, cols), VMEM)],
            [(gate, VMEM), (kappa, VMEM), (weight, VMEM), (inv, VMEM), (search, VMEM), (first, VMEM), (second, VMEM),
             (second_image, VMEM)],
            flops=4 * cells, moved=cells,
        )[0]

    def last_rows(low, count):
        return lambda gate: call(
            functools.partial(last_kernel, low),
            [((count, weeks, cols), VMEM)],
            [(gate, VMEM), (kappa, VMEM), (weight, VMEM), (second, VMEM), (second_image, VMEM)],
            flops=4 * cells, moved=cells,
        )[0]

    sums, (rim, upper, lower) = all_sum(sums, [rim_rows, last_rows(one, two - one), last_rows(two, rows - 1 - two)])
    return call(
        final_kernel,
        [(latent.shape, ANY), (latent.shape, ANY)],
        [(sums, VMEM), (grad, VMEM), (search, VMEM), (image, VMEM), (second, VMEM),
         (rim, VMEM), (upper, VMEM), (lower, VMEM)],
        scratch=[pltpu.VMEM((rows, weeks, cols), F32), pltpu.VMEM((rows, weeks, cols), F32), DMA((rows,)), DMA((rows,))],
        flops=8 * cells, moved=8 * cells, limit=6,
    )


def solution(mesh):
    placed = (
        P(None, "gx", "region"),
        P(None, "gx", "region"),
        P("gx", "region"),
        P("gx", "region"),
        P("gx", "region"),
        P(None, "gx", "region"),
        P("region"),
        P("region"),
    )
    return jax.shard_map(
        shards,
        mesh=mesh,
        in_specs=placed,
        out_specs=(P(None, "gx", "region"), P(None, "gx", "region")),
        check_vma=False,
    )
```

```python
import functools

import jax
import jax.numpy as jnp
from jax import lax
from jax.experimental import pallas as pl
from jax.experimental.pallas import tpu as pltpu
from jax.sharding import PartitionSpec as P

AX = "gx"
LANES = 128
prior_scale = 0.04
time_coupling = 0.5
F32 = jnp.float32
VMEM = pltpu.VMEM
MIB = 1 << 20


def pair_maps(count):
    first = [(i, i ^ 1) for i in range(count) if (i ^ 1) < count]
    second = [(i, ((i + 1) ^ 1) - 1) for i in range(count) if 0 <= ((i + 1) ^ 1) - 1 < count]
    return first, second


def swap_rows(near, far):
    swap, cross = pair_maps(lax.axis_size(AX))
    far = lax.ppermute(far, AX, cross)
    return lax.ppermute(near, AX, swap), far


def all_sum(values, works):
    count = lax.axis_size(AX)
    results = []
    if count & (count - 1):
        return lax.psum(values, AX), [work(values) for work in works]
    rounds = [(1,)] if count > 1 else []
    step = 2
    while step < count:
        wide = 2 * step < count
        rounds.append((step, 2 * step, 3 * step) if wide else (step,))
        step *= 4 if wide else 2
    for number, partners in enumerate(rounds):
        got = [lax.ppermute(values, AX, [(i, i ^ k) for i in range(count)]) for k in partners]
        if number > 0 and len(results) < len(works):
            piece = works[len(results)](values)
            got, piece = lax.optimization_barrier((got, piece))
            results.append(piece)
        values = values + got[0]
        if len(got) > 1:
            values = values + (got[1] + got[2])
    while len(results) < len(works):
        results.append(works[len(results)](values))
    return values, results


def row_of(ref, row):
    return [ref[row, :, c : c + LANES] for c in range(0, ref.shape[2], LANES)]


def put_row(ref, row, tiles):
    for j, tile in enumerate(tiles):
        ref[row, :, j * LANES : (j + 1) * LANES] = tile


def map_row(ref, row):
    return [ref[row, :, c : c + LANES] for c in range(0, ref.shape[2], LANES)]


def masks(weeks):
    lane = lax.broadcasted_iota(jnp.int32, (weeks, LANES), 1)
    week = lax.broadcasted_iota(jnp.int32, (weeks, LANES), 0)
    return lane == 0, lane == LANES - 1, week == 0, week == weeks - 1


def laplace_row(up, mid, down, kappa, mask):
    first, last = mask[0], mask[1]
    count = len(mid)
    to_right = [pltpu.roll(t, 1, 1) for t in mid]
    to_left = [pltpu.roll(t, LANES - 1, 1) for t in mid]
    out = []
    for j in range(count):
        west = jnp.where(first, to_right[j - 1] if j > 0 else 0.0, to_right[j])
        east = jnp.where(last, to_left[j + 1] if j + 1 < count else 0.0, to_left[j])
        out.append((kappa[j] + 4.0) * mid[j] - ((up[j] + down[j]) + (west + east)))
    return out


def temporal_tile(tile, mask):
    weeks = tile.shape[0]
    before = jnp.where(mask[2], tile, pltpu.roll(tile, 1, 0))
    after = jnp.where(mask[3], tile, pltpu.roll(tile, weeks - 1, 0))
    return (2.0 * tile - before) - after


def fold(tiles):
    parts = [t[h : h + 8] for t in tiles for h in range(0, t.shape[0], 8)]
    while len(parts) > 1:
        parts = [a + b for a, b in zip(parts[::2], parts[1::2])] + ([parts[-1]] if len(parts) % 2 else [])
    return parts[0]


def diag_base(kappa):
    return prior_scale * ((kappa + 4.0) * (kappa + 4.0) + 4.0) + 2.0 * time_coupling


def is_odd():
    return lax.axis_index(AX) % 2 == 1


def row_loop(low, high, body, carry=None, most=14):
    count = high - low
    step = max(k for k in range(1, most + 1) if count % k == 0)

    def chunk(i, value):
        for k in range(step):
            value = body(low + i * step + k, value)
        return value

    if step == count:
        return chunk(0, carry)
    if carry is None:
        lax.fori_loop(0, count // step, lambda i, z: (chunk(i, None), z)[1], 0)
        return None
    return lax.fori_loop(0, count // step, chunk, carry)


def pack_kernel(latent, kappa_hbm, land_hbm, first, second, kappa, land, sems):
    weeks, rows, cols = latent.shape
    odd = is_odd()
    copies = []
    for k, (out, base) in enumerate(((first, jnp.where(odd, 0, rows - 2)), (second, jnp.where(odd, rows - 2, 0)))):
        for d in range(2):
            copies.append(pltpu.make_async_copy(
                latent.at[:, base + d, :], out.at[d * weeks : (d + 1) * weeks, :], sems.at[2 * k + d]))
    map_copies = []
    for k, (source, target) in enumerate(((kappa_hbm, kappa), (land_hbm, land))):
        for d, at in enumerate((0, rows - 8)):
            map_copies.append(pltpu.make_async_copy(
                source.at[at : at + 8, :], target.at[8 * d : 8 * d + 8, :], sems.at[4 + 2 * k + d]))
    for copy in copies + map_copies:
        copy.start()
    for copy in map_copies:
        copy.wait()
    at = 2 * weeks
    for d in range(3):
        top, bottom = kappa[d : d + 1, :], kappa[13 + d : 14 + d, :]
        first[at + d : at + d + 1, :] = jnp.where(odd, top, bottom)
        second[at + d : at + d + 1, :] = jnp.where(odd, bottom, top)
    for d in range(2):
        top, bottom = (land[q : q + 1, :].astype(F32) for q in (d, 14 + d))
        first[at + 3 + d : at + 4 + d, :] = jnp.where(odd, top, bottom)
        second[at + 3 + d : at + 4 + d, :] = jnp.where(odd, bottom, top)
    for copy in copies:
        copy.wait()


def rows_first(source, target, shift):
    weeks, rows, cols = source.shape
    for r in range(0, rows, 8):
        for c in range(0, cols, LANES):
            block = source[:, r : r + 8, c : c + LANES].astype(F32)
            target[r + shift : r + shift + 8, :, c : c + LANES] = jnp.swapaxes(block, 0, 1)


def front_kernel(effects, intercepts, latent, covariates, zones, kappa_flat, land_flat, counts,
                 field, image, eta, tally, kappa, land, grad, weight, inv, search, covs, raw, ids_all, cov_sem, sem, zone_sem):
    weeks, rows, cols = latent.shape
    mask = masks(weeks)
    copy = pltpu.make_async_copy(counts, raw, sem)
    cov_copy = pltpu.make_async_copy(covariates, covs, cov_sem)
    zone_copy = pltpu.make_async_copy(zones, ids_all, zone_sem)
    zone_copy.start()
    cov_copy.start()
    copy.start()
    rows_first(latent, field, 2)
    for r in range(rows):
        kappa[r + 3] = kappa_flat[r : r + 1, :]
        land[r] = land_flat[r : r + 1, :].astype(F32)

    def inner_image(r, _):
        put_row(image, r + 1, laplace_row(
            row_of(field, r + 1), row_of(field, r + 2), row_of(field, r + 3), map_row(kappa, r + 3), mask))

    row_loop(1, rows - 1, inner_image)
    zone_copy.wait()
    cov_copy.wait()
    width = 2 * LANES
    for c in range(0, cols, width):
        total = jnp.zeros((rows, width), F32)
        ids = ids_all[:, c : c + width]
        for z in range(intercepts.shape[0]):
            total = jnp.where(ids == z, intercepts[z], total)
        for k in range(covs.shape[0]):
            total = total + effects[k] * covs[k, :, c : c + width].astype(F32)
        for r in range(rows):
            eta[r, :, c : c + width] = total[r : r + 1]
    copy.wait()
    rows_first(raw, tally, 0)
    for r in (0, 1, rows - 2, rows - 1):
        gradient_row(r, field, tally, eta, land, kappa, None, grad, weight, inv, search, mask)
    for r in (2, 3, rows - 4, rows - 3):
        gradient_row(r, field, tally, eta, land, kappa, image, grad, weight, inv, search, mask)


def gradient_row(r, field, tally, eta, land, kappa, image, grad, weight, inv, search, mask):
    eta_row, land_row, kap, count_row = map_row(eta, r), map_row(land, r), map_row(kappa, r + 3), row_of(tally, r)
    if image is not None:
        outer = laplace_row(row_of(image, r), row_of(image, r + 1), row_of(image, r + 2), kap, mask)
    for j, tile in enumerate(row_of(field, r + 2)):
        on = land_row[j]
        curve = jnp.tanh(0.5 * (tile + eta_row[j]))
        heavy = on * (1.0 - curve * curve)
        inverse = 1.0 / (diag_base(kap[j]) + heavy)
        out = on * (count_row[j] - 2.0 - 2.0 * curve) - time_coupling * temporal_tile(tile, mask)
        part = slice(j * LANES, (j + 1) * LANES)
        weight[r + 2, :, part] = heavy
        inv[r + 2, :, part] = inverse
        if image is not None:
            out = out - prior_scale * outer[j]
            search[r + 4, :, part] = out * inverse
        grad[r, :, part] = out


def keep_inside(r, rows, tiles):
    if 0 <= r < rows:
        return tiles
    place, count = lax.axis_index(AX), lax.axis_size(AX)
    keep = jnp.where(place > 0 if r < 0 else place < count - 1, 1.0, 0.0)
    return [keep * t for t in tiles]


def halo_row(r, rows, depth, height, first, second):
    odd = is_odd()
    at = (r + depth if r < 0 else r - rows) * height
    a, b = (first, second) if r < 0 else (second, first)
    return [jnp.where(odd, a[at : at + height, c : c + LANES], b[at : at + height, c : c + LANES])
            for c in range(0, first.shape[1], LANES)]


def halo_line(above, line, first, second):
    odd = is_odd()
    a, b = (first, second) if above else (second, first)
    return [jnp.where(odd, a[line : line + 1, c : c + LANES], b[line : line + 1, c : c + LANES])
            for c in range(0, first.shape[1], LANES)]


def edge_kernel(got_second, got_first, eta, inv, kappa_in, field_in, image_in, grad_in, search_in,
                kappa, field, image, grad, search, first, second):
    weeks = field.shape[1]
    rows, _, cols = eta.shape
    mask = masks(weeks)
    odd = is_odd()
    for d in range(2):
        put_row(field, d, halo_row(d - 2, rows, 2, weeks, got_first, got_second))
        put_row(field, rows + 2 + d, halo_row(rows + d, rows, 2, weeks, got_first, got_second))
    for d in range(3):
        put_row(kappa, d, halo_line(True, 2 * weeks + d, got_first, got_second))
        put_row(kappa, rows + 3 + d, halo_line(False, 2 * weeks + d, got_first, got_second))
    for r in (-1, 0, rows - 1, rows):
        put_row(image, r + 1, keep_inside(r, rows, laplace_row(
            row_of(field, r + 1), row_of(field, r + 2), row_of(field, r + 3), map_row(kappa, r + 3), mask)))
    for r in (0, 1, rows - 2, rows - 1):
        outer = laplace_row(row_of(image, r), row_of(image, r + 1), row_of(image, r + 2), map_row(kappa, r + 3), mask)
        out = [a - prior_scale * b for a, b in zip(row_of(grad, r), outer)]
        put_row(grad, r, out)
        put_row(search, r + 4, [a * b for a, b in zip(out, row_of(inv, r + 2))])
    at = 4 * weeks
    for c in range(0, cols, LANES):
        part = slice(c, c + LANES)
        for d in range(4):
            top, bottom = search[4 + d, :, part], search[rows + d, :, part]
            first[d * weeks : (d + 1) * weeks, part] = jnp.where(odd, top, bottom)
            second[d * weeks : (d + 1) * weeks, part] = jnp.where(odd, bottom, top)
        for d in range(2):
            top, bottom = eta[d, :, part], eta[rows - 2 + d, :, part]
            first[at + d : at + d + 1, part] = jnp.where(odd, top, bottom)
            second[at + d : at + d + 1, part] = jnp.where(odd, bottom, top)


def mass_row(r, source, at, weight, mask):
    mid = row_of(source, at)
    return mid, [time_coupling * temporal_tile(m, mask) + h * m for m, h in zip(mid, row_of(weight, r + 2))]


def hessian_row(r, source, at, image, offset, kappa, weight, mask):
    outer = laplace_row(row_of(image, r + offset - 1), row_of(image, r + offset), row_of(image, r + offset + 1),
                        map_row(kappa, r + 3), mask)
    mid, mass = mass_row(r, source, at, weight, mask)
    return mid, [prior_scale * o + m for o, m in zip(outer, mass)]


def dot_rows(a, b):
    return fold([x * y for x, y in zip(a, b)])


def inner_kernel(kappa, eta, land, tally, field, start_image, grad_in, weight_in, inv_in, search_in,
                 grad, weight, inv, search, first, image, second, second_image, sums):
    weeks = grad.shape[1]
    rows = grad.shape[0]
    mask = masks(weeks)

    def gradient(r, _):
        gradient_row(r, field, tally, eta, land, kappa, start_image, grad, weight, inv, search, mask)

    row_loop(4, rows - 4, gradient, most=8)

    def inner_image(r, _):
        put_row(first, r + 3, laplace_row(
            row_of(search, r + 3), row_of(search, r + 4), row_of(search, r + 5), map_row(kappa, r + 3), mask))

    row_loop(1, rows - 1, inner_image)
    zero = jnp.zeros((8, LANES), F32)

    def apply(r, carry):
        rz, pq, cross, total = carry
        mid, out = hessian_row(r, search, r + 4, first, 3, kappa, weight, mask)
        other = [a * b for a, b in zip(out, row_of(inv, r + 2))]
        mass = [time_coupling * temporal_tile(y, mask) + h * y for y, h in zip(other, row_of(weight, r + 2))]
        put_row(image, r, out)
        put_row(second, r + 2, other)
        return (rz + dot_rows(mid, row_of(grad, r)), pq + dot_rows(mid, out), cross + dot_rows(other, out),
                total + dot_rows(other, mass))

    rz, pq, cross, total = row_loop(2, rows - 2, apply, (zero, zero, zero, zero), most=7)

    def second_inner(r, square):
        out = laplace_row(
            row_of(second, r + 1), row_of(second, r + 2), row_of(second, r + 3), map_row(kappa, r + 3), mask)
        put_row(second_image, r + 1, out)
        return square + dot_rows(out, out)

    square = row_loop(3, rows - 3, second_inner, zero)
    for k, value in enumerate((rz, pq, cross, total + prior_scale * square)):
        sums[8 * k : 8 * k + 8, :] = value


def outer_kernel(old_second, old_first, got_second, got_first, kappa, field, grad, partial,
                 weight_in, inv_in, search_in, first_in, image_in, second_in, second_image_in,
                 weight, inv, search, first, image, second, second_image, sums):
    weeks = grad.shape[1]
    rows = grad.shape[0]
    mask = masks(weeks)
    for d in range(4):
        put_row(search, d, halo_row(d - 4, rows, 4, weeks, got_first, got_second))
        put_row(search, rows + 4 + d, halo_row(rows + d, rows, 4, weeks, got_first, got_second))
    for above in (True, False):
        for d in range(2):
            r = d - 2 if above else rows + d
            eta_row = halo_line(above, 4 * weeks + d, got_first, got_second)
            land_row = halo_line(above, 2 * weeks + 3 + d, old_first, old_second)
            heavy = []
            for j, tile in enumerate(row_of(field, r + 2)):
                curve = jnp.tanh(0.5 * (tile + eta_row[j]))
                heavy.append(land_row[j] * (1.0 - curve * curve))
            put_row(weight, r + 2, heavy)
            put_row(inv, r + 2, [1.0 / (diag_base(k) + h) for k, h in zip(map_row(kappa, r + 3), heavy)])

    for r in (-2, -1, 0, rows - 1, rows, rows + 1):
        put_row(first, r + 3, keep_inside(r, rows, laplace_row(
            row_of(search, r + 3), row_of(search, r + 4), row_of(search, r + 5), map_row(kappa, r + 3), mask)))
    rz, pq, cross, total = (partial[8 * k : 8 * k + 8, :] for k in range(4))
    for r in (-1, 0, 1, rows - 2, rows - 1, rows):
        mid, out = hessian_row(r, search, r + 4, first, 3, kappa, weight, mask)
        other = keep_inside(r, rows, [a * b for a, b in zip(out, row_of(inv, r + 2))])
        put_row(second, r + 2, other)
        if 0 <= r < rows:
            put_row(image, r, out)
            mass = [time_coupling * temporal_tile(y, mask) + h * y for y, h in zip(other, row_of(weight, r + 2))]
            rz, pq, cross = rz + dot_rows(mid, row_of(grad, r)), pq + dot_rows(mid, out), cross + dot_rows(other, out)
            total = total + dot_rows(other, mass)
    for r in (0, 1, 2, rows - 3, rows - 2, rows - 1):
        out = laplace_row(
            row_of(second, r + 1), row_of(second, r + 2), row_of(second, r + 3), map_row(kappa, r + 3), mask)
        put_row(second_image, r + 1, out)
        total = total + prior_scale * dot_rows(out, out)
    sums[...] = jnp.zeros_like(sums)
    for k, value in enumerate((rz, pq, cross, total)):
        sums[k : k + 1, :] = jnp.sum(value, axis=0, keepdims=True)


def last_kernel(low, gate, kappa, weight, second, second_image, last):
    mask = masks(last.shape[1])

    def apply(r, _):
        put_row(last, r, hessian_row(r + low, second, r + low + 2, second_image, 1, kappa, weight, mask)[1])

    row_loop(0, last.shape[0], apply, most=8)


def rim_kernel(gate, kappa, weight, inv, search, first, second, second_image, last):
    rows = second_image.shape[0] - 2
    count = last.shape[0] - 1
    mask = masks(last.shape[1])
    for r, away in ((0, -1), (rows - 1, 1)):
        rim = [r + away * d for d in range(5)]
        tiles = keep_inside(rim[3], rows, laplace_row(
            row_of(search, rim[4] + 4), row_of(search, rim[3] + 4), row_of(search, rim[2] + 4),
            map_row(kappa, rim[3] + 3), mask))
        outer = laplace_row(tiles, row_of(first, rim[2] + 3), row_of(first, rim[1] + 3), map_row(kappa, rim[2] + 3), mask)
        mass = mass_row(rim[2], search, rim[2] + 4, weight, mask)[1]
        tiles = keep_inside(rim[2], rows, [
            (prior_scale * o + m) * d for o, m, d in zip(outer, mass, row_of(inv, rim[2] + 2))])
        tiles = keep_inside(rim[1], rows, laplace_row(
            tiles, row_of(second, rim[1] + 2), row_of(second, r + 2), map_row(kappa, rim[1] + 3), mask))
        outer = laplace_row(
            tiles, row_of(second_image, r + 1), row_of(second_image, r - away + 1), map_row(kappa, r + 3), mask)
        mass = mass_row(r, second, r + 2, weight, mask)[1]
        put_row(last, 0 if r == 0 else count, [prior_scale * o + m for o, m in zip(outer, mass)])

    def apply(r, _):
        put_row(last, r, hessian_row(r, second, r + 2, second_image, 1, kappa, weight, mask)[1])

    row_loop(1, count, apply, most=8)


def final_kernel(sums, grad, search, image, second, rim, lower, newton_out, residual_out, newton, residual, newton_sem, residual_sem):
    rows, weeks, cols = grad.shape
    rz, pq, cross, total = (jnp.sum(sums[k : k + 1, :], axis=1, keepdims=True) for k in range(4))
    first, cross, total = rz / pq, cross / pq, total / pq
    scale = 1.0 / (total - cross * cross)
    along = jnp.broadcast_to((first * total - cross) * scale, (weeks, LANES))
    across = jnp.broadcast_to((first * cross - 1.0) * scale, (weeks, LANES))

    def copies(r):
        return (
            pltpu.make_async_copy(newton.at[r], newton_out.at[:, r, :], newton_sem.at[r]),
            pltpu.make_async_copy(residual.at[r], residual_out.at[:, r, :], residual_sem.at[r]),
        )

    one = rim.shape[0] - 1

    def combine(r, last, at):
        put_row(newton, r, [along * p - across * y for p, y in zip(row_of(search, r + 4), row_of(second, r + 2))])
        put_row(residual, r, [
            g - along * w + across * h for g, w, h in zip(row_of(grad, r), row_of(image, r), row_of(last, r - at))])
        for copy in copies(r):
            copy.start()

    row_loop(0, one, lambda r, _: combine(r, rim, 0), most=8)
    row_loop(one, rows - 1, lambda r, _: combine(r, lower, one), most=8)
    combine(rows - 1, rim, rows - 1 - one)
    for r in range(rows):
        for copy in copies(r):
            copy.wait()


def call(kernel, outs, ins, scratch=(), aliases=None, limit=2, flops=0, moved=0):
    shapes = tuple(VMEM(shape, F32) if space is VMEM else jax.ShapeDtypeStruct(shape, F32) for shape, space in outs)
    return pl.pallas_call(
        kernel,
        out_shape=shapes,
        in_specs=[pl.BlockSpec(memory_space=space) for _, space in ins],
        out_specs=tuple(pl.BlockSpec(memory_space=space) for _, space in outs),
        scratch_shapes=list(scratch),
        input_output_aliases=aliases or {},
        compiler_params=pltpu.CompilerParams(vmem_limit_bytes=limit * MIB),
        cost_estimate=pl.CostEstimate(flops=flops, bytes_accessed=moved, transcendentals=0),
    )(*[pltpu.with_memory_space_constraint(array, space) if space is pltpu.HBM else array for array, space in ins])


def shards(latent, counts, land_mask, region_ids, kappa_sq, covariates, effects, intercepts):
    weeks, rows, cols = latent.shape

    def ext(depth):
        return ((rows + 2 * depth, weeks, cols), VMEM)

    def maps(depth):
        return ((rows + 2 * depth, 1, cols), VMEM)

    cells = weeks * rows * cols
    SMEM, ANY, HBM, DMA = pltpu.SMEM, pl.ANY, pltpu.HBM, pltpu.SemaphoreType.DMA
    packed = ((2 * weeks + 5, cols), VMEM)
    near, far = call(
        pack_kernel,
        [packed, packed],
        [(latent, HBM), (kappa_sq, HBM), (land_mask, HBM)],
        scratch=[pltpu.VMEM((16, cols), F32), pltpu.VMEM((16, cols), jnp.int32), DMA((8,))],
        flops=cells // 16, moved=cells,
    )
    old_near, old_far = swap_rows(near, far)
    field, image, eta, tally, kappa, land, grad, weight, inv, search = call(
        front_kernel,
        [ext(2), ext(1), maps(0), ext(0), maps(3), maps(0), ext(0), ext(2), ext(2), ext(4)],
        [(effects.astype(F32), SMEM), (intercepts, SMEM), (latent, VMEM), (covariates, HBM),
         (region_ids, HBM), (kappa_sq, VMEM), (land_mask, VMEM), (counts, HBM)],
        scratch=[pltpu.VMEM(covariates.shape, covariates.dtype), pltpu.VMEM(counts.shape, jnp.int32),
                 pltpu.VMEM((rows, cols), jnp.int32), DMA, DMA, DMA],
        flops=40 * cells, moved=12 * cells, limit=8,
    )
    packed = ((4 * weeks + 2, cols), VMEM)
    kappa, field, image, grad, search, near, far = call(
        edge_kernel,
        [maps(3), ext(2), ext(1), ext(0), ext(4), packed, packed],
        [(old_far, VMEM), (old_near, VMEM), (eta, VMEM), (inv, VMEM),
         (kappa, VMEM), (field, VMEM), (image, VMEM), (grad, VMEM), (search, VMEM)],
        aliases={4 + k: k for k in range(5)},
        flops=10 * cells, moved=cells,
    )
    near, far = swap_rows(near, far)
    grad, weight, inv, search, first, image, second, second_image, partial = call(
        inner_kernel,
        [ext(0), ext(2), ext(2), ext(4), ext(3), ext(0), ext(2), ext(1), ((32, LANES), VMEM)],
        [(kappa, VMEM), (eta, VMEM), (land, VMEM), (tally, VMEM), (field, VMEM), (image, VMEM),
         (grad, VMEM), (weight, VMEM), (inv, VMEM), (search, VMEM)],
        aliases={6 + k: k for k in range(4)},
        flops=120 * cells, moved=12 * cells,
    )
    weight, inv, search, first, image, second, second_image, sums = call(
        outer_kernel,
        [ext(2), ext(2), ext(4), ext(3), ext(0), ext(2), ext(1), ((8, LANES), VMEM)],
        [(old_far, VMEM), (old_near, VMEM), (far, VMEM), (near, VMEM), (kappa, VMEM), (field, VMEM),
         (grad, VMEM), (partial, VMEM), (weight, VMEM), (inv, VMEM), (search, VMEM), (first, VMEM), (image, VMEM),
         (second, VMEM), (second_image, VMEM)],
        aliases={8 + k: k for k in range(7)},
        flops=20 * cells, moved=cells,
    )
    one = rows // 2 - 1

    def rim_rows(gate):
        return call(
            rim_kernel,
            [((one + 1, weeks, cols), VMEM)],
            [(gate, VMEM), (kappa, VMEM), (weight, VMEM), (inv, VMEM), (search, VMEM), (first, VMEM), (second, VMEM),
             (second_image, VMEM)],
            flops=4 * cells, moved=cells,
        )[0]

    def last_rows(low, count):
        return lambda gate: call(
            functools.partial(last_kernel, low),
            [((count, weeks, cols), VMEM)],
            [(gate, VMEM), (kappa, VMEM), (weight, VMEM), (second, VMEM), (second_image, VMEM)],
            flops=4 * cells, moved=cells,
        )[0]

    sums, (rim, lower) = all_sum(sums, [rim_rows, last_rows(one, rows - 1 - one)])
    return call(
        final_kernel,
        [(latent.shape, ANY), (latent.shape, ANY)],
        [(sums, VMEM), (grad, VMEM), (search, VMEM), (image, VMEM), (second, VMEM),
         (rim, VMEM), (lower, VMEM)],
        scratch=[pltpu.VMEM((rows, weeks, cols), F32), pltpu.VMEM((rows, weeks, cols), F32), DMA((rows,)), DMA((rows,))],
        flops=8 * cells, moved=8 * cells, limit=6,
    )


def solution(mesh):
    placed = (
        P(None, "gx", "region"),
        P(None, "gx", "region"),
        P("gx", "region"),
        P("gx", "region"),
        P("gx", "region"),
        P(None, "gx", "region"),
        P("region"),
        P("region"),
    )
    return jax.shard_map(
        shards,
        mesh=mesh,
        in_specs=placed,
        out_specs=(P(None, "gx", "region"), P(None, "gx", "region")),
        check_vma=False,
    )
```

```python
import functools

import jax
import jax.numpy as jnp
from jax import lax
from jax.experimental import pallas as pl
from jax.experimental.pallas import tpu as pltpu
from jax.sharding import PartitionSpec as P

AX = "gx"
LANES = 128
prior_scale = 0.04
time_coupling = 0.5
F32 = jnp.float32
VMEM = pltpu.VMEM
MIB = 1 << 20


def pair_maps(count):
    first = [(i, i ^ 1) for i in range(count) if (i ^ 1) < count]
    second = [(i, ((i + 1) ^ 1) - 1) for i in range(count) if 0 <= ((i + 1) ^ 1) - 1 < count]
    return first, second


def swap_rows(near, far):
    swap, cross = pair_maps(lax.axis_size(AX))
    far = lax.ppermute(far, AX, cross)
    return lax.ppermute(near, AX, swap), far


def all_sum(values, works):
    count = lax.axis_size(AX)
    results = []
    if count & (count - 1):
        return lax.psum(values, AX), [work(values) for work in works]
    rounds = [(1,)] if count > 1 else []
    step = 2
    while step < count:
        wide = 2 * step < count
        rounds.append((step, 2 * step, 3 * step) if wide else (step,))
        step *= 4 if wide else 2
    for number, partners in enumerate(rounds):
        got = [lax.ppermute(values, AX, [(i, i ^ k) for i in range(count)]) for k in partners]
        if number > 0 and len(results) < len(works):
            piece = works[len(results)](values)
            got, piece = lax.optimization_barrier((got, piece))
            results.append(piece)
        values = values + got[0]
        if len(got) > 1:
            values = values + (got[1] + got[2])
    while len(results) < len(works):
        results.append(works[len(results)](values))
    return values, results


def row_of(ref, row):
    return [ref[row, :, c : c + LANES] for c in range(0, ref.shape[2], LANES)]


def put_row(ref, row, tiles):
    for j, tile in enumerate(tiles):
        ref[row, :, j * LANES : (j + 1) * LANES] = tile


def map_row(ref, row):
    return [ref[row, :, c : c + LANES] for c in range(0, ref.shape[2], LANES)]


def masks(weeks):
    lane = lax.broadcasted_iota(jnp.int32, (weeks, LANES), 1)
    week = lax.broadcasted_iota(jnp.int32, (weeks, LANES), 0)
    return lane == 0, lane == LANES - 1, week == 0, week == weeks - 1


def laplace_row(up, mid, down, kappa, mask):
    first, last = mask[0], mask[1]
    count = len(mid)
    to_right = [pltpu.roll(t, 1, 1) for t in mid]
    to_left = [pltpu.roll(t, LANES - 1, 1) for t in mid]
    out = []
    for j in range(count):
        west = jnp.where(first, to_right[j - 1] if j > 0 else 0.0, to_right[j])
        east = jnp.where(last, to_left[j + 1] if j + 1 < count else 0.0, to_left[j])
        out.append((kappa[j] + 4.0) * mid[j] - ((up[j] + down[j]) + (west + east)))
    return out


def temporal_tile(tile, mask):
    weeks = tile.shape[0]
    before = jnp.where(mask[2], tile, pltpu.roll(tile, 1, 0))
    after = jnp.where(mask[3], tile, pltpu.roll(tile, weeks - 1, 0))
    return (2.0 * tile - before) - after


def fold(tiles):
    parts = [t[h : h + 8] for t in tiles for h in range(0, t.shape[0], 8)]
    while len(parts) > 1:
        parts = [a + b for a, b in zip(parts[::2], parts[1::2])] + ([parts[-1]] if len(parts) % 2 else [])
    return parts[0]


def diag_base(kappa):
    return prior_scale * ((kappa + 4.0) * (kappa + 4.0) + 4.0) + 2.0 * time_coupling


def is_odd():
    return lax.axis_index(AX) % 2 == 1


def row_loop(low, high, body, carry=None, most=14):
    count = high - low
    step = max(k for k in range(1, most + 1) if count % k == 0)

    def chunk(i, value):
        for k in range(step):
            value = body(low + i * step + k, value)
        return value

    if step == count:
        return chunk(0, carry)
    if carry is None:
        lax.fori_loop(0, count // step, lambda i, z: (chunk(i, None), z)[1], 0)
        return None
    return lax.fori_loop(0, count // step, chunk, carry)


def pack_kernel(latent, kappa_hbm, land_hbm, first, second, kappa, land, sems):
    weeks, rows, cols = latent.shape
    odd = is_odd()
    copies = []
    for k, (out, base) in enumerate(((first, jnp.where(odd, 0, rows - 2)), (second, jnp.where(odd, rows - 2, 0)))):
        for d in range(2):
            copies.append(pltpu.make_async_copy(
                latent.at[:, base + d, :], out.at[d * weeks : (d + 1) * weeks, :], sems.at[2 * k + d]))
    map_copies = []
    for k, (source, target) in enumerate(((kappa_hbm, kappa), (land_hbm, land))):
        for d, at in enumerate((0, rows - 8)):
            map_copies.append(pltpu.make_async_copy(
                source.at[at : at + 8, :], target.at[8 * d : 8 * d + 8, :], sems.at[4 + 2 * k + d]))
    for copy in copies + map_copies:
        copy.start()
    for copy in map_copies:
        copy.wait()
    at = 2 * weeks
    for d in range(3):
        top, bottom = kappa[d : d + 1, :], kappa[13 + d : 14 + d, :]
        first[at + d : at + d + 1, :] = jnp.where(odd, top, bottom)
        second[at + d : at + d + 1, :] = jnp.where(odd, bottom, top)
    for d in range(2):
        top, bottom = (land[q : q + 1, :].astype(F32) for q in (d, 14 + d))
        first[at + 3 + d : at + 4 + d, :] = jnp.where(odd, top, bottom)
        second[at + 3 + d : at + 4 + d, :] = jnp.where(odd, bottom, top)
    for copy in copies:
        copy.wait()


def rows_first(source, target, shift):
    weeks, rows, cols = source.shape
    for r in range(0, rows, 8):
        for c in range(0, cols, LANES):
            block = source[:, r : r + 8, c : c + LANES].astype(F32)
            target[r + shift : r + shift + 8, :, c : c + LANES] = jnp.swapaxes(block, 0, 1)


def front_kernel(effects, intercepts, latent, covariates, zones, kappa_flat, land_flat, counts,
                 field, image, eta, tally, kappa, land, grad, weight, inv, search, covs, raw, ids_all, cov_sem, sem, zone_sem):
    weeks, rows, cols = latent.shape
    mask = masks(weeks)
    copy = pltpu.make_async_copy(counts, raw, sem)
    cov_copy = pltpu.make_async_copy(covariates, covs, cov_sem)
    zone_copy = pltpu.make_async_copy(zones, ids_all, zone_sem)
    zone_copy.start()
    cov_copy.start()
    copy.start()
    rows_first(latent, field, 2)
    for r in range(rows):
        kappa[r + 3] = kappa_flat[r : r + 1, :]
        land[r] = land_flat[r : r + 1, :].astype(F32)

    def inner_image(r, _):
        put_row(image, r + 1, laplace_row(
            row_of(field, r + 1), row_of(field, r + 2), row_of(field, r + 3), map_row(kappa, r + 3), mask))

    row_loop(1, rows - 1, inner_image)
    zone_copy.wait()
    cov_copy.wait()
    width = 2 * LANES
    for c in range(0, cols, width):
        total = jnp.zeros((rows, width), F32)
        ids = ids_all[:, c : c + width]
        for z in range(intercepts.shape[0]):
            total = jnp.where(ids == z, intercepts[z], total)
        for k in range(covs.shape[0]):
            total = total + effects[k] * covs[k, :, c : c + width].astype(F32)
        for r in range(rows):
            eta[r, :, c : c + width] = total[r : r + 1]
    copy.wait()
    rows_first(raw, tally, 0)
    for r in (0, 1, rows - 2, rows - 1):
        gradient_row(r, field, tally, eta, land, kappa, None, grad, weight, inv, search, mask)
    for r in (2, 3, rows - 4, rows - 3):
        gradient_row(r, field, tally, eta, land, kappa, image, grad, weight, inv, search, mask)


def gradient_row(r, field, tally, eta, land, kappa, image, grad, weight, inv, search, mask):
    eta_row, land_row, kap, count_row = map_row(eta, r), map_row(land, r), map_row(kappa, r + 3), row_of(tally, r)
    if image is not None:
        outer = laplace_row(row_of(image, r), row_of(image, r + 1), row_of(image, r + 2), kap, mask)
    for j, tile in enumerate(row_of(field, r + 2)):
        on = land_row[j]
        curve = jnp.tanh(0.5 * (tile + eta_row[j]))
        heavy = on * (1.0 - curve * curve)
        inverse = 1.0 / (diag_base(kap[j]) + heavy)
        out = on * (count_row[j] - 2.0 - 2.0 * curve) - time_coupling * temporal_tile(tile, mask)
        part = slice(j * LANES, (j + 1) * LANES)
        weight[r + 2, :, part] = heavy
        inv[r + 2, :, part] = inverse
        if image is not None:
            out = out - prior_scale * outer[j]
            search[r + 4, :, part] = out * inverse
        grad[r, :, part] = out


def keep_inside(r, rows, tiles):
    if 0 <= r < rows:
        return tiles
    place, count = lax.axis_index(AX), lax.axis_size(AX)
    keep = jnp.where(place > 0 if r < 0 else place < count - 1, 1.0, 0.0)
    return [keep * t for t in tiles]


def halo_row(r, rows, depth, height, first, second):
    odd = is_odd()
    at = (r + depth if r < 0 else r - rows) * height
    a, b = (first, second) if r < 0 else (second, first)
    return [jnp.where(odd, a[at : at + height, c : c + LANES], b[at : at + height, c : c + LANES])
            for c in range(0, first.shape[1], LANES)]


def halo_line(above, line, first, second):
    odd = is_odd()
    a, b = (first, second) if above else (second, first)
    return [jnp.where(odd, a[line : line + 1, c : c + LANES], b[line : line + 1, c : c + LANES])
            for c in range(0, first.shape[1], LANES)]


def edge_kernel(got_second, got_first, eta, inv, kappa_in, field_in, image_in, grad_in, search_in,
                kappa, field, image, grad, search, first, second):
    weeks = field.shape[1]
    rows, _, cols = eta.shape
    mask = masks(weeks)
    odd = is_odd()
    for d in range(2):
        put_row(field, d, halo_row(d - 2, rows, 2, weeks, got_first, got_second))
        put_row(field, rows + 2 + d, halo_row(rows + d, rows, 2, weeks, got_first, got_second))
    for d in range(3):
        put_row(kappa, d, halo_line(True, 2 * weeks + d, got_first, got_second))
        put_row(kappa, rows + 3 + d, halo_line(False, 2 * weeks + d, got_first, got_second))
    for r in (-1, 0, rows - 1, rows):
        put_row(image, r + 1, keep_inside(r, rows, laplace_row(
            row_of(field, r + 1), row_of(field, r + 2), row_of(field, r + 3), map_row(kappa, r + 3), mask)))
    for r in (0, 1, rows - 2, rows - 1):
        outer = laplace_row(row_of(image, r), row_of(image, r + 1), row_of(image, r + 2), map_row(kappa, r + 3), mask)
        out = [a - prior_scale * b for a, b in zip(row_of(grad, r), outer)]
        put_row(grad, r, out)
        put_row(search, r + 4, [a * b for a, b in zip(out, row_of(inv, r + 2))])
    at = 4 * weeks
    for c in range(0, cols, LANES):
        part = slice(c, c + LANES)
        for d in range(4):
            top, bottom = search[4 + d, :, part], search[rows + d, :, part]
            first[d * weeks : (d + 1) * weeks, part] = jnp.where(odd, top, bottom)
            second[d * weeks : (d + 1) * weeks, part] = jnp.where(odd, bottom, top)
        for d in range(2):
            top, bottom = eta[d, :, part], eta[rows - 2 + d, :, part]
            first[at + d : at + d + 1, part] = jnp.where(odd, top, bottom)
            second[at + d : at + d + 1, part] = jnp.where(odd, bottom, top)


def halo_weight(r, rows, field, kappa, old_first, old_second, got_first, got_second):
    weeks = field.shape[1]
    d = r + 2 if r < 0 else r - rows
    eta_row = halo_line(r < 0, 4 * weeks + d, got_first, got_second)
    land_row = halo_line(r < 0, 2 * weeks + 3 + d, old_first, old_second)
    heavy = []
    for j, tile in enumerate(row_of(field, r + 2)):
        curve = jnp.tanh(0.5 * (tile + eta_row[j]))
        heavy.append(land_row[j] * (1.0 - curve * curve))
    return heavy, [1.0 / (diag_base(k) + h) for k, h in zip(map_row(kappa, r + 3), heavy)]


def mass_row(r, source, at, weight, mask):
    mid = row_of(source, at)
    return mid, [time_coupling * temporal_tile(m, mask) + h * m for m, h in zip(mid, row_of(weight, r + 2))]


def hessian_row(r, source, at, image, offset, kappa, weight, mask):
    outer = laplace_row(row_of(image, r + offset - 1), row_of(image, r + offset), row_of(image, r + offset + 1),
                        map_row(kappa, r + 3), mask)
    mid, mass = mass_row(r, source, at, weight, mask)
    return mid, [prior_scale * o + m for o, m in zip(outer, mass)]


def dot_rows(a, b):
    return fold([x * y for x, y in zip(a, b)])


def inner_kernel(kappa, eta, land, tally, field, start_image, grad_in, weight_in, inv_in, search_in,
                 grad, weight, inv, search, first, image, second, second_image, sums):
    weeks = grad.shape[1]
    rows = grad.shape[0]
    mask = masks(weeks)

    def gradient(r, _):
        gradient_row(r, field, tally, eta, land, kappa, start_image, grad, weight, inv, search, mask)

    row_loop(4, rows - 4, gradient, most=8)

    def inner_image(r, _):
        put_row(first, r + 3, laplace_row(
            row_of(search, r + 3), row_of(search, r + 4), row_of(search, r + 5), map_row(kappa, r + 3), mask))

    row_loop(1, rows - 1, inner_image)
    zero = jnp.zeros((8, LANES), F32)

    def apply(r, carry):
        rz, pq, cross, total = carry
        mid, out = hessian_row(r, search, r + 4, first, 3, kappa, weight, mask)
        other = [a * b for a, b in zip(out, row_of(inv, r + 2))]
        mass = [time_coupling * temporal_tile(y, mask) + h * y for y, h in zip(other, row_of(weight, r + 2))]
        put_row(image, r, out)
        put_row(second, r + 2, other)
        return (rz + dot_rows(mid, row_of(grad, r)), pq + dot_rows(mid, out), cross + dot_rows(other, out),
                total + dot_rows(other, mass))

    rz, pq, cross, total = row_loop(2, rows - 2, apply, (zero, zero, zero, zero), most=7)

    def second_inner(r, square):
        out = laplace_row(
            row_of(second, r + 1), row_of(second, r + 2), row_of(second, r + 3), map_row(kappa, r + 3), mask)
        put_row(second_image, r + 1, out)
        return square + dot_rows(out, out)

    square = row_loop(3, rows - 3, second_inner, zero)
    for k, value in enumerate((rz, pq, cross, total + prior_scale * square)):
        sums[8 * k : 8 * k + 8, :] = value


def outer_kernel(old_second, old_first, got_second, got_first, kappa, field, grad, partial,
                 weight_in, inv_in, search_in, first_in, image_in, second_in, second_image_in,
                 weight, inv, search, first, image, second, second_image, sums):
    weeks = grad.shape[1]
    rows = grad.shape[0]
    mask = masks(weeks)
    for r in (-3, -2, -1, rows, rows + 1, rows + 2):
        put_row(search, r + 4, halo_row(r, rows, 4, weeks, got_first, got_second))
    for r in (-1, rows):
        heavy, inverse = halo_weight(r, rows, field, kappa, old_first, old_second, got_first, got_second)
        put_row(weight, r + 2, heavy)
        put_row(inv, r + 2, inverse)

    for r in (-2, -1, 0, rows - 1, rows, rows + 1):
        put_row(first, r + 3, keep_inside(r, rows, laplace_row(
            row_of(search, r + 3), row_of(search, r + 4), row_of(search, r + 5), map_row(kappa, r + 3), mask)))
    rz, pq, cross, total = (partial[8 * k : 8 * k + 8, :] for k in range(4))
    for r in (-1, 0, 1, rows - 2, rows - 1, rows):
        mid, out = hessian_row(r, search, r + 4, first, 3, kappa, weight, mask)
        other = keep_inside(r, rows, [a * b for a, b in zip(out, row_of(inv, r + 2))])
        put_row(second, r + 2, other)
        if 0 <= r < rows:
            put_row(image, r, out)
            mass = [time_coupling * temporal_tile(y, mask) + h * y for y, h in zip(other, row_of(weight, r + 2))]
            rz, pq, cross = rz + dot_rows(mid, row_of(grad, r)), pq + dot_rows(mid, out), cross + dot_rows(other, out)
            total = total + dot_rows(other, mass)
    for r in (0, 1, 2, rows - 3, rows - 2, rows - 1):
        out = laplace_row(
            row_of(second, r + 1), row_of(second, r + 2), row_of(second, r + 3), map_row(kappa, r + 3), mask)
        put_row(second_image, r + 1, out)
        total = total + prior_scale * dot_rows(out, out)
    sums[...] = jnp.zeros_like(sums)
    for k, value in enumerate((rz, pq, cross, total)):
        sums[k : k + 1, :] = jnp.sum(value, axis=0, keepdims=True)


def last_kernel(low, gate, kappa, weight, second, second_image, last):
    mask = masks(last.shape[1])

    def apply(r, _):
        put_row(last, r, hessian_row(r + low, second, r + low + 2, second_image, 1, kappa, weight, mask)[1])

    row_loop(0, last.shape[0], apply, most=8)


def rim_kernel(gate, old_first, old_second, got_first, got_second, kappa, field, weight, search, first, second,
               second_image, last):
    rows = second_image.shape[0] - 2
    count = last.shape[0] - 1
    mask = masks(last.shape[1])
    for r, away in ((0, -1), (rows - 1, 1)):
        rim = [r + away * d for d in range(5)]
        tiles = keep_inside(rim[3], rows, laplace_row(
            halo_row(rim[4], rows, 4, last.shape[1], got_first, got_second),
            row_of(search, rim[3] + 4), row_of(search, rim[2] + 4),
            map_row(kappa, rim[3] + 3), mask))
        outer = laplace_row(tiles, row_of(first, rim[2] + 3), row_of(first, rim[1] + 3), map_row(kappa, rim[2] + 3), mask)
        heavy, inverse = halo_weight(rim[2], rows, field, kappa, old_first, old_second, got_first, got_second)
        tiles = keep_inside(rim[2], rows, [
            (prior_scale * o + (time_coupling * temporal_tile(m, mask) + h * m)) * d
            for o, m, h, d in zip(outer, row_of(search, rim[2] + 4), heavy, inverse)])
        tiles = keep_inside(rim[1], rows, laplace_row(
            tiles, row_of(second, rim[1] + 2), row_of(second, r + 2), map_row(kappa, rim[1] + 3), mask))
        outer = laplace_row(
            tiles, row_of(second_image, r + 1), row_of(second_image, r - away + 1), map_row(kappa, r + 3), mask)
        mass = mass_row(r, second, r + 2, weight, mask)[1]
        put_row(last, 0 if r == 0 else count, [prior_scale * o + m for o, m in zip(outer, mass)])

    def apply(r, _):
        put_row(last, r, hessian_row(r, second, r + 2, second_image, 1, kappa, weight, mask)[1])

    row_loop(1, count, apply, most=8)


def final_kernel(sums, grad, search, image, second, rim, lower, newton_out, residual_out, newton, residual, newton_sem, residual_sem):
    rows, weeks, cols = grad.shape
    rz, pq, cross, total = (jnp.sum(sums[k : k + 1, :], axis=1, keepdims=True) for k in range(4))
    first, cross, total = rz / pq, cross / pq, total / pq
    scale = 1.0 / (total - cross * cross)
    along = jnp.broadcast_to((first * total - cross) * scale, (weeks, LANES))
    across = jnp.broadcast_to((first * cross - 1.0) * scale, (weeks, LANES))

    def copies(r):
        return (
            pltpu.make_async_copy(newton.at[r], newton_out.at[:, r, :], newton_sem.at[r]),
            pltpu.make_async_copy(residual.at[r], residual_out.at[:, r, :], residual_sem.at[r]),
        )

    one = rim.shape[0] - 1

    def combine(r, last, at):
        put_row(newton, r, [along * p - across * y for p, y in zip(row_of(search, r + 4), row_of(second, r + 2))])
        put_row(residual, r, [
            g - along * w + across * h for g, w, h in zip(row_of(grad, r), row_of(image, r), row_of(last, r - at))])
        for copy in copies(r):
            copy.start()

    row_loop(0, one, lambda r, _: combine(r, rim, 0), most=5)
    row_loop(one, rows - 1, lambda r, _: combine(r, lower, one), most=5)
    combine(rows - 1, rim, rows - 1 - one)
    for r in range(rows):
        for copy in copies(r):
            copy.wait()


def call(kernel, outs, ins, scratch=(), aliases=None, limit=2, flops=0, moved=0):
    shapes = tuple(VMEM(shape, F32) if space is VMEM else jax.ShapeDtypeStruct(shape, F32) for shape, space in outs)
    return pl.pallas_call(
        kernel,
        out_shape=shapes,
        in_specs=[pl.BlockSpec(memory_space=space) for _, space in ins],
        out_specs=tuple(pl.BlockSpec(memory_space=space) for _, space in outs),
        scratch_shapes=list(scratch),
        input_output_aliases=aliases or {},
        compiler_params=pltpu.CompilerParams(vmem_limit_bytes=limit * MIB),
        cost_estimate=pl.CostEstimate(flops=flops, bytes_accessed=moved, transcendentals=0),
    )(*[pltpu.with_memory_space_constraint(array, space) if space is pltpu.HBM else array for array, space in ins])


def shards(latent, counts, land_mask, region_ids, kappa_sq, covariates, effects, intercepts):
    weeks, rows, cols = latent.shape

    def ext(depth):
        return ((rows + 2 * depth, weeks, cols), VMEM)

    def maps(depth):
        return ((rows + 2 * depth, 1, cols), VMEM)

    cells = weeks * rows * cols
    SMEM, ANY, HBM, DMA = pltpu.SMEM, pl.ANY, pltpu.HBM, pltpu.SemaphoreType.DMA
    packed = ((2 * weeks + 5, cols), VMEM)
    near, far = call(
        pack_kernel,
        [packed, packed],
        [(latent, HBM), (kappa_sq, HBM), (land_mask, HBM)],
        scratch=[pltpu.VMEM((16, cols), F32), pltpu.VMEM((16, cols), jnp.int32), DMA((8,))],
        flops=cells // 16, moved=cells,
    )
    old_near, old_far = swap_rows(near, far)
    field, image, eta, tally, kappa, land, grad, weight, inv, search = call(
        front_kernel,
        [ext(2), ext(1), maps(0), ext(0), maps(3), maps(0), ext(0), ext(2), ext(2), ext(4)],
        [(effects.astype(F32), SMEM), (intercepts, SMEM), (latent, VMEM), (covariates, HBM),
         (region_ids, HBM), (kappa_sq, VMEM), (land_mask, VMEM), (counts, HBM)],
        scratch=[pltpu.VMEM(covariates.shape, covariates.dtype), pltpu.VMEM(counts.shape, jnp.int32),
                 pltpu.VMEM((rows, cols), jnp.int32), DMA, DMA, DMA],
        flops=40 * cells, moved=12 * cells, limit=8,
    )
    packed = ((4 * weeks + 2, cols), VMEM)
    kappa, field, image, grad, search, near, far = call(
        edge_kernel,
        [maps(3), ext(2), ext(1), ext(0), ext(4), packed, packed],
        [(old_far, VMEM), (old_near, VMEM), (eta, VMEM), (inv, VMEM),
         (kappa, VMEM), (field, VMEM), (image, VMEM), (grad, VMEM), (search, VMEM)],
        aliases={4 + k: k for k in range(5)},
        flops=10 * cells, moved=cells,
    )
    near, far = swap_rows(near, far)
    grad, weight, inv, search, first, image, second, second_image, partial = call(
        inner_kernel,
        [ext(0), ext(2), ext(2), ext(4), ext(3), ext(0), ext(2), ext(1), ((32, LANES), VMEM)],
        [(kappa, VMEM), (eta, VMEM), (land, VMEM), (tally, VMEM), (field, VMEM), (image, VMEM),
         (grad, VMEM), (weight, VMEM), (inv, VMEM), (search, VMEM)],
        aliases={6 + k: k for k in range(4)},
        flops=120 * cells, moved=12 * cells,
    )
    weight, inv, search, first, image, second, second_image, sums = call(
        outer_kernel,
        [ext(2), ext(2), ext(4), ext(3), ext(0), ext(2), ext(1), ((8, LANES), VMEM)],
        [(old_far, VMEM), (old_near, VMEM), (far, VMEM), (near, VMEM), (kappa, VMEM), (field, VMEM),
         (grad, VMEM), (partial, VMEM), (weight, VMEM), (inv, VMEM), (search, VMEM), (first, VMEM), (image, VMEM),
         (second, VMEM), (second_image, VMEM)],
        aliases={8 + k: k for k in range(7)},
        flops=20 * cells, moved=cells,
    )
    one = rows // 2 - 1

    def rim_rows(gate):
        return call(
            rim_kernel,
            [((one + 1, weeks, cols), VMEM)],
            [(gate, VMEM), (old_near, VMEM), (old_far, VMEM), (near, VMEM), (far, VMEM), (kappa, VMEM), (field, VMEM),
             (weight, VMEM), (search, VMEM), (first, VMEM), (second, VMEM), (second_image, VMEM)],
            flops=4 * cells, moved=cells,
        )[0]

    def last_rows(low, count):
        return lambda gate: call(
            functools.partial(last_kernel, low),
            [((count, weeks, cols), VMEM)],
            [(gate, VMEM), (kappa, VMEM), (weight, VMEM), (second, VMEM), (second_image, VMEM)],
            flops=4 * cells, moved=cells,
        )[0]

    sums, (rim, lower) = all_sum(sums, [rim_rows, last_rows(one, rows - 1 - one)])
    return call(
        final_kernel,
        [(latent.shape, ANY), (latent.shape, ANY)],
        [(sums, VMEM), (grad, VMEM), (search, VMEM), (image, VMEM), (second, VMEM),
         (rim, VMEM), (lower, VMEM)],
        scratch=[pltpu.VMEM((rows, weeks, cols), F32), pltpu.VMEM((rows, weeks, cols), F32), DMA((rows,)), DMA((rows,))],
        flops=8 * cells, moved=8 * cells, limit=6,
    )


def solution(mesh):
    placed = (
        P(None, "gx", "region"),
        P(None, "gx", "region"),
        P("gx", "region"),
        P("gx", "region"),
        P("gx", "region"),
        P(None, "gx", "region"),
        P("region"),
        P("region"),
    )
    return jax.shard_map(
        shards,
        mesh=mesh,
        in_specs=placed,
        out_specs=(P(None, "gx", "region"), P(None, "gx", "region")),
        check_vma=False,
    )
```

```python
import functools

import jax
import jax.numpy as jnp
from jax import lax
from jax.experimental import pallas as pl
from jax.experimental.pallas import tpu as pltpu
from jax.sharding import PartitionSpec as P

AX = "gx"
LANES = 128
prior_scale = 0.04
time_coupling = 0.5
F32 = jnp.float32
VMEM = pltpu.VMEM
MIB = 1 << 20


def pair_maps(count):
    first = [(i, i ^ 1) for i in range(count) if (i ^ 1) < count]
    second = [(i, ((i + 1) ^ 1) - 1) for i in range(count) if 0 <= ((i + 1) ^ 1) - 1 < count]
    return first, second


def swap_rows(near, far):
    swap, cross = pair_maps(lax.axis_size(AX))
    far = lax.ppermute(far, AX, cross)
    return lax.ppermute(near, AX, swap), far


def all_sum(values, works):
    count = lax.axis_size(AX)
    results = []
    if count & (count - 1):
        return lax.psum(values, AX), [work(values) for work in works]
    rounds = [(1,)] if count > 1 else []
    step = 2
    while step < count:
        wide = 2 * step < count
        rounds.append((step, 2 * step, 3 * step) if wide else (step,))
        step *= 4 if wide else 2
    rounds = rounds[:1] + rounds[:0:-1]
    for number, partners in enumerate(rounds):
        got = [lax.ppermute(values, AX, [(i, i ^ k) for i in range(count)]) for k in partners]
        if number > 0 and len(results) < len(works):
            piece = works[len(results)](values)
            got, piece = lax.optimization_barrier((got, piece))
            results.append(piece)
        values = values + got[0]
        if len(got) > 1:
            values = values + (got[1] + got[2])
    while len(results) < len(works):
        results.append(works[len(results)](values))
    return values, results


def row_of(ref, row):
    return [ref[row, :, c : c + LANES] for c in range(0, ref.shape[2], LANES)]


def put_row(ref, row, tiles):
    for j, tile in enumerate(tiles):
        ref[row, :, j * LANES : (j + 1) * LANES] = tile


def map_row(ref, row):
    return [ref[row, :, c : c + LANES] for c in range(0, ref.shape[2], LANES)]


def masks(weeks):
    lane = lax.broadcasted_iota(jnp.int32, (weeks, LANES), 1)
    week = lax.broadcasted_iota(jnp.int32, (weeks, LANES), 0)
    return lane == 0, lane == LANES - 1, week == 0, week == weeks - 1


def laplace_row(up, mid, down, kappa, mask):
    first, last = mask[0], mask[1]
    count = len(mid)
    to_right = [pltpu.roll(t, 1, 1) for t in mid]
    to_left = [pltpu.roll(t, LANES - 1, 1) for t in mid]
    out = []
    for j in range(count):
        west = jnp.where(first, to_right[j - 1] if j > 0 else 0.0, to_right[j])
        east = jnp.where(last, to_left[j + 1] if j + 1 < count else 0.0, to_left[j])
        out.append((kappa[j] + 4.0) * mid[j] - ((up[j] + down[j]) + (west + east)))
    return out


def temporal_tile(tile, mask):
    weeks = tile.shape[0]
    before = jnp.where(mask[2], tile, pltpu.roll(tile, 1, 0))
    after = jnp.where(mask[3], tile, pltpu.roll(tile, weeks - 1, 0))
    return (2.0 * tile - before) - after


def fold(tiles):
    parts = [t[h : h + 8] for t in tiles for h in range(0, t.shape[0], 8)]
    while len(parts) > 1:
        parts = [a + b for a, b in zip(parts[::2], parts[1::2])] + ([parts[-1]] if len(parts) % 2 else [])
    return parts[0]


def diag_base(kappa):
    return prior_scale * ((kappa + 4.0) * (kappa + 4.0) + 4.0) + 2.0 * time_coupling


def is_odd():
    return lax.axis_index(AX) % 2 == 1


def row_loop(low, high, body, carry=None, most=14):
    count = high - low
    step = max(k for k in range(1, most + 1) if count % k == 0)

    def chunk(i, value):
        for k in range(step):
            value = body(low + i * step + k, value)
        return value

    if step == count:
        return chunk(0, carry)
    if carry is None:
        lax.fori_loop(0, count // step, lambda i, z: (chunk(i, None), z)[1], 0)
        return None
    return lax.fori_loop(0, count // step, chunk, carry)


def pack_kernel(latent, kappa_hbm, land_hbm, first, second, kappa, land, sems):
    weeks, rows, cols = latent.shape
    odd = is_odd()
    copies = []
    for k, (out, base) in enumerate(((first, jnp.where(odd, 0, rows - 2)), (second, jnp.where(odd, rows - 2, 0)))):
        for d in range(2):
            copies.append(pltpu.make_async_copy(
                latent.at[:, base + d, :], out.at[d * weeks : (d + 1) * weeks, :], sems.at[2 * k + d]))
    map_copies = []
    for k, (source, target) in enumerate(((kappa_hbm, kappa), (land_hbm, land))):
        for d, at in enumerate((0, rows - 8)):
            map_copies.append(pltpu.make_async_copy(
                source.at[at : at + 8, :], target.at[8 * d : 8 * d + 8, :], sems.at[4 + 2 * k + d]))
    for copy in copies + map_copies:
        copy.start()
    for copy in map_copies:
        copy.wait()
    at = 2 * weeks
    for d in range(3):
        top, bottom = kappa[d : d + 1, :], kappa[13 + d : 14 + d, :]
        first[at + d : at + d + 1, :] = jnp.where(odd, top, bottom)
        second[at + d : at + d + 1, :] = jnp.where(odd, bottom, top)
    for d in range(2):
        top, bottom = (land[q : q + 1, :].astype(F32) for q in (d, 14 + d))
        first[at + 3 + d : at + 4 + d, :] = jnp.where(odd, top, bottom)
        second[at + 3 + d : at + 4 + d, :] = jnp.where(odd, bottom, top)
    for copy in copies:
        copy.wait()


def rows_first(source, target, shift):
    weeks, rows, cols = source.shape
    for r in range(0, rows, 8):
        for c in range(0, cols, LANES):
            block = source[:, r : r + 8, c : c + LANES].astype(F32)
            target[r + shift : r + shift + 8, :, c : c + LANES] = jnp.swapaxes(block, 0, 1)


def front_kernel(effects, intercepts, latent, covariates, zones, kappa_flat, land_flat, counts,
                 field, image, eta, tally, kappa, land, grad, weight, inv, search, covs, raw, ids_all, cov_sem, sem, zone_sem):
    weeks, rows, cols = latent.shape
    mask = masks(weeks)
    copy = pltpu.make_async_copy(counts, raw, sem)
    cov_copy = pltpu.make_async_copy(covariates, covs, cov_sem)
    zone_copy = pltpu.make_async_copy(zones, ids_all, zone_sem)
    zone_copy.start()
    cov_copy.start()
    copy.start()
    rows_first(latent, field, 2)
    for r in range(rows):
        kappa[r + 3] = kappa_flat[r : r + 1, :]
        land[r] = land_flat[r : r + 1, :].astype(F32)

    def inner_image(r, _):
        put_row(image, r + 1, laplace_row(
            row_of(field, r + 1), row_of(field, r + 2), row_of(field, r + 3), map_row(kappa, r + 3), mask))

    row_loop(1, rows - 1, inner_image)
    zone_copy.wait()
    cov_copy.wait()
    width = 2 * LANES
    for c in range(0, cols, width):
        total = jnp.zeros((rows, width), F32)
        ids = ids_all[:, c : c + width]
        for z in range(intercepts.shape[0]):
            total = jnp.where(ids == z, intercepts[z], total)
        for k in range(covs.shape[0]):
            total = total + effects[k] * covs[k, :, c : c + width].astype(F32)
        for r in range(rows):
            eta[r, :, c : c + width] = total[r : r + 1]
    copy.wait()
    rows_first(raw, tally, 0)
    for r in (0, 1, rows - 2, rows - 1):
        gradient_row(r, field, tally, eta, land, kappa, None, grad, weight, inv, search, mask)
    for r in (2, 3, rows - 4, rows - 3):
        gradient_row(r, field, tally, eta, land, kappa, image, grad, weight, inv, search, mask)


def gradient_row(r, field, tally, eta, land, kappa, image, grad, weight, inv, search, mask):
    eta_row, land_row, kap, count_row = map_row(eta, r), map_row(land, r), map_row(kappa, r + 3), row_of(tally, r)
    if image is not None:
        outer = laplace_row(row_of(image, r), row_of(image, r + 1), row_of(image, r + 2), kap, mask)
    for j, tile in enumerate(row_of(field, r + 2)):
        on = land_row[j]
        curve = jnp.tanh(0.5 * (tile + eta_row[j]))
        heavy = on * (1.0 - curve * curve)
        inverse = 1.0 / (diag_base(kap[j]) + heavy)
        out = on * (count_row[j] - 2.0 - 2.0 * curve) - time_coupling * temporal_tile(tile, mask)
        part = slice(j * LANES, (j + 1) * LANES)
        weight[r + 2, :, part] = heavy
        inv[r + 2, :, part] = inverse
        if image is not None:
            out = out - prior_scale * outer[j]
            search[r + 4, :, part] = out * inverse
        grad[r, :, part] = out


def keep_inside(r, rows, tiles):
    if 0 <= r < rows:
        return tiles
    place, count = lax.axis_index(AX), lax.axis_size(AX)
    keep = jnp.where(place > 0 if r < 0 else place < count - 1, 1.0, 0.0)
    return [keep * t for t in tiles]


def halo_row(r, rows, depth, height, first, second):
    odd = is_odd()
    at = (r + depth if r < 0 else r - rows) * height
    a, b = (first, second) if r < 0 else (second, first)
    return [jnp.where(odd, a[at : at + height, c : c + LANES], b[at : at + height, c : c + LANES])
            for c in range(0, first.shape[1], LANES)]


def halo_line(above, line, first, second):
    odd = is_odd()
    a, b = (first, second) if above else (second, first)
    return [jnp.where(odd, a[line : line + 1, c : c + LANES], b[line : line + 1, c : c + LANES])
            for c in range(0, first.shape[1], LANES)]


def edge_kernel(got_second, got_first, eta, inv, kappa_in, field_in, image_in, grad_in, search_in,
                kappa, field, image, grad, search, first, second):
    weeks = field.shape[1]
    rows, _, cols = eta.shape
    mask = masks(weeks)
    odd = is_odd()
    for d in range(2):
        put_row(field, d, halo_row(d - 2, rows, 2, weeks, got_first, got_second))
        put_row(field, rows + 2 + d, halo_row(rows + d, rows, 2, weeks, got_first, got_second))
    for d in range(3):
        put_row(kappa, d, halo_line(True, 2 * weeks + d, got_first, got_second))
        put_row(kappa, rows + 3 + d, halo_line(False, 2 * weeks + d, got_first, got_second))
    for r in (-1, 0, rows - 1, rows):
        put_row(image, r + 1, keep_inside(r, rows, laplace_row(
            row_of(field, r + 1), row_of(field, r + 2), row_of(field, r + 3), map_row(kappa, r + 3), mask)))
    for r in (0, 1, rows - 2, rows - 1):
        outer = laplace_row(row_of(image, r), row_of(image, r + 1), row_of(image, r + 2), map_row(kappa, r + 3), mask)
        out = [a - prior_scale * b for a, b in zip(row_of(grad, r), outer)]
        put_row(grad, r, out)
        put_row(search, r + 4, [a * b for a, b in zip(out, row_of(inv, r + 2))])
    at = 4 * weeks
    for c in range(0, cols, LANES):
        part = slice(c, c + LANES)
        for d in range(4):
            top, bottom = search[4 + d, :, part], search[rows + d, :, part]
            first[d * weeks : (d + 1) * weeks, part] = jnp.where(odd, top, bottom)
            second[d * weeks : (d + 1) * weeks, part] = jnp.where(odd, bottom, top)
        for d in range(2):
            top, bottom = eta[d, :, part], eta[rows - 2 + d, :, part]
            first[at + d : at + d + 1, part] = jnp.where(odd, top, bottom)
            second[at + d : at + d + 1, part] = jnp.where(odd, bottom, top)


def halo_weight(r, rows, field, kappa, old_first, old_second, got_first, got_second):
    weeks = field.shape[1]
    d = r + 2 if r < 0 else r - rows
    eta_row = halo_line(r < 0, 4 * weeks + d, got_first, got_second)
    land_row = halo_line(r < 0, 2 * weeks + 3 + d, old_first, old_second)
    heavy = []
    for j, tile in enumerate(row_of(field, r + 2)):
        curve = jnp.tanh(0.5 * (tile + eta_row[j]))
        heavy.append(land_row[j] * (1.0 - curve * curve))
    return heavy, [1.0 / (diag_base(k) + h) for k, h in zip(map_row(kappa, r + 3), heavy)]


def mass_row(r, source, at, weight, mask):
    mid = row_of(source, at)
    return mid, [time_coupling * temporal_tile(m, mask) + h * m for m, h in zip(mid, row_of(weight, r + 2))]


def hessian_row(r, source, at, image, offset, kappa, weight, mask):
    outer = laplace_row(row_of(image, r + offset - 1), row_of(image, r + offset), row_of(image, r + offset + 1),
                        map_row(kappa, r + 3), mask)
    mid, mass = mass_row(r, source, at, weight, mask)
    return mid, [prior_scale * o + m for o, m in zip(outer, mass)]


def dot_rows(a, b):
    return fold([x * y for x, y in zip(a, b)])


def inner_kernel(kappa, eta, land, tally, field, start_image, grad_in, weight_in, inv_in, search_in,
                 grad, weight, inv, search, first, image, second, second_image, sums):
    weeks = grad.shape[1]
    rows = grad.shape[0]
    mask = masks(weeks)

    def gradient(r, _):
        gradient_row(r, field, tally, eta, land, kappa, start_image, grad, weight, inv, search, mask)

    row_loop(4, rows - 4, gradient, most=8)

    def inner_image(r, _):
        put_row(first, r + 3, laplace_row(
            row_of(search, r + 3), row_of(search, r + 4), row_of(search, r + 5), map_row(kappa, r + 3), mask))

    row_loop(1, rows - 1, inner_image)
    zero = jnp.zeros((8, LANES), F32)

    def apply(r, carry):
        rz, pq, cross, total = carry
        mid, out = hessian_row(r, search, r + 4, first, 3, kappa, weight, mask)
        other = [a * b for a, b in zip(out, row_of(inv, r + 2))]
        mass = [time_coupling * temporal_tile(y, mask) + h * y for y, h in zip(other, row_of(weight, r + 2))]
        put_row(image, r, out)
        put_row(second, r + 2, other)
        return (rz + dot_rows(mid, row_of(grad, r)), pq + dot_rows(mid, out), cross + dot_rows(other, out),
                total + dot_rows(other, mass))

    rz, pq, cross, total = row_loop(2, rows - 2, apply, (zero, zero, zero, zero), most=7)

    def second_inner(r, square):
        out = laplace_row(
            row_of(second, r + 1), row_of(second, r + 2), row_of(second, r + 3), map_row(kappa, r + 3), mask)
        put_row(second_image, r + 1, out)
        return square + dot_rows(out, out)

    square = row_loop(3, rows - 3, second_inner, zero)
    for k, value in enumerate((rz, pq, cross, total + prior_scale * square)):
        sums[8 * k : 8 * k + 8, :] = value


def outer_kernel(old_second, old_first, got_second, got_first, kappa, field, grad, partial,
                 weight_in, inv_in, search_in, first_in, image_in, second_in, second_image_in,
                 weight, inv, search, first, image, second, second_image, sums):
    weeks = grad.shape[1]
    rows = grad.shape[0]
    mask = masks(weeks)
    for r in (-3, -2, -1, rows, rows + 1, rows + 2):
        put_row(search, r + 4, halo_row(r, rows, 4, weeks, got_first, got_second))
    for r in (-1, rows):
        heavy, inverse = halo_weight(r, rows, field, kappa, old_first, old_second, got_first, got_second)
        put_row(weight, r + 2, heavy)
        put_row(inv, r + 2, inverse)

    for r in (-2, -1, 0, rows - 1, rows, rows + 1):
        put_row(first, r + 3, keep_inside(r, rows, laplace_row(
            row_of(search, r + 3), row_of(search, r + 4), row_of(search, r + 5), map_row(kappa, r + 3), mask)))
    rz, pq, cross, total = (partial[8 * k : 8 * k + 8, :] for k in range(4))
    for r in (-1, 0, 1, rows - 2, rows - 1, rows):
        mid, out = hessian_row(r, search, r + 4, first, 3, kappa, weight, mask)
        other = keep_inside(r, rows, [a * b for a, b in zip(out, row_of(inv, r + 2))])
        put_row(second, r + 2, other)
        if 0 <= r < rows:
            put_row(image, r, out)
            mass = [time_coupling * temporal_tile(y, mask) + h * y for y, h in zip(other, row_of(weight, r + 2))]
            rz, pq, cross = rz + dot_rows(mid, row_of(grad, r)), pq + dot_rows(mid, out), cross + dot_rows(other, out)
            total = total + dot_rows(other, mass)
    for r in (0, 1, 2, rows - 3, rows - 2, rows - 1):
        out = laplace_row(
            row_of(second, r + 1), row_of(second, r + 2), row_of(second, r + 3), map_row(kappa, r + 3), mask)
        put_row(second_image, r + 1, out)
        total = total + prior_scale * dot_rows(out, out)
    sums[...] = jnp.zeros_like(sums)
    for k, value in enumerate((rz, pq, cross, total)):
        sums[k : k + 1, :] = jnp.sum(value, axis=0, keepdims=True)


def last_kernel(low, gate, kappa, weight, second, second_image, last):
    mask = masks(last.shape[1])

    def apply(r, _):
        put_row(last, r, hessian_row(r + low, second, r + low + 2, second_image, 1, kappa, weight, mask)[1])

    row_loop(0, last.shape[0], apply, most=8)


def rim_kernel(gate, old_first, old_second, got_first, got_second, kappa, field, weight, search, first, second,
               second_image, last):
    rows = second_image.shape[0] - 2
    count = last.shape[0] - 1
    mask = masks(last.shape[1])
    for r, away in ((0, -1), (rows - 1, 1)):
        rim = [r + away * d for d in range(5)]
        tiles = keep_inside(rim[3], rows, laplace_row(
            halo_row(rim[4], rows, 4, last.shape[1], got_first, got_second),
            row_of(search, rim[3] + 4), row_of(search, rim[2] + 4),
            map_row(kappa, rim[3] + 3), mask))
        outer = laplace_row(tiles, row_of(first, rim[2] + 3), row_of(first, rim[1] + 3), map_row(kappa, rim[2] + 3), mask)
        heavy, inverse = halo_weight(rim[2], rows, field, kappa, old_first, old_second, got_first, got_second)
        tiles = keep_inside(rim[2], rows, [
            (prior_scale * o + (time_coupling * temporal_tile(m, mask) + h * m)) * d
            for o, m, h, d in zip(outer, row_of(search, rim[2] + 4), heavy, inverse)])
        tiles = keep_inside(rim[1], rows, laplace_row(
            tiles, row_of(second, rim[1] + 2), row_of(second, r + 2), map_row(kappa, rim[1] + 3), mask))
        outer = laplace_row(
            tiles, row_of(second_image, r + 1), row_of(second_image, r - away + 1), map_row(kappa, r + 3), mask)
        mass = mass_row(r, second, r + 2, weight, mask)[1]
        put_row(last, 0 if r == 0 else count, [prior_scale * o + m for o, m in zip(outer, mass)])

    def apply(r, _):
        put_row(last, r, hessian_row(r, second, r + 2, second_image, 1, kappa, weight, mask)[1])

    row_loop(1, count, apply, most=8)


def final_kernel(sums, grad, search, image, second, rim, lower, newton_out, residual_out, newton, residual, newton_sem, residual_sem):
    rows, weeks, cols = grad.shape
    rz, pq, cross, total = (jnp.sum(sums[k : k + 1, :], axis=1, keepdims=True) for k in range(4))
    first, cross, total = rz / pq, cross / pq, total / pq
    scale = 1.0 / (total - cross * cross)
    along = jnp.broadcast_to((first * total - cross) * scale, (weeks, LANES))
    across = jnp.broadcast_to((first * cross - 1.0) * scale, (weeks, LANES))

    def copies(r):
        return (
            pltpu.make_async_copy(newton.at[r], newton_out.at[:, r, :], newton_sem.at[r]),
            pltpu.make_async_copy(residual.at[r], residual_out.at[:, r, :], residual_sem.at[r]),
        )

    one = rim.shape[0] - 1

    def combine(r, last, at):
        put_row(newton, r, [along * p - across * y for p, y in zip(row_of(search, r + 4), row_of(second, r + 2))])
        put_row(residual, r, [
            g - along * w + across * h for g, w, h in zip(row_of(grad, r), row_of(image, r), row_of(last, r - at))])
        for copy in copies(r):
            copy.start()

    row_loop(0, one, lambda r, _: combine(r, rim, 0), most=5)
    row_loop(one, rows - 1, lambda r, _: combine(r, lower, one), most=5)
    combine(rows - 1, rim, rows - 1 - one)
    for r in range(rows):
        for copy in copies(r):
            copy.wait()


def call(kernel, outs, ins, scratch=(), aliases=None, limit=2, flops=0, moved=0):
    shapes = tuple(VMEM(shape, F32) if space is VMEM else jax.ShapeDtypeStruct(shape, F32) for shape, space in outs)
    return pl.pallas_call(
        kernel,
        out_shape=shapes,
        in_specs=[pl.BlockSpec(memory_space=space) for _, space in ins],
        out_specs=tuple(pl.BlockSpec(memory_space=space) for _, space in outs),
        scratch_shapes=list(scratch),
        input_output_aliases=aliases or {},
        compiler_params=pltpu.CompilerParams(vmem_limit_bytes=limit * MIB),
        cost_estimate=pl.CostEstimate(flops=flops, bytes_accessed=moved, transcendentals=0),
    )(*[pltpu.with_memory_space_constraint(array, space) if space is pltpu.HBM else array for array, space in ins])


def shards(latent, counts, land_mask, region_ids, kappa_sq, covariates, effects, intercepts):
    weeks, rows, cols = latent.shape

    def ext(depth):
        return ((rows + 2 * depth, weeks, cols), VMEM)

    def maps(depth):
        return ((rows + 2 * depth, 1, cols), VMEM)

    cells = weeks * rows * cols
    SMEM, ANY, HBM, DMA = pltpu.SMEM, pl.ANY, pltpu.HBM, pltpu.SemaphoreType.DMA
    packed = ((2 * weeks + 5, cols), VMEM)
    near, far = call(
        pack_kernel,
        [packed, packed],
        [(latent, HBM), (kappa_sq, HBM), (land_mask, HBM)],
        scratch=[pltpu.VMEM((16, cols), F32), pltpu.VMEM((16, cols), jnp.int32), DMA((8,))],
        flops=cells // 16, moved=cells,
    )
    old_near, old_far = swap_rows(near, far)
    field, image, eta, tally, kappa, land, grad, weight, inv, search = call(
        front_kernel,
        [ext(2), ext(1), maps(0), ext(0), maps(3), maps(0), ext(0), ext(2), ext(2), ext(4)],
        [(effects.astype(F32), SMEM), (intercepts, SMEM), (latent, VMEM), (covariates, HBM),
         (region_ids, HBM), (kappa_sq, VMEM), (land_mask, VMEM), (counts, HBM)],
        scratch=[pltpu.VMEM(covariates.shape, covariates.dtype), pltpu.VMEM(counts.shape, jnp.int32),
                 pltpu.VMEM((rows, cols), jnp.int32), DMA, DMA, DMA],
        flops=40 * cells, moved=12 * cells, limit=8,
    )
    packed = ((4 * weeks + 2, cols), VMEM)
    kappa, field, image, grad, search, near, far = call(
        edge_kernel,
        [maps(3), ext(2), ext(1), ext(0), ext(4), packed, packed],
        [(old_far, VMEM), (old_near, VMEM), (eta, VMEM), (inv, VMEM),
         (kappa, VMEM), (field, VMEM), (image, VMEM), (grad, VMEM), (search, VMEM)],
        aliases={4 + k: k for k in range(5)},
        flops=10 * cells, moved=cells,
    )
    near, far = swap_rows(near, far)
    grad, weight, inv, search, first, image, second, second_image, partial = call(
        inner_kernel,
        [ext(0), ext(2), ext(2), ext(4), ext(3), ext(0), ext(2), ext(1), ((32, LANES), VMEM)],
        [(kappa, VMEM), (eta, VMEM), (land, VMEM), (tally, VMEM), (field, VMEM), (image, VMEM),
         (grad, VMEM), (weight, VMEM), (inv, VMEM), (search, VMEM)],
        aliases={6 + k: k for k in range(4)},
        flops=120 * cells, moved=12 * cells,
    )
    weight, inv, search, first, image, second, second_image, sums = call(
        outer_kernel,
        [ext(2), ext(2), ext(4), ext(3), ext(0), ext(2), ext(1), ((8, LANES), VMEM)],
        [(old_far, VMEM), (old_near, VMEM), (far, VMEM), (near, VMEM), (kappa, VMEM), (field, VMEM),
         (grad, VMEM), (partial, VMEM), (weight, VMEM), (inv, VMEM), (search, VMEM), (first, VMEM), (image, VMEM),
         (second, VMEM), (second_image, VMEM)],
        aliases={8 + k: k for k in range(7)},
        flops=20 * cells, moved=cells,
    )
    one = rows // 2 - 1

    def rim_rows(gate):
        return call(
            rim_kernel,
            [((one + 1, weeks, cols), VMEM)],
            [(gate, VMEM), (old_near, VMEM), (old_far, VMEM), (near, VMEM), (far, VMEM), (kappa, VMEM), (field, VMEM),
             (weight, VMEM), (search, VMEM), (first, VMEM), (second, VMEM), (second_image, VMEM)],
            flops=4 * cells, moved=cells,
        )[0]

    def last_rows(low, count):
        return lambda gate: call(
            functools.partial(last_kernel, low),
            [((count, weeks, cols), VMEM)],
            [(gate, VMEM), (kappa, VMEM), (weight, VMEM), (second, VMEM), (second_image, VMEM)],
            flops=4 * cells, moved=cells,
        )[0]

    sums, (rim, lower) = all_sum(sums, [rim_rows, last_rows(one, rows - 1 - one)])
    return call(
        final_kernel,
        [(latent.shape, ANY), (latent.shape, ANY)],
        [(sums, VMEM), (grad, VMEM), (search, VMEM), (image, VMEM), (second, VMEM),
         (rim, VMEM), (lower, VMEM)],
        scratch=[pltpu.VMEM((rows, weeks, cols), F32), pltpu.VMEM((rows, weeks, cols), F32), DMA((rows,)), DMA((rows,))],
        flops=8 * cells, moved=8 * cells, limit=6,
    )


def solution(mesh):
    placed = (
        P(None, "gx", "region"),
        P(None, "gx", "region"),
        P("gx", "region"),
        P("gx", "region"),
        P("gx", "region"),
        P(None, "gx", "region"),
        P("region"),
        P("region"),
    )
    return jax.shard_map(
        shards,
        mesh=mesh,
        in_specs=placed,
        out_specs=(P(None, "gx", "region"), P(None, "gx", "region")),
        check_vma=False,
    )
```
